32 devices in a mesh: narrow: 4 (over z), wide: 8 (over y, x, core).
Axes of the slice: x: 2, y: 2, z: 4, core: 2. Of those that a mesh axis runs over, the one named last changes fastest.
Arguments:
- sources: float32 [16, 16, 32, 256], P(None, 'wide', 'narrow')
- well_columns: int32 [16], replicated, may hold values from 0 to 511
- column_active: int32 [16, 32], P('wide', 'narrow'), may hold values 0 or 1
- perm_root: float32 [16, 32, 256], P('wide', 'narrow'), may hold values from 0.5 to 2
- storage_term: float32 [16, 32, 256], P('wide', 'narrow'), may hold values from 0.2 to 2
- inverse_blocks: bfloat16 [16, 32, 2, 128, 128], P('wide', 'narrow')
Outputs:
- solution: float32 [16, 16, 32, 256], P(None, 'wide', 'narrow')
- residual: float32 [16, 16, 32, 256], P(None, 'wide', 'narrow')
The draws below stay inside these ranges and needn't reach their ends.
All inputs are finite; a program needn't handle non-finite values. No bound on the sum of `column_active` on one device may be relied on, other than what follows from the above.
Results may differ from the reference program's by a relative error of at most 0.0085.
Values sent between devices are 32-bit elements; how exact they have to be, the bound alone decides.
No kernel may reach another device: no remote copies, remote signals or barrier semaphores. Data moves between devices by JAX's collectives and lax.ppermute only.
A program may use at most 64 MiB of HBM per device.

```python
import math
import jax
import jax.numpy as jnp
from jax import lax

K = 16
NZ = 256
BLK = 128
ITERS = 3
NX = 16
NY = 32
NB = 2


def draw_sources(key, part):
    first, second = jax.random.split(key, 2)
    shape = (K, NX, NY, NZ)
    positions = jnp.arange(NX, dtype=jnp.float32)
    rising = 1.0 + 2.0 * positions / max(NX - 1, 1)
    rough = jnp.exp(jax.random.uniform(second, shape, jnp.float32, -0.7, 0.7))
    core = jnp.clip(jax.random.normal(first, shape, jnp.float32), -6.0, 6.0)
    return 3.0 * core * rough * rising[None, :, None, None]


def draw_inverse_blocks(key, part):
    first, second = jax.random.split(key, 2)
    shape = (NX, NY, NZ // BLK, BLK, BLK)
    noise = jax.random.uniform(first, shape, jnp.float32, -1.0, 1.0)
    sym = 0.5 * (noise + jnp.swapaxes(noise, -1, -2))
    rows = jnp.arange(BLK, dtype=jnp.int32)
    ident = (rows[:, None] == rows[None, :]).astype(jnp.float32)
    diag_vals = 1.0 + 0.5 * jax.random.uniform(second, shape[:-1], jnp.float32)
    matrix = sym * (1.0 / BLK) * (1.0 - ident) + ident * diag_vals[..., None]
    return matrix.astype(jnp.bfloat16)


def with_ends(values, stream_key, smallest, largest):
    longest = values.shape.index(max(values.shape))
    spots = []
    for shift in (0, 1):
        where = [jax.random.randint(jax.random.fold_in(stream_key, axis), (), 0, length) for axis, length in enumerate(values.shape)]
        where[longest] = (where[longest] + shift) % values.shape[longest]
        spots.append(tuple(where))
    return values.at[spots[0]].set(smallest).at[spots[1]].set(largest)


def block_scale(own_key, shape, shards, least, high):
    def one(position, parts):
        steps = jax.random.uniform(jax.random.fold_in(jax.random.fold_in(own_key, 6), position), (parts,), jnp.float32, least / len(shards), high / len(shards))
        return jnp.repeat(jnp.exp(steps), shape[position] // parts).reshape((-1,) + (1,) * (len(shape) - position - 1))

    loudness = one(*shards[0])
    for cut in shards[1:]:
        loudness = loudness * one(*cut)
    return loudness


def setup_inputs(seed: int = 0) -> dict:
    splits = jax.random.split(jax.random.key(seed), 7)
    return {
        "sources": draw_sources(jax.random.fold_in(splits[6], 71), 0),
        "well_columns": with_ends(jax.random.randint(splits[1], (K,), 0, NX * NY), jax.random.fold_in(splits[1], 1), 0, (NX * NY) - 1).astype(jnp.int32),
        "column_active": with_ends((jax.random.randint(splits[2], (NX, NY), 0, 10) < 9).astype(jnp.int32), jax.random.fold_in(splits[2], 1), 0, 1),
        "perm_root": jnp.clip(jnp.exp(math.log(2.0) - 1.3862944 * jax.random.uniform(splits[3], (NX, NY, NZ), jnp.float32) ** block_scale(splits[3], (NX, NY, NZ), ((0, 8), (1, 4)), -0.2, 0.2)), 0.5, 2.0),
        "storage_term": jnp.clip(jnp.exp(math.log(2.0) - 2.3025851 * jax.random.uniform(splits[4], (NX, NY, NZ), jnp.float32) ** block_scale(splits[4], (NX, NY, NZ), ((0, 8), (1, 4)), -0.2, 0.2)), 0.2, 2.0),
        "inverse_blocks": draw_inverse_blocks(jax.random.fold_in(splits[6], 71), 0),
    }


WELL_RATE = 4.0

def coupling(padded, coef_pad):
    center = padded[:, 1:-1, 1:-1]
    coef = coef_pad[1:-1, 1:-1]
    total = coef_pad[2:, 1:-1] * (center - padded[:, 2:, 1:-1]) + coef_pad[:-2, 1:-1] * (center - padded[:, :-2, 1:-1])
    total = total + coef_pad[1:-1, 2:] * (center - padded[:, 1:-1, 2:]) + coef_pad[1:-1, :-2] * (center - padded[:, 1:-1, :-2])
    zero_layer = jnp.zeros_like(center[..., :1])
    zero_coef = jnp.zeros_like(coef[..., :1])
    upper = jnp.concatenate([center[..., 1:], zero_layer], -1)
    upper_coef = jnp.concatenate([coef[..., 1:], zero_coef], -1)
    lower = jnp.concatenate([zero_layer, center[..., :-1]], -1)
    lower_coef = jnp.concatenate([zero_coef, coef[..., :-1]], -1)
    total = total + upper_coef * (center - upper) + lower_coef * (center - lower)
    return coef * total

def operate(values, diag_term, coef_pad):
    padded = jnp.pad(values, ((0, 0), (1, 1), (1, 1), (0, 0)))
    return diag_term * values + coupling(padded, coef_pad)

def precondition(values, inverse_blocks):
    rounded = values.astype(jnp.bfloat16)
    rounded = lax.optimization_barrier(rounded).astype(jnp.float32)
    shaped = rounded.reshape(K, NX, NY, NB, BLK)
    moved = jnp.moveaxis(shaped, 1, 0)

    def one_row(pieces):
        return jnp.einsum('ybij,kybj->kybi', pieces[0].astype(jnp.float32), pieces[1], precision=lax.Precision.HIGHEST)
    output = lax.map(one_row, (inverse_blocks, moved))
    return jnp.moveaxis(output, 0, 1).reshape(K, NX, NY, NZ)

def gram_of(left, right):
    return jnp.einsum('kxyz,lxyz->kl', left, right, precision=lax.Precision.HIGHEST)

def combine(values, coefs):
    return jnp.einsum('kxyz,kl->lxyz', values, coefs, precision=lax.Precision.HIGHEST)

def solve_gram(matrix, target):
    sym = 0.5 * (matrix + matrix.T)
    factor = jnp.linalg.cholesky(sym)
    inner = lax.linalg.triangular_solve(factor, target, left_side=True, lower=True)
    return lax.linalg.triangular_solve(factor, inner, left_side=True, lower=True, transpose_a=True)

def reference(sources, well_columns, column_active, perm_root, storage_term, inverse_blocks):
    active = column_active.astype(jnp.float32)[..., None]
    coef = perm_root * active
    coef_pad = jnp.pad(coef, ((1, 1), (1, 1), (0, 0)))
    diag_term = active * storage_term + (1.0 - active)
    column_ids = jnp.arange(NX * NY, dtype=jnp.int32).reshape(NX, NY)
    wells = (column_ids[None] == well_columns[:, None, None]).astype(jnp.float32)
    residual = sources + WELL_RATE * wells[..., None]
    solution = jnp.zeros_like(residual)
    zset = precondition(residual, inverse_blocks)
    res_gram = gram_of(zset, residual)
    direction = zset
    for iteration in range(ITERS):
        image = operate(direction, diag_term, coef_pad)
        curv_gram = gram_of(direction, image)
        step_size = solve_gram(curv_gram, res_gram)
        solution = solution + combine(direction, step_size)
        residual = residual - combine(image, step_size)
        if iteration + 1 < ITERS:
            zset = precondition(residual, inverse_blocks)
            new_gram = gram_of(zset, residual)
            conj_coef = solve_gram(res_gram, new_gram)
            direction = zset + combine(direction, conj_coef)
            res_gram = new_gram
    return (solution, residual)
```

```python
import functools

import jax
import jax.numpy as jnp
from jax import lax
from jax.experimental import pallas as pl
from jax.experimental.pallas import tpu as pltpu
from jax.sharding import PartitionSpec as P

ITERS = 3
WELL_RATE = 4.0
VMEM_BYTES = 24 * 1024 * 1024
VMEM = pl.BlockSpec(memory_space=pltpu.VMEM)
SMEM = pl.BlockSpec(memory_space=pltpu.SMEM)
HIGHEST = lax.Precision.HIGHEST


def call(kernel, out_shape, in_specs, *args, flops=0, scratch=()):
    shapes = [jax.ShapeDtypeStruct(shape, jnp.float32) for shape in out_shape]
    size = sum(a.size * a.dtype.itemsize for a in args) + sum(s.size * 4 for s in shapes)
    return pl.pallas_call(
        kernel,
        out_shape=shapes,
        in_specs=in_specs,
        out_specs=[VMEM] * len(shapes),
        scratch_shapes=list(scratch),
        compiler_params=pltpu.CompilerParams(vmem_limit_bytes=VMEM_BYTES),
        cost_estimate=pl.CostEstimate(flops=flops, bytes_accessed=size, transcendentals=0),
    )(*args)


def apply_blocks(value, blocks_ref, col):
    count, layers = value.shape
    parts = []
    size = blocks_ref.shape[-1]
    for b in range(layers // size):
        piece = value[:, b * size : (b + 1) * size]
        high = piece.astype(jnp.bfloat16)
        low = (piece - high.astype(jnp.float32)).astype(jnp.bfloat16)
        both = jnp.concatenate([high, low], axis=0)
        out = jnp.dot(both, blocks_ref[col, b], preferred_element_type=jnp.float32)
        parts.append(out[:count] + out[count:])
    return jnp.concatenate(parts, axis=1)


def write_edges(sides_ref, cols, v_ref, coef_ref, edges):
    cols_x, cols_y = cols
    count = v_ref.shape[1]
    odd_wide, odd_narrow = sides_ref[0], sides_ref[1]
    for slot, (ref, odd) in enumerate(zip(edges, (odd_wide, odd_wide, odd_narrow, odd_narrow))):
        at_low = odd if slot % 2 == 0 else 1 - odd
        number = cols_y if slot < 2 else cols_x
        for i in range(number):
            if slot < 2:
                col = jnp.where(at_low == 1, 0, (cols_x - 1) * cols_y) + i
            else:
                col = i * cols_y + jnp.where(at_low == 1, 0, cols_y - 1)
            ref[i * count : (i + 1) * count, :] = v_ref[col]
            if coef_ref is not None:
                ref[number * count + i : number * count + i + 1, :] = coef_ref[pl.ds(col, 1), :]


def start_kernel(cols, sides_ref, r_ref, coef_ref, blocks_ref, v_ref, *edges):
    for col in range(cols[0] * cols[1]):
        v_ref[col] = apply_blocks(r_ref[col], blocks_ref, col)
    write_edges(sides_ref, cols, v_ref, coef_ref, edges)


def neighbours(sides_ref, cols, count, got, got_coefs):
    cols_x, cols_y = cols
    odd_wide, odd_narrow = sides_ref[0] == 1, sides_ref[1] == 1

    def beyond(v_ref, coef_ref, x, y, step_x, step_y):
        nx, ny = x + step_x, y + step_y
        if 0 <= nx < cols_x and 0 <= ny < cols_y:
            col = nx * cols_y + ny
            return v_ref[col], coef_ref[col : col + 1, :]
        if step_x:
            pair, odd, i, number, low = got[0:2], odd_wide, y, cols_y, step_x < 0
            coefs = got_coefs[0:2]
        else:
            pair, odd, i, number, low = got[2:4], odd_narrow, x, cols_x, step_y < 0
            coefs = got_coefs[2:4]
        first, second = (ref[i * count : (i + 1) * count, :] for ref in pair)
        row = number * count + i
        c_first, c_second = (ref[row : row + 1, :] for ref in coefs)
        if low:
            return jnp.where(odd, first, second), jnp.where(odd, c_first, c_second)
        return jnp.where(odd, second, first), jnp.where(odd, c_second, c_first)

    return beyond


def operate(beyond, cols, v_ref, coef_ref, diag_ref, x, y):
    col = x * cols[1] + y
    center = v_ref[col]
    layers = center.shape[-1]
    coef = coef_ref[col : col + 1, :]
    lane = lax.broadcasted_iota(jnp.int32, (1, layers), 1)
    total = jnp.zeros_like(center)
    for step_x, step_y in ((1, 0), (-1, 0), (0, 1), (0, -1)):
        other, other_coef = beyond(v_ref, coef_ref, x, y, step_x, step_y)
        total = total + other_coef * (center - other)
    upper_coef = jnp.where(lane == layers - 1, 0.0, pltpu.roll(coef, layers - 1, 1))
    lower_coef = jnp.where(lane == 0, 0.0, pltpu.roll(coef, 1, 1))
    total = total + upper_coef * (center - pltpu.roll(center, layers - 1, 1))
    total = total + lower_coef * (center - pltpu.roll(center, 1, 1))
    return diag_ref[col : col + 1, :] * center + coef * total


def step_kernel(cols, sides_ref, v_ref, coef_ref, diag_ref, blocks_ref, *refs):
    got, got_coefs, (w_ref, next_ref), edges = refs[:4], refs[4:8], refs[8:10], refs[10:14]
    count = v_ref.shape[1]
    beyond = neighbours(sides_ref, cols, count, got, got_coefs)
    for x in range(cols[0]):
        for y in range(cols[1]):
            col = x * cols[1] + y
            w = operate(beyond, cols, v_ref, coef_ref, diag_ref, x, y)
            w_ref[col] = w
            next_ref[col] = apply_blocks(w, blocks_ref, col)
    write_edges(sides_ref, cols, next_ref, None, edges)


def gram(left, right):
    return lax.dot_general(
        left, right, (((1,), (1,)), ((), ())), precision=HIGHEST, preferred_element_type=jnp.float32
    )


def gram_kernel(pairs, *refs):
    arrays, out_ref = refs[:-1], refs[-1]
    count = arrays[0].shape[1]
    for slot, (left, right) in enumerate(pairs):
        total = jnp.zeros((count, count), jnp.float32)
        for col in range(arrays[0].shape[0]):
            total = total + gram(arrays[left][col], arrays[right][col])
        out_ref[:, slot * count : (slot + 1) * count] = total


def last_kernel(cols, sides_ref, v_ref, coef_ref, diag_ref, early_ref, late_ref, *refs):
    got, got_coefs, (w_ref, out_ref) = refs[:4], refs[4:8], refs[8:10]
    count = v_ref.shape[1]
    beyond = neighbours(sides_ref, cols, count, got, got_coefs)
    total = jnp.zeros((count, count), jnp.float32)
    for x in range(cols[0]):
        for y in range(cols[1]):
            col = x * cols[1] + y
            w = operate(beyond, cols, v_ref, coef_ref, diag_ref, x, y)
            w_ref[col] = w
            total = total + gram(v_ref[col], w)
    grams = [early_ref[...], late_ref[...], total]
    used = sum(g.shape[1] for g in grams)
    lanes = out_ref.shape[2]
    grams.append(jnp.zeros((count, lanes - used), jnp.float32))
    joint = jnp.concatenate(grams, axis=1)
    for peer in range(out_ref.shape[0]):
        out_ref[peer] = joint


def symmetric(matrix):
    return 0.5 * (matrix + matrix.T)


def solve_spd(matrix, target):
    size = matrix.shape[0]
    rows = lax.broadcasted_iota(jnp.int32, (size, size), 0)
    lanes = lax.broadcasted_iota(jnp.int32, (size, size), 1)
    eye = rows == lanes
    down = lax.rsqrt(jnp.sum(jnp.where(eye, matrix, 0.0), axis=1, keepdims=True))
    across = lax.rsqrt(jnp.sum(jnp.where(eye, matrix, 0.0), axis=0, keepdims=True))
    work = jnp.concatenate([down * matrix * across, down * target], axis=1)
    width = work.shape[1]
    row_ids = lax.broadcasted_iota(jnp.int32, (size, 1), 0)
    for p in range(size):
        pivot_row = work[p : p + 1, :]
        scaled = pivot_row / pivot_row[:, p : p + 1]
        column = work[:, p : p + 1]
        work = jnp.where(row_ids == p, scaled, work - column * scaled)
    return down * work[:, size:width]


def finish_kernel(blocks, sums_ref, r_ref, *refs):
    v_refs, w_refs, (x_ref, out_ref) = refs[:blocks], refs[blocks : 2 * blocks], refs[2 * blocks :]
    count = r_ref.shape[1]
    joint = sums_ref[0]
    for peer in range(1, sums_ref.shape[0]):
        joint = joint + sums_ref[peer]
    moments = [
        symmetric(joint[:, i * count : (i + 1) * count]) for i in range(2 * blocks)
    ]
    matrix = jnp.concatenate(
        [
            jnp.concatenate([moments[1 + i + j] for j in range(blocks)], axis=1)
            for i in range(blocks)
        ],
        axis=0,
    )
    target = jnp.concatenate(moments[:blocks], axis=0)
    coefs = solve_spd(matrix, target).T
    for col in range(r_ref.shape[0]):
        v = jnp.concatenate([ref[col] for ref in v_refs], axis=0)
        w = jnp.concatenate([ref[col] for ref in w_refs], axis=0)
        x_ref[col] = jnp.dot(coefs, v, precision=HIGHEST, preferred_element_type=jnp.float32)
        out_ref[col] = r_ref[col] - jnp.dot(
            coefs, w, precision=HIGHEST, preferred_element_type=jnp.float32
        )


def exchange(edges):
    out = []
    for slot, edge in enumerate(edges):
        axis = "wide" if slot < 2 else "narrow"
        peers = lax.axis_size(axis)
        pairs = [(i, i + 1) for i in range(slot % 2, peers - 1, 2)]
        out.append(lax.ppermute(edge, axis, pairs + [(j, i) for i, j in pairs]))
    return out


def on_device(sources, well_columns, column_active, perm_root, storage_term, inverse_blocks):
    count, cols_x, cols_y, layers = sources.shape
    cols = (cols_x, cols_y)
    number = cols_x * cols_y
    wide, narrow = lax.axis_index("wide"), lax.axis_index("narrow")
    devices = lax.axis_size("narrow") * lax.axis_size("wide")
    grid_y = cols_y * lax.axis_size("narrow")
    column_ids = (
        (wide * cols_x + jnp.arange(cols_x, dtype=jnp.int32))[:, None] * grid_y
        + narrow * cols_y
        + jnp.arange(cols_y, dtype=jnp.int32)[None, :]
    )
    wells = (column_ids.reshape(-1, 1) == well_columns[None]).astype(jnp.float32)
    active = column_active.astype(jnp.float32)[..., None]
    coef = (perm_root * active).reshape(number, layers)
    diag_term = (active * storage_term + (1.0 - active)).reshape(number, layers)
    rhs = jnp.transpose(sources, (1, 2, 0, 3)).reshape(number, count, layers)
    rhs = rhs + WELL_RATE * wells[..., None]
    blocks = inverse_blocks.reshape((number,) + inverse_blocks.shape[2:])
    sides = jnp.stack([wide % 2, narrow % 2]).astype(jnp.int32)
    state = (number, count, layers)
    apply_flops = 4 * count * number * layers * inverse_blocks.shape[-1]
    gram_flops = 12 * count * count * number * layers

    numbers = (cols_y, cols_y, cols_x, cols_x)
    first_edges = [(n * (count + 1), layers) for n in numbers]
    later_edges = [(n * count, layers) for n in numbers]
    v, *edges = call(
        functools.partial(start_kernel, cols),
        [state] + first_edges,
        [SMEM] + [VMEM] * 3,
        sides, rhs, coef, blocks,
        flops=apply_flops,
    )
    vs, ws, grams = [v], [], []
    got_coefs = got = exchange(edges)
    for j in range(1, ITERS):
        w, v, *edges = call(
            functools.partial(step_kernel, cols),
            [state, state] + later_edges,
            [SMEM] + [VMEM] * 12,
            sides, vs[-1], coef, diag_term, blocks, *got, *got_coefs,
            flops=apply_flops,
        )
        vs.append(v)
        ws.append(w)
        got = exchange(edges)
        arrays = [vs[-2], v, w] + ([rhs] if j == 1 else [])
        pairs = ([(0, 3)] if j == 1 else []) + [(0, 2), (1, 2)]
        grams += call(
            functools.partial(gram_kernel, pairs),
            [(count, len(pairs) * count)],
            [VMEM] * len(arrays),
            *arrays,
            flops=len(pairs) * gram_flops,
        )
    lanes = 128
    w, joint = call(
        functools.partial(last_kernel, cols),
        [state, (devices, count, lanes)],
        [SMEM] + [VMEM] * 13,
        sides, vs[-1], coef, diag_term, *grams, *got, *got_coefs,
        flops=gram_flops,
    )
    ws.append(w)
    joint = lax.all_to_all(joint, ("narrow", "wide"), 0, 0)
    outs = call(
        functools.partial(finish_kernel, ITERS),
        [state, state],
        [VMEM] * (2 + 2 * ITERS),
        joint, rhs, *vs, *ws,
        flops=24 * ITERS * count * count * number * layers,
    )
    return tuple(
        jnp.transpose(o.reshape(cols_x, cols_y, count, layers), (2, 0, 1, 3)) for o in outs
    )


def solution(mesh):
    in_specs = (
        P(None, "wide", "narrow", None),
        P(),
        P("wide", "narrow"),
        P("wide", "narrow", None),
        P("wide", "narrow", None),
        P("wide", "narrow", None, None, None),
    )
    out_specs = (P(None, "wide", "narrow", None), P(None, "wide", "narrow", None))
    return jax.shard_map(
        on_device, mesh=mesh, in_specs=in_specs, out_specs=out_specs, check_vma=False
    )
```

```python
import functools

import jax
import jax.numpy as jnp
from jax import lax
from jax.experimental import pallas as pl
from jax.experimental.pallas import tpu as pltpu
from jax.sharding import PartitionSpec as P

ITERS = 3
WELL_RATE = 4.0
VMEM_BYTES = 24 * 1024 * 1024
VMEM = pl.BlockSpec(memory_space=pltpu.VMEM)
SMEM = pl.BlockSpec(memory_space=pltpu.SMEM)


def call(kernel, out_shape, in_specs, *args, flops=0, scratch=()):
    shapes = [jax.ShapeDtypeStruct(shape, jnp.float32) for shape in out_shape]
    size = sum(a.size * a.dtype.itemsize for a in args) + sum(s.size * 4 for s in shapes)
    return pl.pallas_call(
        kernel,
        out_shape=shapes,
        in_specs=in_specs,
        out_specs=[VMEM] * len(shapes),
        scratch_shapes=list(scratch),
        compiler_params=pltpu.CompilerParams(vmem_limit_bytes=VMEM_BYTES),
        cost_estimate=pl.CostEstimate(flops=flops, bytes_accessed=size, transcendentals=0),
    )(*args)


def split(value):
    high = value.astype(jnp.bfloat16)
    return high, (value - high.astype(jnp.float32)).astype(jnp.bfloat16)


def apply_blocks(value, blocks_ref, col):
    count, layers = value.shape
    parts = []
    size = blocks_ref.shape[-1]
    for b in range(layers // size):
        both = jnp.concatenate(split(value[:, b * size : (b + 1) * size]), axis=0)
        out = jnp.dot(both, blocks_ref[col, b], preferred_element_type=jnp.float32)
        parts.append(out[:count] + out[count:])
    return jnp.concatenate(parts, axis=1)


def write_edges(sides_ref, cols, v_ref, coef_ref, edges):
    cols_x, cols_y = cols
    count = v_ref.shape[1]
    for slot, ref in enumerate(edges):
        odd = sides_ref[slot // 2]
        at_low = odd if slot % 2 == 0 else 1 - odd
        number = cols_y if slot < 2 else cols_x
        for i in range(number):
            if slot < 2:
                col = jnp.where(at_low == 1, 0, (cols_x - 1) * cols_y) + i
            else:
                col = i * cols_y + jnp.where(at_low == 1, 0, cols_y - 1)
            ref[i * count : (i + 1) * count, :] = v_ref[col]
            if coef_ref is not None:
                ref[number * count + i : number * count + i + 1, :] = coef_ref[pl.ds(col, 1), :]


def start_kernel(
    cols, sides_ref, wells_ref, active_ref, sources_ref, perm_ref, storage_ref, blocks_ref,
    r_ref, v_ref, coef_ref, diag_ref, *edges,
):
    cols_x, cols_y = cols
    _, count, layers = r_ref.shape
    row = lax.broadcasted_iota(jnp.int32, (count, layers), 0)
    wells = jnp.zeros((count, layers), jnp.int32)
    for k in range(count):
        wells = jnp.where(row == k, wells_ref[k], wells)
    for x in range(cols_x):
        across = jnp.transpose(sources_ref[:, x], (1, 0, 2))
        for y in range(cols_y):
            col = x * cols_y + y
            active = active_ref[x, y].astype(jnp.float32)
            coef_ref[col : col + 1, :] = active * perm_ref[col : col + 1, :]
            diag_ref[col : col + 1, :] = active * storage_ref[col : col + 1, :] + (1.0 - active)
            column_id = sides_ref[6] + x * sides_ref[7] + y
            r = across[y] + jnp.where(wells == column_id, WELL_RATE, 0.0)
            r_ref[col] = r
            v_ref[col] = apply_blocks(r, blocks_ref, col)
    write_edges(sides_ref, cols, v_ref, coef_ref, edges)


def neighbours(sides_ref, cols, count, got, got_coefs):
    cols_x, cols_y = cols

    def beyond(v_ref, coef_ref, x, y, step_x, step_y):
        nx, ny = x + step_x, y + step_y
        if 0 <= nx < cols_x and 0 <= ny < cols_y:
            col = nx * cols_y + ny
            return v_ref[col], coef_ref[col : col + 1, :]
        if step_x:
            axis, i, number, low = 0, y, cols_y, step_x < 0
        else:
            axis, i, number, low = 1, x, cols_x, step_y < 0
        odd = sides_ref[axis] == 1
        inside = sides_ref[2 + 2 * axis + (0 if low else 1)].astype(jnp.float32)
        first, second = (
            ref[i * count : (i + 1) * count, :] for ref in got[2 * axis : 2 * axis + 2]
        )
        row = number * count + i
        c_first, c_second = (ref[row : row + 1, :] for ref in got_coefs[2 * axis : 2 * axis + 2])
        if low:
            value, coef = jnp.where(odd, first, second), jnp.where(odd, c_first, c_second)
        else:
            value, coef = jnp.where(odd, second, first), jnp.where(odd, c_second, c_first)
        return value, coef * inside

    return beyond


def operate(beyond, cols, v_ref, coef_ref, diag_ref, x, y):
    col = x * cols[1] + y
    center = v_ref[col]
    layers = center.shape[-1]
    coef = coef_ref[col : col + 1, :]
    lane = lax.broadcasted_iota(jnp.int32, (1, layers), 1)
    total = jnp.zeros_like(center)
    for step_x, step_y in ((1, 0), (-1, 0), (0, 1), (0, -1)):
        other, other_coef = beyond(v_ref, coef_ref, x, y, step_x, step_y)
        total = total + other_coef * (center - other)
    upper_coef = jnp.where(lane == layers - 1, 0.0, pltpu.roll(coef, layers - 1, 1))
    lower_coef = jnp.where(lane == 0, 0.0, pltpu.roll(coef, 1, 1))
    total = total + upper_coef * (center - pltpu.roll(center, layers - 1, 1))
    total = total + lower_coef * (center - pltpu.roll(center, 1, 1))
    return diag_ref[col : col + 1, :] * center + coef * total


def step_kernel(cols, sides_ref, v_ref, coef_ref, diag_ref, blocks_ref, *refs):
    got, got_coefs, (w_ref, next_ref), edges = refs[:4], refs[4:8], refs[8:10], refs[10:14]
    count = v_ref.shape[1]
    beyond = neighbours(sides_ref, cols, count, got, got_coefs)
    for x in range(cols[0]):
        for y in range(cols[1]):
            col = x * cols[1] + y
            w = operate(beyond, cols, v_ref, coef_ref, diag_ref, x, y)
            w_ref[col] = w
            next_ref[col] = apply_blocks(w, blocks_ref, col)
    write_edges(sides_ref, cols, next_ref, None, edges)


def split_gram(left, right):
    return lax.dot_general(
        jnp.concatenate(split(left), axis=0),
        jnp.concatenate(split(right), axis=0),
        (((1,), (1,)), ((), ())),
        preferred_element_type=jnp.float32,
    )


def fold(total):
    count = total.shape[0] // 2
    total = total[:count] + total[count:]
    total = total[:, :count] + total[:, count:]
    return 0.5 * (total + total.T)


def gram_kernel(pairs, *refs):
    arrays, out_ref = refs[:-1], refs[-1]
    count = arrays[0].shape[1]
    for slot, (left, right) in enumerate(pairs):
        total = jnp.zeros((2 * count, 2 * count), jnp.float32)
        for col in range(arrays[0].shape[0]):
            total = total + split_gram(arrays[left][col], arrays[right][col])
        out_ref[:, slot * count : (slot + 1) * count] = fold(total)


def pack(squares):
    count = squares[0].shape[0]
    row = lax.broadcasted_iota(jnp.int32, (count, count), 0)
    lane = lax.broadcasted_iota(jnp.int32, (count, count), 1)
    halves = [
        jnp.where(row >= lane, first, second)
        for first, second in zip(squares[0::2], squares[1::2])
    ]
    diagonals = [
        jnp.sum(jnp.where(row == lane, second, 0.0), axis=1, keepdims=True)
        for second in squares[1::2]
    ]
    used = len(halves) * (count + 1)
    packed = jnp.concatenate(
        halves + diagonals + [jnp.zeros((count, 64 - used), jnp.float32)], axis=1
    )
    return jnp.concatenate([packed[: count // 2], packed[count // 2 :]], axis=1)


def unpack(packed, number):
    count = 2 * packed.shape[0]
    packed = jnp.concatenate([packed[:, :64], packed[:, 64:]], axis=0)
    row = lax.broadcasted_iota(jnp.int32, (count, count), 0)
    lane = lax.broadcasted_iota(jnp.int32, (count, count), 1)
    squares = []
    for i in range(number // 2):
        half = packed[:, i * count : (i + 1) * count]
        place = number // 2 * count + i
        turned = half.T
        squares.append(jnp.where(row >= lane, half, turned))
        second = jnp.where(row <= lane, half, turned)
        squares.append(jnp.where(row == lane, packed[:, place : place + 1], second))
    return squares


def last_kernel(cols, sides_ref, v_ref, coef_ref, diag_ref, early_ref, late_ref, *refs):
    got, got_coefs, (w_ref, out_ref) = refs[:4], refs[4:8], refs[8:10]
    count = v_ref.shape[1]
    beyond = neighbours(sides_ref, cols, count, got, got_coefs)
    total = jnp.zeros((2 * count, 2 * count), jnp.float32)
    for x in range(cols[0]):
        for y in range(cols[1]):
            col = x * cols[1] + y
            w = operate(beyond, cols, v_ref, coef_ref, diag_ref, x, y)
            w_ref[col] = w
            total = total + split_gram(v_ref[col], w)
    squares = [
        ref[:, i * count : (i + 1) * count]
        for ref in (early_ref, late_ref)
        for i in range(ref.shape[1] // count)
    ]
    packed = pack(squares + [fold(total)])
    for peer in range(out_ref.shape[0]):
        out_ref[peer] = packed


def solve_spd(matrix, target):
    size = matrix.shape[0]
    rows = lax.broadcasted_iota(jnp.int32, (size, size), 0)
    lanes = lax.broadcasted_iota(jnp.int32, (size, size), 1)
    eye = rows == lanes
    down = lax.rsqrt(jnp.sum(jnp.where(eye, matrix, 0.0), axis=1, keepdims=True))
    across = lax.rsqrt(jnp.sum(jnp.where(eye, matrix, 0.0), axis=0, keepdims=True))
    work = jnp.concatenate([down * matrix * across, down * target], axis=1)
    width = work.shape[1]
    row_ids = lax.broadcasted_iota(jnp.int32, (size, 1), 0)
    for p in range(size):
        pivot_row = work[p : p + 1, :]
        scaled = pivot_row / pivot_row[:, p : p + 1]
        column = work[:, p : p + 1]
        work = jnp.where(row_ids == p, scaled, work - column * scaled)
    return down * work[:, size:width]


def finish_kernel(blocks, sums_ref, r_ref, *refs):
    v_refs, w_refs, (x_ref, out_ref) = refs[:blocks], refs[blocks : 2 * blocks], refs[2 * blocks :]
    cols_x, cols_y = x_ref.shape[1:3]
    joint = sums_ref[0]
    for peer in range(1, sums_ref.shape[0]):
        joint = joint + sums_ref[peer]
    moments = unpack(joint, 2 * blocks)
    matrix = jnp.concatenate(
        [
            jnp.concatenate([moments[1 + i + j] for j in range(blocks)], axis=1)
            for i in range(blocks)
        ],
        axis=0,
    )
    target = jnp.concatenate(moments[:blocks], axis=0)
    coefs = solve_spd(matrix, target).T
    high, rest = coefs.astype(jnp.bfloat16), coefs - coefs.astype(jnp.bfloat16).astype(jnp.float32)
    middle, low = split(rest)
    left = jnp.concatenate([high, high, middle, middle, low], axis=1)

    def combine(values, col):
        highs, lows = zip(*(split(ref[col]) for ref in values))
        right = jnp.concatenate(highs + lows + highs + lows + highs, axis=0)
        return jnp.dot(left, right, preferred_element_type=jnp.float32)

    for x in range(cols_x):
        columns = range(x * cols_y, (x + 1) * cols_y)
        x_ref[:, x] = jnp.transpose(
            jnp.stack([combine(v_refs, col) for col in columns]), (1, 0, 2)
        )
        out_ref[:, x] = jnp.transpose(
            jnp.stack([r_ref[col] - combine(w_refs, col) for col in columns]), (1, 0, 2)
        )


def exchange(edges):
    out = []
    for slot, edge in enumerate(edges):
        axis = "wide" if slot < 2 else "narrow"
        peers = lax.axis_size(axis)
        pairs = [(i, (i + 1) % peers) for i in range(slot % 2, peers, 2)]
        out.append(lax.ppermute(edge, axis, pairs + [(j, i) for i, j in pairs]))
    return out


def on_device(sources, well_columns, column_active, perm_root, storage_term, inverse_blocks):
    count, cols_x, cols_y, layers = sources.shape
    cols = (cols_x, cols_y)
    number = cols_x * cols_y
    wide, narrow = lax.axis_index("wide"), lax.axis_index("narrow")
    peers_x, peers_y = lax.axis_size("wide"), lax.axis_size("narrow")
    grid_y = cols_y * peers_y
    sides = jnp.stack(
        [
            wide % 2,
            narrow % 2,
            (wide > 0).astype(jnp.int32),
            (wide < peers_x - 1).astype(jnp.int32),
            (narrow > 0).astype(jnp.int32),
            (narrow < peers_y - 1).astype(jnp.int32),
            wide * cols_x * grid_y + narrow * cols_y,
            jnp.full((), grid_y, jnp.int32),
        ]
    ).astype(jnp.int32)
    blocks = inverse_blocks.reshape((number,) + inverse_blocks.shape[2:])
    state, rows = (number, count, layers), (number, layers)
    apply_flops = 4 * count * number * layers * inverse_blocks.shape[-1]
    gram_flops = 8 * count * count * number * layers

    numbers = (cols_y, cols_y, cols_x, cols_x)
    first_edges = [(n * (count + 1), layers) for n in numbers]
    later_edges = [(n * count, layers) for n in numbers]
    rhs, v, coef, diag_term, *edges = call(
        functools.partial(start_kernel, cols),
        [state, state, rows, rows] + first_edges,
        [SMEM] * 3 + [VMEM] * 4,
        sides,
        well_columns,
        column_active,
        sources,
        perm_root.reshape(rows),
        storage_term.reshape(rows),
        blocks,
        flops=apply_flops,
    )
    vs, ws, grams = [v], [], []
    got_coefs = got = exchange(edges)
    for j in range(1, ITERS):
        w, v, *edges = call(
            functools.partial(step_kernel, cols),
            [state, state] + later_edges,
            [SMEM] + [VMEM] * 12,
            sides, vs[-1], coef, diag_term, blocks, *got, *got_coefs,
            flops=apply_flops,
        )
        vs.append(v)
        ws.append(w)
        got = exchange(edges)
        arrays = [vs[-2], v, w] + ([rhs] if j == 1 else [])
        pairs = ([(0, 3)] if j == 1 else []) + [(0, 2), (1, 2)]
        grams += call(
            functools.partial(gram_kernel, pairs),
            [(count, len(pairs) * count)],
            [VMEM] * len(arrays),
            *arrays,
            flops=len(pairs) * gram_flops,
        )
    w, joint = call(
        functools.partial(last_kernel, cols),
        [state, (peers_x * peers_y, count // 2, 128)],
        [SMEM] + [VMEM] * 13,
        sides, vs[-1], coef, diag_term, *grams, *got, *got_coefs,
        flops=gram_flops,
    )
    ws.append(w)
    joint = lax.all_to_all(joint, ("narrow", "wide"), 0, 0)
    outs = call(
        functools.partial(finish_kernel, ITERS),
        [sources.shape] * 2,
        [VMEM] * (2 + 2 * ITERS),
        joint, rhs, *vs, *ws,
        flops=24 * ITERS * count * count * number * layers,
    )
    return tuple(outs)


def solution(mesh):
    in_specs = (
        P(None, "wide", "narrow", None),
        P(),
        P("wide", "narrow"),
        P("wide", "narrow", None),
        P("wide", "narrow", None),
        P("wide", "narrow", None, None, None),
    )
    out_specs = (P(None, "wide", "narrow", None), P(None, "wide", "narrow", None))
    return jax.shard_map(
        on_device, mesh=mesh, in_specs=in_specs, out_specs=out_specs, check_vma=False
    )
```

```python
import functools

import jax
import jax.numpy as jnp
from jax import lax
from jax.experimental import pallas as pl
from jax.experimental.pallas import tpu as pltpu
from jax.sharding import PartitionSpec as P

ITERS = 3
WELL_RATE = 4.0
VMEM_BYTES = 24 * 1024 * 1024
VMEM = pl.BlockSpec(memory_space=pltpu.VMEM)
SMEM = pl.BlockSpec(memory_space=pltpu.SMEM)
HBM = pl.BlockSpec(memory_space=pltpu.HBM)
SCALE = 64.0
AHEAD = 6


def call(kernel, out_shape, in_specs, *args, flops=0, out_specs=None, scratch=()):
    shapes = [
        s if isinstance(s, jax.ShapeDtypeStruct) else jax.ShapeDtypeStruct(s, jnp.float32)
        for s in out_shape
    ]
    size = sum(a.size * a.dtype.itemsize for a in args) + sum(s.size * 4 for s in shapes)
    return pl.pallas_call(
        kernel,
        out_shape=shapes,
        in_specs=in_specs,
        out_specs=out_specs or [VMEM] * len(shapes),
        scratch_shapes=list(scratch),
        compiler_params=pltpu.CompilerParams(vmem_limit_bytes=VMEM_BYTES),
        cost_estimate=pl.CostEstimate(flops=flops, bytes_accessed=size, transcendentals=0),
    )(*args)


def split(value):
    high = value.astype(jnp.bfloat16)
    return high, (value - high.astype(jnp.float32)).astype(jnp.bfloat16)


def apply_blocks(value, blocks_ref, col):
    count, layers = value.shape
    parts = []
    size = blocks_ref.shape[-1]
    for b in range(layers // size):
        both = jnp.concatenate(split(value[:, b * size : (b + 1) * size]), axis=0)
        out = jnp.dot(both, blocks_ref[col, b], preferred_element_type=jnp.float32)
        parts.append(out[:count] + out[count:])
    return jnp.concatenate(parts, axis=1)


def write_edges(sides_ref, cols, v_ref, coef_ref, edges):
    cols_x, cols_y = cols
    count = v_ref.shape[1]
    for slot, ref in enumerate(edges):
        odd = sides_ref[slot // 2]
        at_low = odd if slot % 2 == 0 else 1 - odd
        number = cols_y if slot < 2 else cols_x
        for i in range(number):
            if slot < 2:
                col = jnp.where(at_low == 1, 0, (cols_x - 1) * cols_y) + i
            else:
                col = i * cols_y + jnp.where(at_low == 1, 0, cols_y - 1)
            ref[i * count : (i + 1) * count, :] = v_ref[col]
            if coef_ref is not None:
                ref[number * count + i : number * count + i + 1, :] = coef_ref[pl.ds(col, 1), :]


def start_kernel(
    cols, sides_ref, wells_hbm, active_hbm, sources_hbm, perm_hbm, storage_hbm, blocks_hbm,
    r_ref, v_ref, coef_ref, diag_ref, blocks_ref, *refs,
):
    edges = refs[:4]
    wells_ref, active_ref, sources_ref, perm_ref, storage_ref, small_sem, big_sem, block_sem = refs[4:]
    cols_x, cols_y = cols
    _, count, layers = r_ref.shape
    small = [
        pltpu.make_async_copy(source, target, small_sem.at[i])
        for i, (source, target) in enumerate(
            (
                (wells_hbm, wells_ref),
                (active_hbm, active_ref),
                (perm_hbm, perm_ref),
                (storage_hbm, storage_ref),
            )
        )
    ]
    sources = [
        pltpu.make_async_copy(sources_hbm.at[:, x], sources_ref.at[:, x], big_sem.at[x])
        for x in range(cols_x)
    ]
    blocks = [
        pltpu.make_async_copy(
            blocks_hbm.at[pl.ds(x * cols_y, cols_y)],
            blocks_ref.at[pl.ds(x * cols_y, cols_y)],
            block_sem.at[x],
        )
        for x in range(cols_x)
    ]
    for copy in small:
        copy.start()
    for pair in zip(sources, blocks):
        for copy in pair:
            copy.start()
    for copy in small:
        copy.wait()
    row = lax.broadcasted_iota(jnp.int32, (count, layers), 0)
    wells = jnp.zeros((count, layers), jnp.int32)
    for k in range(count):
        wells = jnp.where(row == k, wells_ref[k], wells)
    for x in range(cols_x):
        for y in range(cols_y):
            col = x * cols_y + y
            active = active_ref[x, y].astype(jnp.float32)
            coef_ref[col : col + 1, :] = active * perm_ref[col : col + 1, :]
            diag_ref[col : col + 1, :] = active * storage_ref[col : col + 1, :] + (1.0 - active)
    for x in range(cols_x):
        sources[x].wait()
        across = jnp.transpose(sources_ref[:, x], (1, 0, 2))
        blocks[x].wait()
        for y in range(cols_y):
            col = x * cols_y + y
            column_id = sides_ref[6] + x * sides_ref[7] + y
            r = across[y] + jnp.where(wells == column_id, WELL_RATE, 0.0)
            r_ref[col] = r
            v_ref[col] = apply_blocks(r, blocks_ref, col)
    write_edges(sides_ref, cols, v_ref, coef_ref, edges)


def neighbours(sides_ref, cols, count, got, got_coefs):
    cols_x, cols_y = cols

    def beyond(v_ref, coef_ref, x, y, step_x, step_y):
        nx, ny = x + step_x, y + step_y
        if 0 <= nx < cols_x and 0 <= ny < cols_y:
            col = nx * cols_y + ny
            return v_ref[col], coef_ref[col : col + 1, :]
        if step_x:
            axis, i, number, low = 0, y, cols_y, step_x < 0
        else:
            axis, i, number, low = 1, x, cols_x, step_y < 0
        odd = sides_ref[axis] == 1
        inside = sides_ref[2 + 2 * axis + (0 if low else 1)].astype(jnp.float32)
        first, second = (
            ref[i * count : (i + 1) * count, :] for ref in got[2 * axis : 2 * axis + 2]
        )
        row = number * count + i
        c_first, c_second = (ref[row : row + 1, :] for ref in got_coefs[2 * axis : 2 * axis + 2])
        if low:
            value, coef = jnp.where(odd, first, second), jnp.where(odd, c_first, c_second)
        else:
            value, coef = jnp.where(odd, second, first), jnp.where(odd, c_second, c_first)
        return value, coef * inside

    return beyond


def operate(beyond, cols, v_ref, coef_ref, diag_ref, x, y):
    col = x * cols[1] + y
    center = v_ref[col]
    layers = center.shape[-1]
    coef = coef_ref[col : col + 1, :]
    lane = lax.broadcasted_iota(jnp.int32, (1, layers), 1)
    total = jnp.zeros_like(center)
    for step_x, step_y in ((1, 0), (-1, 0), (0, 1), (0, -1)):
        other, other_coef = beyond(v_ref, coef_ref, x, y, step_x, step_y)
        total = total + other_coef * (center - other)
    upper_coef = jnp.where(lane == layers - 1, 0.0, pltpu.roll(coef, layers - 1, 1))
    lower_coef = jnp.where(lane == 0, 0.0, pltpu.roll(coef, 1, 1))
    total = total + upper_coef * (center - pltpu.roll(center, layers - 1, 1))
    total = total + lower_coef * (center - pltpu.roll(center, 1, 1))
    return (diag_ref[col : col + 1, :] * center + coef * total) * (1.0 / SCALE)


def step_kernel(cols, sides_ref, v_ref, coef_ref, diag_ref, blocks_ref, *refs):
    got, got_coefs, (w_ref, next_ref), edges = refs[:4], refs[4:8], refs[8:10], refs[10:14]
    count = v_ref.shape[1]
    beyond = neighbours(sides_ref, cols, count, got, got_coefs)
    for x in range(cols[0]):
        for y in range(cols[1]):
            col = x * cols[1] + y
            w = operate(beyond, cols, v_ref, coef_ref, diag_ref, x, y)
            w_ref[col] = w
            next_ref[col] = apply_blocks(w, blocks_ref, col)
    write_edges(sides_ref, cols, next_ref, None, edges)


def split_gram(left, right):
    return lax.dot_general(
        jnp.concatenate(split(left), axis=0),
        jnp.concatenate(split(right), axis=0),
        (((1,), (1,)), ((), ())),
        preferred_element_type=jnp.float32,
    )


def fold(total):
    count = total.shape[0] // 2
    total = total[:count] + total[count:]
    total = total[:, :count] + total[:, count:]
    return 0.5 * (total + total.T)


def gram_kernel(pairs, *refs):
    arrays, out_ref = refs[:-1], refs[-1]
    count = arrays[0].shape[1]
    for slot, (left, right) in enumerate(pairs):
        total = jnp.zeros((2 * count, 2 * count), jnp.float32)
        for col in range(arrays[0].shape[0]):
            total = total + split_gram(arrays[left][col], arrays[right][col])
        out_ref[:, slot * count : (slot + 1) * count] = fold(total)


def pack(squares):
    count = squares[0].shape[0]
    row = lax.broadcasted_iota(jnp.int32, (count, count), 0)
    lane = lax.broadcasted_iota(jnp.int32, (count, count), 1)
    halves = [
        jnp.where(row >= lane, first, second)
        for first, second in zip(squares[0::2], squares[1::2])
    ]
    diagonals = [
        jnp.sum(jnp.where(row == lane, second, 0.0), axis=1, keepdims=True)
        for second in squares[1::2]
    ]
    used = len(halves) * (count + 1)
    packed = jnp.concatenate(
        halves + diagonals + [jnp.zeros((count, 64 - used), jnp.float32)], axis=1
    )
    return jnp.concatenate([packed[: count // 2], packed[count // 2 :]], axis=1)


def unpack(packed, number):
    count = 2 * packed.shape[0]
    packed = jnp.concatenate([packed[:, :64], packed[:, 64:]], axis=0)
    row = lax.broadcasted_iota(jnp.int32, (count, count), 0)
    lane = lax.broadcasted_iota(jnp.int32, (count, count), 1)
    squares = []
    for i in range(number // 2):
        half = packed[:, i * count : (i + 1) * count]
        place = number // 2 * count + i
        turned = half.T
        squares.append(jnp.where(row >= lane, half, turned))
        second = jnp.where(row <= lane, half, turned)
        squares.append(jnp.where(row == lane, packed[:, place : place + 1], second))
    return squares


def last_kernel(cols, sides_ref, v_ref, coef_ref, diag_ref, early_ref, late_ref, *refs):
    got, got_coefs, (w_ref, out_ref) = refs[:4], refs[4:8], refs[8:10]
    count = v_ref.shape[1]
    beyond = neighbours(sides_ref, cols, count, got, got_coefs)
    total = jnp.zeros((2 * count, 2 * count), jnp.float32)
    for x in range(cols[0]):
        for y in range(cols[1]):
            col = x * cols[1] + y
            w = operate(beyond, cols, v_ref, coef_ref, diag_ref, x, y)
            w_ref[col] = w
            total = total + split_gram(v_ref[col], w)
    squares = [
        ref[:, i * count : (i + 1) * count]
        for ref in (early_ref, late_ref)
        for i in range(ref.shape[1] // count)
    ]
    packed = pack(squares + [fold(total)])
    for peer in range(out_ref.shape[0]):
        out_ref[peer] = packed


def solve_spd(matrix, target):
    size, width = matrix.shape[0], matrix.shape[1] + target.shape[1]
    lanes = 128
    work = jnp.concatenate(
        [matrix, target, jnp.zeros((size, lanes - width), jnp.float32)], axis=1
    )
    row = lax.broadcasted_iota(jnp.int32, (size, lanes), 0)

    def spread(p):
        return jnp.broadcast_to(work[:, p : p + 1], (size, lanes))

    ahead = {p: spread(p) for p in range(AHEAD)}
    inverses = jnp.zeros((size, lanes), jnp.float32)
    for p in range(size):
        column = ahead.pop(p)
        if p + AHEAD < size:
            ahead[p + AHEAD] = spread(p + AHEAD)
        inverse = 1.0 / column[p : p + 1, :]
        inverses = jnp.where(row == p, inverse, inverses)
        factor = jnp.where(row == p, 0.0, column)

        def eliminate(value):
            return value - factor * jnp.broadcast_to(value[p : p + 1, :] * inverse, value.shape)

        ahead = {q: eliminate(value) for q, value in ahead.items()}
        work = eliminate(work)
    return work[:, size:width] * inverses[:, size:width]


def finish_kernel(blocks, sums_ref, r_ref, *refs):
    v_refs, w_refs, (x_hbm, out_hbm) = refs[:blocks], refs[blocks : 2 * blocks], refs[2 * blocks : 2 * blocks + 2]
    x_ref, out_ref, sem = refs[2 * blocks + 2 :]
    cols_x, cols_y = x_ref.shape[1:3]
    joint = sums_ref[0]
    for peer in range(1, sums_ref.shape[0]):
        joint = joint + sums_ref[peer]
    moments = unpack(joint, 2 * blocks)
    matrix = jnp.concatenate(
        [
            jnp.concatenate([moments[1 + i + j] for j in range(blocks)], axis=1)
            for i in range(blocks)
        ],
        axis=0,
    )
    target = jnp.concatenate(moments[:blocks], axis=0)
    coefs = solve_spd(matrix, target).T
    high = coefs.astype(jnp.bfloat16)
    middle, low = split(coefs - high.astype(jnp.float32))
    left = jnp.concatenate([high, high, middle, middle, low], axis=1)

    def combine(values, col):
        highs, lows = zip(*(split(ref[col]) for ref in values))
        right = jnp.concatenate(highs + lows + highs + lows + highs, axis=0)
        return jnp.dot(left, right, preferred_element_type=jnp.float32)

    copies = []
    for x in range(cols_x):
        columns = range(x * cols_y, (x + 1) * cols_y)
        out_ref[:, x] = jnp.transpose(
            jnp.stack([r_ref[col] - combine(w_refs, col) for col in columns]), (1, 0, 2)
        )
        copies.append(
            pltpu.make_async_copy(out_ref.at[:, x], out_hbm.at[:, x], sem.at[2 * x])
        )
        copies[-1].start()
        x_ref[:, x] = jnp.transpose(
            jnp.stack([combine(v_refs, col) * (1.0 / SCALE) for col in columns]), (1, 0, 2)
        )
        copies.append(
            pltpu.make_async_copy(x_ref.at[:, x], x_hbm.at[:, x], sem.at[2 * x + 1])
        )
        copies[-1].start()
    for copy in copies:
        copy.wait()


def exchange(edges):
    out = []
    for slot, edge in enumerate(edges):
        axis = "wide" if slot < 2 else "narrow"
        peers = lax.axis_size(axis)
        pairs = [(i, (i + 1) % peers) for i in range(slot % 2, peers, 2)]
        out.append(lax.ppermute(edge, axis, pairs + [(j, i) for i, j in pairs]))
    return out


def on_device(sources, well_columns, column_active, perm_root, storage_term, inverse_blocks):
    count, cols_x, cols_y, layers = sources.shape
    cols = (cols_x, cols_y)
    number = cols_x * cols_y
    wide, narrow = lax.axis_index("wide"), lax.axis_index("narrow")
    peers_x, peers_y = lax.axis_size("wide"), lax.axis_size("narrow")
    grid_y = cols_y * peers_y
    sides = jnp.stack(
        [
            wide % 2,
            narrow % 2,
            (wide > 0).astype(jnp.int32),
            (wide < peers_x - 1).astype(jnp.int32),
            (narrow > 0).astype(jnp.int32),
            (narrow < peers_y - 1).astype(jnp.int32),
            wide * cols_x * grid_y + narrow * cols_y,
            jnp.full((), grid_y, jnp.int32),
        ]
    ).astype(jnp.int32)
    blocks = inverse_blocks.reshape((number,) + inverse_blocks.shape[2:])
    state, rows = (number, count, layers), (number, layers)
    apply_flops = 4 * count * number * layers * inverse_blocks.shape[-1]
    gram_flops = 8 * count * count * number * layers

    numbers = (cols_y, cols_y, cols_x, cols_x)
    first_edges = [(n * (count + 1), layers) for n in numbers]
    later_edges = [(n * count, layers) for n in numbers]
    rhs, v, coef, diag_term, blocks, *edges = call(
        functools.partial(start_kernel, cols),
        [state, state, rows, rows, jax.ShapeDtypeStruct(blocks.shape, blocks.dtype)]
        + first_edges,
        [SMEM] + [HBM] * 6,
        sides,
        well_columns,
        column_active,
        sources,
        perm_root.reshape(rows),
        storage_term.reshape(rows),
        blocks,
        flops=apply_flops,
        scratch=[
            pltpu.SMEM(well_columns.shape, jnp.int32),
            pltpu.SMEM(column_active.shape, jnp.int32),
            pltpu.VMEM(sources.shape, jnp.float32),
            pltpu.VMEM(rows, jnp.float32),
            pltpu.VMEM(rows, jnp.float32),
            pltpu.SemaphoreType.DMA((4,)),
            pltpu.SemaphoreType.DMA((cols_x,)),
            pltpu.SemaphoreType.DMA((cols_x,)),
        ],
    )
    vs, ws, grams = [v], [], []
    got_coefs = got = exchange(edges)
    for j in range(1, ITERS):
        w, v, *edges = call(
            functools.partial(step_kernel, cols),
            [state, state] + later_edges,
            [SMEM] + [VMEM] * 12,
            sides, vs[-1], coef, diag_term, blocks, *got, *got_coefs,
            flops=apply_flops,
        )
        vs.append(v)
        ws.append(w)
        got = exchange(edges)
        arrays = [vs[-2], v, w] + ([rhs] if j == 1 else [])
        pairs = ([(0, 3)] if j == 1 else []) + [(0, 2), (1, 2)]
        grams += call(
            functools.partial(gram_kernel, pairs),
            [(count, len(pairs) * count)],
            [VMEM] * len(arrays),
            *arrays,
            flops=len(pairs) * gram_flops,
        )
    w, joint = call(
        functools.partial(last_kernel, cols),
        [state, (peers_x * peers_y, count // 2, 128)],
        [SMEM] + [VMEM] * 13,
        sides, vs[-1], coef, diag_term, *grams, *got, *got_coefs,
        flops=gram_flops,
    )
    ws.append(w)
    joint = lax.all_to_all(joint, ("narrow", "wide"), 0, 0)
    outs = call(
        functools.partial(finish_kernel, ITERS),
        [sources.shape] * 2,
        [VMEM] * (2 + 2 * ITERS),
        joint, rhs, *vs, *ws,
        flops=24 * ITERS * count * count * number * layers,
        out_specs=[HBM, HBM],
        scratch=[
            pltpu.VMEM(sources.shape, jnp.float32),
            pltpu.VMEM(sources.shape, jnp.float32),
            pltpu.SemaphoreType.DMA((2 * cols_x,)),
        ],
    )
    return tuple(outs)


def solution(mesh):
    in_specs = (
        P(None, "wide", "narrow", None),
        P(),
        P("wide", "narrow"),
        P("wide", "narrow", None),
        P("wide", "narrow", None),
        P("wide", "narrow", None, None, None),
    )
    out_specs = (P(None, "wide", "narrow", None), P(None, "wide", "narrow", None))
    return jax.shard_map(
        on_device, mesh=mesh, in_specs=in_specs, out_specs=out_specs, check_vma=False
    )
```

```python
import functools

import jax
import jax.numpy as jnp
from jax import lax
from jax.experimental import pallas as pl
from jax.experimental.pallas import tpu as pltpu
from jax.sharding import PartitionSpec as P

ITERS = 3
WELL_RATE = 4.0
VMEM_BYTES = 24 * 1024 * 1024
VMEM = pl.BlockSpec(memory_space=pltpu.VMEM)
SMEM = pl.BlockSpec(memory_space=pltpu.SMEM)
HBM = pl.BlockSpec(memory_space=pltpu.HBM)
SCALE = 64.0
AHEAD = 6


def call(kernel, out_shape, in_specs, *args, flops=0, out_specs=None, scratch=()):
    shapes = [
        s if isinstance(s, jax.ShapeDtypeStruct) else jax.ShapeDtypeStruct(s, jnp.float32)
        for s in out_shape
    ]
    size = sum(a.size * a.dtype.itemsize for a in args) + sum(s.size * 4 for s in shapes)
    return pl.pallas_call(
        kernel,
        out_shape=shapes,
        in_specs=in_specs,
        out_specs=out_specs or [VMEM] * len(shapes),
        scratch_shapes=list(scratch),
        compiler_params=pltpu.CompilerParams(vmem_limit_bytes=VMEM_BYTES),
        cost_estimate=pl.CostEstimate(flops=flops, bytes_accessed=size, transcendentals=0),
    )(*args)


def split(value):
    high = value.astype(jnp.bfloat16)
    return high, (value - high.astype(jnp.float32)).astype(jnp.bfloat16)


def apply_blocks(value, blocks_ref, col):
    count, layers = value.shape
    parts = []
    size = blocks_ref.shape[-1]
    for b in range(layers // size):
        both = jnp.concatenate(split(value[:, b * size : (b + 1) * size]), axis=0)
        out = jnp.dot(both, blocks_ref[col, b], preferred_element_type=jnp.float32)
        parts.append(out[:count] + out[count:])
    return jnp.concatenate(parts, axis=1)


def write_edges(sides_ref, cols, v_ref, coef_ref, edges):
    cols_x, cols_y = cols
    count = v_ref.shape[1]
    for slot, ref in enumerate(edges):
        odd = sides_ref[slot // 2]
        at_low = odd if slot % 2 == 0 else 1 - odd
        number = cols_y if slot < 2 else cols_x
        for i in range(number):
            if slot < 2:
                col = jnp.where(at_low == 1, 0, (cols_x - 1) * cols_y) + i
            else:
                col = i * cols_y + jnp.where(at_low == 1, 0, cols_y - 1)
            ref[i * count : (i + 1) * count, :] = v_ref[col]
            if coef_ref is not None:
                ref[number * count + i : number * count + i + 1, :] = coef_ref[pl.ds(col, 1), :]


def start_kernel(
    cols, sides_ref, wells_hbm, active_hbm, sources_hbm, perm_hbm, storage_hbm, blocks_hbm,
    r_ref, v_ref, coef_ref, diag_ref, blocks_ref, *refs,
):
    edges = refs[:4]
    wells_ref, active_ref, sources_ref, perm_ref, storage_ref, small_sem, big_sem, block_sem = refs[4:]
    cols_x, cols_y = cols
    _, count, layers = r_ref.shape
    small = [
        pltpu.make_async_copy(source, target, small_sem.at[i])
        for i, (source, target) in enumerate(
            (
                (wells_hbm, wells_ref),
                (active_hbm, active_ref),
                (perm_hbm, perm_ref),
                (storage_hbm, storage_ref),
            )
        )
    ]
    sources = [
        pltpu.make_async_copy(sources_hbm.at[:, x], sources_ref.at[:, x], big_sem.at[x])
        for x in range(cols_x)
    ]
    blocks = [
        pltpu.make_async_copy(
            blocks_hbm.at[pl.ds(x * cols_y, cols_y)],
            blocks_ref.at[pl.ds(x * cols_y, cols_y)],
            block_sem.at[x],
        )
        for x in range(cols_x)
    ]
    for copy in small:
        copy.start()
    for pair in zip(sources, blocks):
        for copy in pair:
            copy.start()
    for copy in small:
        copy.wait()
    row = lax.broadcasted_iota(jnp.int32, (count, layers), 0)
    wells = jnp.zeros((count, layers), jnp.int32)
    for k in range(count):
        wells = jnp.where(row == k, wells_ref[k], wells)
    for x in range(cols_x):
        for y in range(cols_y):
            col = x * cols_y + y
            active = active_ref[x, y].astype(jnp.float32)
            coef_ref[col : col + 1, :] = active * perm_ref[col : col + 1, :]
            diag_ref[col : col + 1, :] = active * storage_ref[col : col + 1, :] + (1.0 - active)
    for x in range(cols_x):
        sources[x].wait()
        across = jnp.transpose(sources_ref[:, x], (1, 0, 2))
        blocks[x].wait()
        for y in range(cols_y):
            col = x * cols_y + y
            column_id = sides_ref[6] + x * sides_ref[7] + y
            r = across[y] + jnp.where(wells == column_id, WELL_RATE, 0.0)
            r_ref[col] = r
            v_ref[col] = apply_blocks(r, blocks_ref, col)
    write_edges(sides_ref, cols, v_ref, coef_ref, edges)


def neighbours(sides_ref, cols, count, got, got_coefs):
    cols_x, cols_y = cols

    def beyond(v_ref, coef_ref, x, y, step_x, step_y):
        nx, ny = x + step_x, y + step_y
        if 0 <= nx < cols_x and 0 <= ny < cols_y:
            col = nx * cols_y + ny
            return v_ref[col], coef_ref[col : col + 1, :]
        if step_x:
            axis, i, number, low = 0, y, cols_y, step_x < 0
        else:
            axis, i, number, low = 1, x, cols_x, step_y < 0
        odd = sides_ref[axis] == 1
        inside = sides_ref[2 + 2 * axis + (0 if low else 1)].astype(jnp.float32)
        first, second = (
            ref[i * count : (i + 1) * count, :] for ref in got[2 * axis : 2 * axis + 2]
        )
        row = number * count + i
        c_first, c_second = (ref[row : row + 1, :] for ref in got_coefs[2 * axis : 2 * axis + 2])
        if low:
            value, coef = jnp.where(odd, first, second), jnp.where(odd, c_first, c_second)
        else:
            value, coef = jnp.where(odd, second, first), jnp.where(odd, c_second, c_first)
        return value, coef * inside

    return beyond


def operate(beyond, cols, v_ref, coef_ref, diag_ref, x, y):
    col = x * cols[1] + y
    center = v_ref[col]
    layers = center.shape[-1]
    coef = coef_ref[col : col + 1, :]
    lane = lax.broadcasted_iota(jnp.int32, (1, layers), 1)
    total = jnp.zeros_like(center)
    for step_x, step_y in ((1, 0), (-1, 0), (0, 1), (0, -1)):
        other, other_coef = beyond(v_ref, coef_ref, x, y, step_x, step_y)
        total = total + other_coef * (center - other)
    upper_coef = jnp.where(lane == layers - 1, 0.0, pltpu.roll(coef, layers - 1, 1))
    lower_coef = jnp.where(lane == 0, 0.0, pltpu.roll(coef, 1, 1))
    total = total + upper_coef * (center - pltpu.roll(center, layers - 1, 1))
    total = total + lower_coef * (center - pltpu.roll(center, 1, 1))
    return (diag_ref[col : col + 1, :] * center + coef * total) * (1.0 / SCALE)


def step_kernel(cols, sides_ref, v_ref, coef_ref, diag_ref, blocks_ref, *refs):
    got, got_coefs, (w_ref, next_ref), edges = refs[:4], refs[4:8], refs[8:10], refs[10:14]
    count = v_ref.shape[1]
    beyond = neighbours(sides_ref, cols, count, got, got_coefs)
    for x in range(cols[0]):
        for y in range(cols[1]):
            col = x * cols[1] + y
            w = operate(beyond, cols, v_ref, coef_ref, diag_ref, x, y)
            w_ref[col] = w
            next_ref[col] = apply_blocks(w, blocks_ref, col)
    write_edges(sides_ref, cols, next_ref, None, edges)


def split_gram(left, right):
    return lax.dot_general(
        jnp.concatenate(split(left), axis=0),
        jnp.concatenate(split(right), axis=0),
        (((1,), (1,)), ((), ())),
        preferred_element_type=jnp.float32,
    )


def fold(total):
    count = total.shape[0] // 2
    total = total[:count] + total[count:]
    total = total[:, :count] + total[:, count:]
    return 0.5 * (total + total.T)


def gram_kernel(pairs, *refs):
    arrays, out_ref = refs[:-1], refs[-1]
    count = arrays[0].shape[1]
    for slot, (left, right) in enumerate(pairs):
        total = jnp.zeros((2 * count, 2 * count), jnp.float32)
        for col in range(arrays[0].shape[0]):
            total = total + split_gram(arrays[left][col], arrays[right][col])
        out_ref[:, slot * count : (slot + 1) * count] = fold(total)


def pack(squares):
    count = squares[0].shape[0]
    row = lax.broadcasted_iota(jnp.int32, (count, count), 0)
    lane = lax.broadcasted_iota(jnp.int32, (count, count), 1)
    halves = [
        jnp.where(row >= lane, first, second)
        for first, second in zip(squares[0::2], squares[1::2])
    ]
    diagonals = [
        jnp.sum(jnp.where(row == lane, second, 0.0), axis=1, keepdims=True)
        for second in squares[1::2]
    ]
    used = len(halves) * (count + 1)
    packed = jnp.concatenate(
        halves + diagonals + [jnp.zeros((count, 64 - used), jnp.float32)], axis=1
    )
    return jnp.concatenate([packed[: count // 2], packed[count // 2 :]], axis=1)


def unpack(packed, number):
    count = 2 * packed.shape[0]
    packed = jnp.concatenate([packed[:, :64], packed[:, 64:]], axis=0)
    row = lax.broadcasted_iota(jnp.int32, (count, count), 0)
    lane = lax.broadcasted_iota(jnp.int32, (count, count), 1)
    squares = []
    for i in range(number // 2):
        half = packed[:, i * count : (i + 1) * count]
        place = number // 2 * count + i
        turned = half.T
        squares.append(jnp.where(row >= lane, half, turned))
        second = jnp.where(row <= lane, half, turned)
        squares.append(jnp.where(row == lane, packed[:, place : place + 1], second))
    return squares


def last_kernel(cols, sides_ref, v_ref, coef_ref, diag_ref, early_ref, late_ref, *refs):
    got, got_coefs, (w_ref, out_ref) = refs[:4], refs[4:8], refs[8:10]
    count = v_ref.shape[1]
    beyond = neighbours(sides_ref, cols, count, got, got_coefs)
    total = jnp.zeros((2 * count, 2 * count), jnp.float32)
    for x in range(cols[0]):
        for y in range(cols[1]):
            col = x * cols[1] + y
            w = operate(beyond, cols, v_ref, coef_ref, diag_ref, x, y)
            w_ref[col] = w
            total = total + split_gram(v_ref[col], w)
    squares = [
        ref[:, i * count : (i + 1) * count]
        for ref in (early_ref, late_ref)
        for i in range(ref.shape[1] // count)
    ]
    packed = pack(squares + [fold(total)])
    for peer in range(out_ref.shape[0]):
        out_ref[peer] = packed


def solve_spd(matrix, target):
    size, width = matrix.shape[0], matrix.shape[1] + target.shape[1]
    lanes = 128
    work = jnp.concatenate(
        [matrix, target, jnp.zeros((size, lanes - width), jnp.float32)], axis=1
    )
    row = lax.broadcasted_iota(jnp.int32, (size, lanes), 0)

    def spread(p):
        return jnp.broadcast_to(work[:, p : p + 1], (size, lanes))

    ahead = {p: spread(p) for p in range(AHEAD)}
    inverses = jnp.zeros((size, lanes), jnp.float32)
    for p in range(size):
        column = ahead.pop(p)
        if p + AHEAD < size:
            ahead[p + AHEAD] = spread(p + AHEAD)
        inverse = 1.0 / column[p : p + 1, :]
        inverses = jnp.where(row == p, inverse, inverses)
        factor = jnp.where(row == p, 0.0, column)

        def eliminate(value):
            return value - factor * jnp.broadcast_to(value[p : p + 1, :] * inverse, value.shape)

        ahead = {q: eliminate(value) for q, value in ahead.items()}
        work = eliminate(work)
    return work[:, size:width] * inverses[:, size:width]


def finish_kernel(blocks, sums_ref, r_ref, *refs):
    v_refs, w_refs, (x_hbm, out_hbm) = refs[:blocks], refs[blocks : 2 * blocks], refs[2 * blocks : 2 * blocks + 2]
    x_ref, out_ref, sem = refs[2 * blocks + 2 :]
    cols_x, cols_y = x_ref.shape[1:3]
    joint = sums_ref[0]
    for peer in range(1, sums_ref.shape[0]):
        joint = joint + sums_ref[peer]
    moments = unpack(joint, 2 * blocks)
    matrix = jnp.concatenate(
        [
            jnp.concatenate([moments[1 + i + j] for j in range(blocks)], axis=1)
            for i in range(blocks)
        ],
        axis=0,
    )
    target = jnp.concatenate(moments[:blocks], axis=0)
    coefs = solve_spd(matrix, target).T
    high = coefs.astype(jnp.bfloat16)
    middle, low = split(coefs - high.astype(jnp.float32))
    left = jnp.concatenate([high, high, middle, middle, low], axis=1)

    def combine(values, col):
        highs, lows = zip(*(split(ref[col]) for ref in values))
        right = jnp.concatenate(highs + lows + highs + lows + highs, axis=0)
        return jnp.dot(left, right, preferred_element_type=jnp.float32)

    copies = []
    for x in range(cols_x):
        columns = range(x * cols_y, (x + 1) * cols_y)
        out_ref[:, x] = jnp.transpose(
            jnp.stack([r_ref[col] - combine(w_refs, col) for col in columns]), (1, 0, 2)
        )
        copies.append(
            pltpu.make_async_copy(out_ref.at[:, x], out_hbm.at[:, x], sem.at[2 * x])
        )
        copies[-1].start()
        x_ref[:, x] = jnp.transpose(
            jnp.stack([combine(v_refs, col) * (1.0 / SCALE) for col in columns]), (1, 0, 2)
        )
        copies.append(
            pltpu.make_async_copy(x_ref.at[:, x], x_hbm.at[:, x], sem.at[2 * x + 1])
        )
        copies[-1].start()
    for copy in copies:
        copy.wait()


def exchange(edges):
    out = []
    for slot, edge in enumerate(edges):
        axis = "wide" if slot < 2 else "narrow"
        peers = lax.axis_size(axis)
        pairs = [(i, (i + 1) % peers) for i in range(slot % 2, peers, 2)]
        out.append(lax.ppermute(edge, axis, pairs + [(j, i) for i, j in pairs]))
    return out


def on_device(sources, well_columns, column_active, perm_root, storage_term, inverse_blocks):
    count, cols_x, cols_y, layers = sources.shape
    cols = (cols_x, cols_y)
    number = cols_x * cols_y
    wide, narrow = lax.axis_index("wide"), lax.axis_index("narrow")
    peers_x, peers_y = lax.axis_size("wide"), lax.axis_size("narrow")
    grid_y = cols_y * peers_y
    sides = jnp.stack(
        [
            wide % 2,
            narrow % 2,
            (wide > 0).astype(jnp.int32),
            (wide < peers_x - 1).astype(jnp.int32),
            (narrow > 0).astype(jnp.int32),
            (narrow < peers_y - 1).astype(jnp.int32),
            wide * cols_x * grid_y + narrow * cols_y,
            jnp.full((), grid_y, jnp.int32),
        ]
    ).astype(jnp.int32)
    blocks = inverse_blocks.reshape((number,) + inverse_blocks.shape[2:])
    state, rows = (number, count, layers), (number, layers)
    apply_flops = 4 * count * number * layers * inverse_blocks.shape[-1]
    gram_flops = 8 * count * count * number * layers

    numbers = (cols_y, cols_y, cols_x, cols_x)
    first_edges = [(n * (count + 1), layers) for n in numbers]
    later_edges = [(n * count, layers) for n in numbers]
    rhs, v, coef, diag_term, blocks, *edges = call(
        functools.partial(start_kernel, cols),
        [state, state, rows, rows, jax.ShapeDtypeStruct(blocks.shape, blocks.dtype)]
        + first_edges,
        [SMEM] + [HBM] * 6,
        sides,
        *(
            pltpu.with_memory_space_constraint(a, pltpu.HBM)
            for a in (
                well_columns,
                column_active,
                sources,
                perm_root.reshape(rows),
                storage_term.reshape(rows),
                blocks,
            )
        ),
        flops=apply_flops,
        scratch=[
            pltpu.SMEM(well_columns.shape, jnp.int32),
            pltpu.SMEM(column_active.shape, jnp.int32),
            pltpu.VMEM(sources.shape, jnp.float32),
            pltpu.VMEM(rows, jnp.float32),
            pltpu.VMEM(rows, jnp.float32),
            pltpu.SemaphoreType.DMA((4,)),
            pltpu.SemaphoreType.DMA((cols_x,)),
            pltpu.SemaphoreType.DMA((cols_x,)),
        ],
    )
    vs, ws, grams = [v], [], []
    got_coefs = got = exchange(edges)
    for j in range(1, ITERS):
        w, v, *edges = call(
            functools.partial(step_kernel, cols),
            [state, state] + later_edges,
            [SMEM] + [VMEM] * 12,
            sides, vs[-1], coef, diag_term, blocks, *got, *got_coefs,
            flops=apply_flops,
        )
        vs.append(v)
        ws.append(w)
        got = exchange(edges)
        arrays = [vs[-2], v, w] + ([rhs] if j == 1 else [])
        pairs = ([(0, 3)] if j == 1 else []) + [(0, 2), (1, 2)]
        grams += call(
            functools.partial(gram_kernel, pairs),
            [(count, len(pairs) * count)],
            [VMEM] * len(arrays),
            *arrays,
            flops=len(pairs) * gram_flops,
        )
    w, joint = call(
        functools.partial(last_kernel, cols),
        [state, (peers_x * peers_y, count // 2, 128)],
        [SMEM] + [VMEM] * 13,
        sides, vs[-1], coef, diag_term, *grams, *got, *got_coefs,
        flops=gram_flops,
    )
    ws.append(w)
    joint = lax.all_to_all(joint, ("narrow", "wide"), 0, 0)
    outs = call(
        functools.partial(finish_kernel, ITERS),
        [sources.shape] * 2,
        [VMEM] * (2 + 2 * ITERS),
        joint, rhs, *vs, *ws,
        flops=24 * ITERS * count * count * number * layers,
        out_specs=[HBM, HBM],
        scratch=[
            pltpu.VMEM(sources.shape, jnp.float32),
            pltpu.VMEM(sources.shape, jnp.float32),
            pltpu.SemaphoreType.DMA((2 * cols_x,)),
        ],
    )
    return tuple(outs)


def solution(mesh):
    in_specs = (
        P(None, "wide", "narrow", None),
        P(),
        P("wide", "narrow"),
        P("wide", "narrow", None),
        P("wide", "narrow", None),
        P("wide", "narrow", None, None, None),
    )
    out_specs = (P(None, "wide", "narrow", None), P(None, "wide", "narrow", None))
    return jax.shard_map(
        on_device, mesh=mesh, in_specs=in_specs, out_specs=out_specs, check_vma=False
    )
```

```python
import functools

import jax
import jax.numpy as jnp
import numpy as np
from jax import lax
from jax.experimental import pallas as pl
from jax.experimental.pallas import tpu as pltpu
from jax.sharding import PartitionSpec as P

ITERS = 3
WELL_RATE = 4.0
VMEM_BYTES = 24 * 1024 * 1024
VMEM = pl.BlockSpec(memory_space=pltpu.VMEM)
SMEM = pl.BlockSpec(memory_space=pltpu.SMEM)
HBM = pl.BlockSpec(memory_space=pltpu.HBM)
SCALE = 64.0
AHEAD = 6


def call(kernel, out_shape, in_specs, *args, flops=0, out_specs=None, scratch=()):
    shapes = [
        s if isinstance(s, jax.ShapeDtypeStruct) else jax.ShapeDtypeStruct(s, jnp.float32)
        for s in out_shape
    ]
    size = sum(a.size * a.dtype.itemsize for a in args) + sum(s.size * 4 for s in shapes)
    return pl.pallas_call(
        kernel,
        out_shape=shapes,
        in_specs=in_specs,
        out_specs=out_specs or [VMEM] * len(shapes),
        scratch_shapes=list(scratch),
        compiler_params=pltpu.CompilerParams(vmem_limit_bytes=VMEM_BYTES),
        cost_estimate=pl.CostEstimate(flops=flops, bytes_accessed=size, transcendentals=0),
    )(*args)


def split(value):
    high = value.astype(jnp.bfloat16)
    return high, (value - high.astype(jnp.float32)).astype(jnp.bfloat16)


def apply_blocks(value, blocks_ref, col):
    count, layers = value.shape
    parts = []
    size = blocks_ref.shape[-1]
    for b in range(layers // size):
        both = jnp.concatenate(split(value[:, b * size : (b + 1) * size]), axis=0)
        out = jnp.dot(both, blocks_ref[col, b], preferred_element_type=jnp.float32)
        parts.append(out[:count] + out[count:])
    return jnp.concatenate(parts, axis=1)


def write_edges(sides_ref, cols, v_ref, coef_ref, edges):
    cols_x, cols_y = cols
    count = v_ref.shape[1]
    for slot, ref in enumerate(edges):
        odd = sides_ref[slot // 2]
        at_low = odd if slot % 2 == 0 else 1 - odd
        number = cols_y if slot < 2 else cols_x
        for i in range(number):
            if slot < 2:
                col = jnp.where(at_low == 1, 0, (cols_x - 1) * cols_y) + i
            else:
                col = i * cols_y + jnp.where(at_low == 1, 0, cols_y - 1)
            ref[i * count : (i + 1) * count, :] = v_ref[col]
            if coef_ref is not None:
                ref[number * count + i : number * count + i + 1, :] = coef_ref[pl.ds(col, 1), :]


def start_kernel(
    cols, sides_ref, wells_hbm, active_hbm, sources_hbm, perm_hbm, storage_hbm, blocks_hbm,
    r_ref, v_ref, coef_ref, diag_ref, blocks_ref, *refs,
):
    edges = refs[:4]
    wells_ref, active_ref, sources_ref, perm_ref, storage_ref, small_sem, big_sem, block_sem = refs[4:]
    cols_x, cols_y = cols
    _, count, layers = r_ref.shape
    small = [
        pltpu.make_async_copy(source, target, small_sem.at[i])
        for i, (source, target) in enumerate(
            (
                (wells_hbm, wells_ref),
                (active_hbm, active_ref),
                (perm_hbm, perm_ref),
                (storage_hbm, storage_ref),
            )
        )
    ]
    sources = [
        pltpu.make_async_copy(sources_hbm.at[:, x], sources_ref.at[:, x], big_sem.at[x])
        for x in range(cols_x)
    ]
    blocks = [
        pltpu.make_async_copy(
            blocks_hbm.at[pl.ds(x * cols_y, cols_y)],
            blocks_ref.at[pl.ds(x * cols_y, cols_y)],
            block_sem.at[x],
        )
        for x in range(cols_x)
    ]
    for copy in small:
        copy.start()
    for pair in zip(sources, blocks):
        for copy in pair:
            copy.start()
    for copy in small:
        copy.wait()
    row = lax.broadcasted_iota(jnp.int32, (count, layers), 0)
    wells = jnp.zeros((count, layers), jnp.int32)
    for k in range(count):
        wells = jnp.where(row == k, wells_ref[k], wells)
    for x in range(cols_x):
        for y in range(cols_y):
            col = x * cols_y + y
            active = active_ref[x, y].astype(jnp.float32)
            coef_ref[col : col + 1, :] = active * perm_ref[col : col + 1, :]
            diag_ref[col : col + 1, :] = active * storage_ref[col : col + 1, :] + (1.0 - active)
    for x in range(cols_x):
        sources[x].wait()
        across = jnp.transpose(sources_ref[:, x], (1, 0, 2))
        blocks[x].wait()
        for y in range(cols_y):
            col = x * cols_y + y
            column_id = sides_ref[6] + x * sides_ref[7] + y
            r = across[y] + jnp.where(wells == column_id, WELL_RATE, 0.0)
            r_ref[col] = r
            v_ref[col] = apply_blocks(r, blocks_ref, col)
    write_edges(sides_ref, cols, v_ref, coef_ref, edges)


def neighbours(sides_ref, cols, count, got, got_coefs):
    cols_x, cols_y = cols

    def beyond(v_ref, coef_ref, x, y, step_x, step_y):
        nx, ny = x + step_x, y + step_y
        if 0 <= nx < cols_x and 0 <= ny < cols_y:
            col = nx * cols_y + ny
            return v_ref[col], coef_ref[col : col + 1, :]
        if step_x:
            axis, i, number, low = 0, y, cols_y, step_x < 0
        else:
            axis, i, number, low = 1, x, cols_x, step_y < 0
        odd = sides_ref[axis] == 1
        inside = sides_ref[2 + 2 * axis + (0 if low else 1)].astype(jnp.float32)
        first, second = (
            ref[i * count : (i + 1) * count, :] for ref in got[2 * axis : 2 * axis + 2]
        )
        row = number * count + i
        c_first, c_second = (ref[row : row + 1, :] for ref in got_coefs[2 * axis : 2 * axis + 2])
        if low:
            value, coef = jnp.where(odd, first, second), jnp.where(odd, c_first, c_second)
        else:
            value, coef = jnp.where(odd, second, first), jnp.where(odd, c_second, c_first)
        return value, coef * inside

    return beyond


def operate(beyond, cols, v_ref, coef_ref, diag_ref, x, y):
    col = x * cols[1] + y
    center = v_ref[col]
    layers = center.shape[-1]
    coef = coef_ref[col : col + 1, :]
    lane = lax.broadcasted_iota(jnp.int32, (1, layers), 1)
    total = jnp.zeros_like(center)
    for step_x, step_y in ((1, 0), (-1, 0), (0, 1), (0, -1)):
        other, other_coef = beyond(v_ref, coef_ref, x, y, step_x, step_y)
        total = total + other_coef * (center - other)
    upper_coef = jnp.where(lane == layers - 1, 0.0, pltpu.roll(coef, layers - 1, 1))
    lower_coef = jnp.where(lane == 0, 0.0, pltpu.roll(coef, 1, 1))
    total = total + upper_coef * (center - pltpu.roll(center, layers - 1, 1))
    total = total + lower_coef * (center - pltpu.roll(center, 1, 1))
    return (diag_ref[col : col + 1, :] * center + coef * total) * (1.0 / SCALE)


def step_kernel(cols, sides_ref, v_ref, coef_ref, diag_ref, blocks_ref, *refs):
    got, got_coefs, (w_ref, next_ref), edges = refs[:4], refs[4:8], refs[8:10], refs[10:14]
    count = v_ref.shape[1]
    beyond = neighbours(sides_ref, cols, count, got, got_coefs)
    for x in range(cols[0]):
        for y in range(cols[1]):
            col = x * cols[1] + y
            w = operate(beyond, cols, v_ref, coef_ref, diag_ref, x, y)
            w_ref[col] = w
            next_ref[col] = apply_blocks(w, blocks_ref, col)
    write_edges(sides_ref, cols, next_ref, None, edges)


def split_gram(left, right):
    return lax.dot_general(
        jnp.concatenate(split(left), axis=0),
        jnp.concatenate(split(right), axis=0),
        (((1,), (1,)), ((), ())),
        preferred_element_type=jnp.float32,
    )


def fold(total):
    count = total.shape[0] // 2
    total = total[:count] + total[count:]
    total = total[:, :count] + total[:, count:]
    return 0.5 * (total + total.T)


def gram_kernel(pairs, *refs):
    arrays, out_ref = refs[:-1], refs[-1]
    count = arrays[0].shape[1]
    for slot, (left, right) in enumerate(pairs):
        total = jnp.zeros((2 * count, 2 * count), jnp.float32)
        for col in range(arrays[0].shape[0]):
            total = total + split_gram(arrays[left][col], arrays[right][col])
        out_ref[:, slot * count : (slot + 1) * count] = fold(total)


def pack(squares):
    count = squares[0].shape[0]
    row = lax.broadcasted_iota(jnp.int32, (count, count), 0)
    lane = lax.broadcasted_iota(jnp.int32, (count, count), 1)
    halves = [
        jnp.where(row >= lane, first, second)
        for first, second in zip(squares[0::2], squares[1::2])
    ]
    diagonals = [
        jnp.sum(jnp.where(row == lane, second, 0.0), axis=1, keepdims=True)
        for second in squares[1::2]
    ]
    used = len(halves) * (count + 1)
    packed = jnp.concatenate(
        halves + diagonals + [jnp.zeros((count, 64 - used), jnp.float32)], axis=1
    )
    return jnp.concatenate([packed[: count // 2], packed[count // 2 :]], axis=1)


def unpack(packed, number):
    count = 2 * packed.shape[0]
    packed = jnp.concatenate([packed[:, :64], packed[:, 64:]], axis=0)
    row = lax.broadcasted_iota(jnp.int32, (count, count), 0)
    lane = lax.broadcasted_iota(jnp.int32, (count, count), 1)
    squares = []
    for i in range(number // 2):
        half = packed[:, i * count : (i + 1) * count]
        place = number // 2 * count + i
        turned = half.T
        squares.append(jnp.where(row >= lane, half, turned))
        second = jnp.where(row <= lane, half, turned)
        squares.append(jnp.where(row == lane, packed[:, place : place + 1], second))
    return squares


def last_kernel(cols, sides_ref, v_ref, coef_ref, diag_ref, early_ref, late_ref, *refs):
    got, got_coefs, (w_ref, out_ref) = refs[:4], refs[4:8], refs[8:10]
    count = v_ref.shape[1]
    beyond = neighbours(sides_ref, cols, count, got, got_coefs)
    total = jnp.zeros((2 * count, 2 * count), jnp.float32)
    for x in range(cols[0]):
        for y in range(cols[1]):
            col = x * cols[1] + y
            w = operate(beyond, cols, v_ref, coef_ref, diag_ref, x, y)
            w_ref[col] = w
            total = total + split_gram(v_ref[col], w)
    squares = [
        ref[:, i * count : (i + 1) * count]
        for ref in (early_ref, late_ref)
        for i in range(ref.shape[1] // count)
    ]
    packed = pack(squares + [fold(total)])
    for peer in range(out_ref.shape[0]):
        out_ref[peer] = packed


def solve_spd(matrix, target):
    size, width = matrix.shape[0], matrix.shape[1] + target.shape[1]
    lanes = 128
    work = jnp.concatenate(
        [matrix, target, jnp.zeros((size, lanes - width), jnp.float32)], axis=1
    )
    row = lax.broadcasted_iota(jnp.int32, (size, lanes), 0)

    def spread(p):
        return jnp.broadcast_to(work[:, p : p + 1], (size, lanes))

    ahead = {p: spread(p) for p in range(AHEAD)}
    inverses = jnp.zeros((size, lanes), jnp.float32)
    for p in range(size):
        column = ahead.pop(p)
        if p + AHEAD < size:
            ahead[p + AHEAD] = spread(p + AHEAD)
        inverse = 1.0 / column[p : p + 1, :]
        inverses = jnp.where(row == p, inverse, inverses)
        factor = jnp.where(row == p, 0.0, column)

        def eliminate(value):
            return value - factor * jnp.broadcast_to(value[p : p + 1, :] * inverse, value.shape)

        ahead = {q: eliminate(value) for q, value in ahead.items()}
        work = eliminate(work)
    return work[:, size:width] * inverses[:, size:width]


def finish_kernel(blocks, sums_ref, r_ref, *refs):
    v_refs, w_refs, (x_hbm, out_hbm) = refs[:blocks], refs[blocks : 2 * blocks], refs[2 * blocks : 2 * blocks + 2]
    x_ref, out_ref, sem = refs[2 * blocks + 2 :]
    cols_x, cols_y = x_ref.shape[1:3]
    joint = sums_ref[0]
    for peer in range(1, sums_ref.shape[0]):
        joint = joint + sums_ref[peer]
    moments = unpack(joint, 2 * blocks)
    matrix = jnp.concatenate(
        [
            jnp.concatenate([moments[1 + i + j] for j in range(blocks)], axis=1)
            for i in range(blocks)
        ],
        axis=0,
    )
    target = jnp.concatenate(moments[:blocks], axis=0)
    coefs = solve_spd(matrix, target).T
    high = coefs.astype(jnp.bfloat16)
    middle, low = split(coefs - high.astype(jnp.float32))
    left = jnp.concatenate([high, high, middle, middle, low], axis=1)

    def combine(values, col):
        highs, lows = zip(*(split(ref[col]) for ref in values))
        right = jnp.concatenate(highs + lows + highs + lows + highs, axis=0)
        return jnp.dot(left, right, preferred_element_type=jnp.float32)

    copies = []
    for x in range(cols_x):
        columns = range(x * cols_y, (x + 1) * cols_y)
        out_ref[:, x] = jnp.transpose(
            jnp.stack([r_ref[col] - combine(w_refs, col) for col in columns]), (1, 0, 2)
        )
        copies.append(
            pltpu.make_async_copy(out_ref.at[:, x], out_hbm.at[:, x], sem.at[2 * x])
        )
        copies[-1].start()
        x_ref[:, x] = jnp.transpose(
            jnp.stack([combine(v_refs, col) * (1.0 / SCALE) for col in columns]), (1, 0, 2)
        )
        copies.append(
            pltpu.make_async_copy(x_ref.at[:, x], x_hbm.at[:, x], sem.at[2 * x + 1])
        )
        copies[-1].start()
    for copy in copies:
        copy.wait()


def pairing(sizes, axis, phase):
    transfers = []
    for place in np.ndindex(*sizes):
        partner = list(place)
        partner[axis] += 1 if place[axis] % 2 == phase else -1
        if not 0 <= partner[axis] < sizes[axis]:
            partner = list(place)
            partner[1 - axis] ^= 1
            if partner[1 - axis] >= sizes[1 - axis]:
                continue
        transfers.append(tuple(int(np.ravel_multi_index(p, sizes)) for p in (place, partner)))
    return transfers


def exchange(edges):
    axes = ("narrow", "wide")
    sizes = tuple(lax.axis_size(axis) for axis in axes)
    out = [None] * len(edges)
    for slot in (1, 3, 2, 0):
        out[slot] = lax.ppermute(edges[slot], axes, pairing(sizes, 1 - slot // 2, slot % 2))
    return out


def on_device(sources, well_columns, column_active, perm_root, storage_term, inverse_blocks):
    count, cols_x, cols_y, layers = sources.shape
    cols = (cols_x, cols_y)
    number = cols_x * cols_y
    wide, narrow = lax.axis_index("wide"), lax.axis_index("narrow")
    peers_x, peers_y = lax.axis_size("wide"), lax.axis_size("narrow")
    grid_y = cols_y * peers_y
    sides = jnp.stack(
        [
            wide % 2,
            narrow % 2,
            (wide > 0).astype(jnp.int32),
            (wide < peers_x - 1).astype(jnp.int32),
            (narrow > 0).astype(jnp.int32),
            (narrow < peers_y - 1).astype(jnp.int32),
            wide * cols_x * grid_y + narrow * cols_y,
            jnp.full((), grid_y, jnp.int32),
        ]
    ).astype(jnp.int32)
    blocks = inverse_blocks.reshape((number,) + inverse_blocks.shape[2:])
    state, rows = (number, count, layers), (number, layers)
    apply_flops = 4 * count * number * layers * inverse_blocks.shape[-1]
    gram_flops = 8 * count * count * number * layers

    numbers = (cols_y, cols_y, cols_x, cols_x)
    first_edges = [(n * (count + 1), layers) for n in numbers]
    later_edges = [(n * count, layers) for n in numbers]
    rhs, v, coef, diag_term, blocks, *edges = call(
        functools.partial(start_kernel, cols),
        [state, state, rows, rows, jax.ShapeDtypeStruct(blocks.shape, blocks.dtype)]
        + first_edges,
        [SMEM] + [HBM] * 6,
        sides,
        *(
            pltpu.with_memory_space_constraint(a, pltpu.HBM)
            for a in (
                well_columns,
                column_active,
                sources,
                perm_root.reshape(rows),
                storage_term.reshape(rows),
                blocks,
            )
        ),
        flops=apply_flops,
        scratch=[
            pltpu.SMEM(well_columns.shape, jnp.int32),
            pltpu.SMEM(column_active.shape, jnp.int32),
            pltpu.VMEM(sources.shape, jnp.float32),
            pltpu.VMEM(rows, jnp.float32),
            pltpu.VMEM(rows, jnp.float32),
            pltpu.SemaphoreType.DMA((4,)),
            pltpu.SemaphoreType.DMA((cols_x,)),
            pltpu.SemaphoreType.DMA((cols_x,)),
        ],
    )
    vs, ws, grams = [v], [], []
    got_coefs = got = exchange(edges)
    for j in range(1, ITERS):
        w, v, *edges = call(
            functools.partial(step_kernel, cols),
            [state, state] + later_edges,
            [SMEM] + [VMEM] * 12,
            sides, vs[-1], coef, diag_term, blocks, *got, *got_coefs,
            flops=apply_flops,
        )
        vs.append(v)
        ws.append(w)
        got = exchange(edges)
        arrays = [vs[-2], v, w] + ([rhs] if j == 1 else [])
        pairs = ([(0, 3)] if j == 1 else []) + [(0, 2), (1, 2)]
        grams += call(
            functools.partial(gram_kernel, pairs),
            [(count, len(pairs) * count)],
            [VMEM] * len(arrays),
            *arrays,
            flops=len(pairs) * gram_flops,
        )
    w, joint = call(
        functools.partial(last_kernel, cols),
        [state, (peers_x * peers_y, count // 2, 128)],
        [SMEM] + [VMEM] * 13,
        sides, vs[-1], coef, diag_term, *grams, *got, *got_coefs,
        flops=gram_flops,
    )
    ws.append(w)
    joint = lax.all_to_all(joint, ("narrow", "wide"), 0, 0)
    outs = call(
        functools.partial(finish_kernel, ITERS),
        [sources.shape] * 2,
        [VMEM] * (2 + 2 * ITERS),
        joint, rhs, *vs, *ws,
        flops=24 * ITERS * count * count * number * layers,
        out_specs=[HBM, HBM],
        scratch=[
            pltpu.VMEM(sources.shape, jnp.float32),
            pltpu.VMEM(sources.shape, jnp.float32),
            pltpu.SemaphoreType.DMA((2 * cols_x,)),
        ],
    )
    return tuple(outs)


def solution(mesh):
    in_specs = (
        P(None, "wide", "narrow", None),
        P(),
        P("wide", "narrow"),
        P("wide", "narrow", None),
        P("wide", "narrow", None),
        P("wide", "narrow", None, None, None),
    )
    out_specs = (P(None, "wide", "narrow", None), P(None, "wide", "narrow", None))
    return jax.shard_map(
        on_device, mesh=mesh, in_specs=in_specs, out_specs=out_specs, check_vma=False
    )
```

```python
import functools

import jax
import jax.numpy as jnp
import numpy as np
from jax import lax
from jax.experimental import pallas as pl
from jax.experimental.pallas import tpu as pltpu
from jax.sharding import PartitionSpec as P

ITERS = 3
WELL_RATE = 4.0
VMEM_BYTES = 24 * 1024 * 1024
VMEM = pl.BlockSpec(memory_space=pltpu.VMEM)
HBM = pl.BlockSpec(memory_space=pltpu.HBM)
SCALE = 64.0
AHEAD = 6


def call(kernel, out_shape, in_specs, *args, flops=0, out_specs=None, scratch=()):
    shapes = [
        s if isinstance(s, jax.ShapeDtypeStruct) else jax.ShapeDtypeStruct(s, jnp.float32)
        for s in out_shape
    ]
    size = sum(a.size * a.dtype.itemsize for a in args) + sum(s.size * 4 for s in shapes)
    return pl.pallas_call(
        kernel,
        out_shape=shapes,
        in_specs=in_specs,
        out_specs=out_specs or [VMEM] * len(shapes),
        scratch_shapes=list(scratch),
        compiler_params=pltpu.CompilerParams(vmem_limit_bytes=VMEM_BYTES),
        cost_estimate=pl.CostEstimate(flops=flops, bytes_accessed=size, transcendentals=0),
    )(*args)


def split(value):
    high = value.astype(jnp.bfloat16)
    return high, (value - high.astype(jnp.float32)).astype(jnp.bfloat16)


def apply_blocks(value, blocks_ref, col):
    count, layers = value.shape
    parts = []
    size = blocks_ref.shape[-1]
    for b in range(layers // size):
        both = jnp.concatenate(split(value[:, b * size : (b + 1) * size]), axis=0)
        out = jnp.dot(both, blocks_ref[col, b], preferred_element_type=jnp.float32)
        parts.append(out[:count] + out[count:])
    return jnp.concatenate(parts, axis=1)


AXES = ("narrow", "wide")
ORDER = (3, 1, 0, 2)


def write_edges(cols, v_ref, coef_ref, edges):
    cols_x, cols_y = cols
    count = v_ref.shape[1]
    for slot, ref in zip(ORDER, edges):
        odd = lax.rem(lax.axis_index(AXES[slot // 2]), 2)
        at_low = odd if slot % 2 == 0 else 1 - odd
        number = cols_x if slot < 2 else cols_y
        for i in range(number):
            if slot >= 2:
                col = jnp.where(at_low == 1, 0, (cols_x - 1) * cols_y) + i
            else:
                col = i * cols_y + jnp.where(at_low == 1, 0, cols_y - 1)
            ref[i * count : (i + 1) * count, :] = v_ref[col]
            if coef_ref is not None:
                ref[number * count + i : number * count + i + 1, :] = coef_ref[pl.ds(col, 1), :]


def start_kernel(
    cols, wells_hbm, active_hbm, sources_hbm, perm_hbm, storage_hbm, blocks_hbm,
    r_ref, v_ref, coef_ref, diag_ref, blocks_ref, *refs,
):
    edges = refs[:4]
    wells_ref, active_ref, sources_ref, perm_ref, storage_ref, small_sem, big_sem, block_sem = refs[4:]
    cols_x, cols_y = cols
    _, count, layers = r_ref.shape
    small = [
        pltpu.make_async_copy(source, target, small_sem.at[i])
        for i, (source, target) in enumerate(
            (
                (wells_hbm, wells_ref),
                (active_hbm, active_ref),
                (perm_hbm, perm_ref),
                (storage_hbm, storage_ref),
            )
        )
    ]
    sources = [
        pltpu.make_async_copy(sources_hbm.at[:, x], sources_ref.at[:, x], big_sem.at[x])
        for x in range(cols_x)
    ]
    blocks = [
        pltpu.make_async_copy(
            blocks_hbm.at[pl.ds(x * cols_y, cols_y)],
            blocks_ref.at[pl.ds(x * cols_y, cols_y)],
            block_sem.at[x],
        )
        for x in range(cols_x)
    ]
    for copy in small:
        copy.start()
    for pair in zip(sources, blocks):
        for copy in pair:
            copy.start()
    for copy in small:
        copy.wait()
    row = lax.broadcasted_iota(jnp.int32, (count, layers), 0)
    wells = jnp.zeros((count, layers), jnp.int32)
    for k in range(count):
        wells = jnp.where(row == k, wells_ref[k], wells)
    for x in range(cols_x):
        for y in range(cols_y):
            col = x * cols_y + y
            active = active_ref[x, y].astype(jnp.float32)
            coef_ref[col : col + 1, :] = active * perm_ref[col : col + 1, :]
            diag_ref[col : col + 1, :] = active * storage_ref[col : col + 1, :] + (1.0 - active)
    grid_y = cols_y * lax.axis_size("narrow")
    first_x, first_y = lax.axis_index("wide") * cols_x, lax.axis_index("narrow") * cols_y
    for x in range(cols_x):
        sources[x].wait()
        across = jnp.transpose(sources_ref[:, x], (1, 0, 2))
        blocks[x].wait()
        for y in range(cols_y):
            col = x * cols_y + y
            column_id = (first_x + x) * grid_y + first_y + y
            r = across[y] + jnp.where(wells == column_id, WELL_RATE, 0.0)
            r_ref[col] = r
            v_ref[col] = apply_blocks(r, blocks_ref, col)
    write_edges(cols, v_ref, coef_ref, edges)


def neighbours(cols, count, got, got_coefs):
    cols_x, cols_y = cols

    def beyond(v_ref, coef_ref, x, y, step_x, step_y):
        nx, ny = x + step_x, y + step_y
        if 0 <= nx < cols_x and 0 <= ny < cols_y:
            col = nx * cols_y + ny
            return v_ref[col], coef_ref[col : col + 1, :]
        if step_x:
            axis, i, number, low = 1, y, cols_y, step_x < 0
        else:
            axis, i, number, low = 0, x, cols_x, step_y < 0
        place = lax.axis_index(AXES[axis])
        odd = lax.rem(place, 2) == 1
        end = 0 if low else lax.axis_size(AXES[axis]) - 1
        inside = (place != end).astype(jnp.float32)
        first, second = (
            ref[i * count : (i + 1) * count, :] for ref in got[2 * axis : 2 * axis + 2]
        )
        row = number * count + i
        c_first, c_second = (ref[row : row + 1, :] for ref in got_coefs[2 * axis : 2 * axis + 2])
        if low:
            value, coef = jnp.where(odd, first, second), jnp.where(odd, c_first, c_second)
        else:
            value, coef = jnp.where(odd, second, first), jnp.where(odd, c_second, c_first)
        return value, coef * inside

    return beyond


def operate(beyond, cols, v_ref, coef_ref, diag_ref, x, y):
    col = x * cols[1] + y
    center = v_ref[col]
    layers = center.shape[-1]
    coef = coef_ref[col : col + 1, :]
    lane = lax.broadcasted_iota(jnp.int32, (1, layers), 1)
    total = jnp.zeros_like(center)
    for step_x, step_y in ((1, 0), (-1, 0), (0, 1), (0, -1)):
        other, other_coef = beyond(v_ref, coef_ref, x, y, step_x, step_y)
        total = total + other_coef * (center - other)
    upper_coef = jnp.where(lane == layers - 1, 0.0, pltpu.roll(coef, layers - 1, 1))
    lower_coef = jnp.where(lane == 0, 0.0, pltpu.roll(coef, 1, 1))
    total = total + upper_coef * (center - pltpu.roll(center, layers - 1, 1))
    total = total + lower_coef * (center - pltpu.roll(center, 1, 1))
    return (diag_ref[col : col + 1, :] * center + coef * total) * (1.0 / SCALE)


def step_kernel(cols, v_ref, coef_ref, diag_ref, blocks_ref, *refs):
    got, got_coefs, (w_ref, next_ref), edges = refs[:4], refs[4:8], refs[8:10], refs[10:14]
    count = v_ref.shape[1]
    beyond = neighbours(cols, count, got, got_coefs)
    for x in range(cols[0]):
        for y in range(cols[1]):
            col = x * cols[1] + y
            w = operate(beyond, cols, v_ref, coef_ref, diag_ref, x, y)
            w_ref[col] = w
            next_ref[col] = apply_blocks(w, blocks_ref, col)
    write_edges(cols, next_ref, None, edges)


def split_gram(left, right):
    return lax.dot_general(
        jnp.concatenate(split(left), axis=0),
        jnp.concatenate(split(right), axis=0),
        (((1,), (1,)), ((), ())),
        preferred_element_type=jnp.float32,
    )


def fold(total):
    count = total.shape[0] // 2
    total = total[:count] + total[count:]
    total = total[:, :count] + total[:, count:]
    return 0.5 * (total + total.T)


def gram_kernel(pairs, *refs):
    arrays, out_ref = refs[:-1], refs[-1]
    count = arrays[0].shape[1]
    for slot, (left, right) in enumerate(pairs):
        total = jnp.zeros((2 * count, 2 * count), jnp.float32)
        for col in range(arrays[0].shape[0]):
            total = total + split_gram(arrays[left][col], arrays[right][col])
        out_ref[:, slot * count : (slot + 1) * count] = fold(total)


def pack(squares):
    count = squares[0].shape[0]
    row = lax.broadcasted_iota(jnp.int32, (count, count), 0)
    lane = lax.broadcasted_iota(jnp.int32, (count, count), 1)
    halves = [
        jnp.where(row >= lane, first, second)
        for first, second in zip(squares[0::2], squares[1::2])
    ]
    diagonals = [
        jnp.sum(jnp.where(row == lane, second, 0.0), axis=1, keepdims=True)
        for second in squares[1::2]
    ]
    used = len(halves) * (count + 1)
    packed = jnp.concatenate(
        halves + diagonals + [jnp.zeros((count, 64 - used), jnp.float32)], axis=1
    )
    return jnp.concatenate([packed[: count // 2], packed[count // 2 :]], axis=1)


def unpack(packed, number):
    count = 2 * packed.shape[0]
    packed = jnp.concatenate([packed[:, :64], packed[:, 64:]], axis=0)
    row = lax.broadcasted_iota(jnp.int32, (count, count), 0)
    lane = lax.broadcasted_iota(jnp.int32, (count, count), 1)
    squares = []
    for i in range(number // 2):
        half = packed[:, i * count : (i + 1) * count]
        place = number // 2 * count + i
        turned = half.T
        squares.append(jnp.where(row >= lane, half, turned))
        second = jnp.where(row <= lane, half, turned)
        squares.append(jnp.where(row == lane, packed[:, place : place + 1], second))
    return squares


def last_kernel(cols, v_ref, coef_ref, diag_ref, early_ref, late_ref, *refs):
    got, got_coefs, (w_ref, out_ref) = refs[:4], refs[4:8], refs[8:10]
    count = v_ref.shape[1]
    beyond = neighbours(cols, count, got, got_coefs)
    total = jnp.zeros((2 * count, 2 * count), jnp.float32)
    for x in range(cols[0]):
        for y in range(cols[1]):
            col = x * cols[1] + y
            w = operate(beyond, cols, v_ref, coef_ref, diag_ref, x, y)
            w_ref[col] = w
            total = total + split_gram(v_ref[col], w)
    squares = [
        ref[:, i * count : (i + 1) * count]
        for ref in (early_ref, late_ref)
        for i in range(ref.shape[1] // count)
    ]
    packed = pack(squares + [fold(total)])
    for peer in range(out_ref.shape[0]):
        out_ref[peer] = packed


def solve_spd(matrix, target):
    size, width = matrix.shape[0], matrix.shape[1] + target.shape[1]
    lanes = 128
    work = jnp.concatenate(
        [matrix, target, jnp.zeros((size, lanes - width), jnp.float32)], axis=1
    )
    row = lax.broadcasted_iota(jnp.int32, (size, lanes), 0)

    def spread(p):
        return jnp.broadcast_to(work[:, p : p + 1], (size, lanes))

    ahead = {p: spread(p) for p in range(AHEAD)}
    inverses = jnp.zeros((size, lanes), jnp.float32)
    for p in range(size):
        column = ahead.pop(p)
        if p + AHEAD < size:
            ahead[p + AHEAD] = spread(p + AHEAD)
        inverse = 1.0 / column[p : p + 1, :]
        inverses = jnp.where(row == p, inverse, inverses)
        factor = jnp.where(row == p, 0.0, column)

        def eliminate(value):
            return value - factor * jnp.broadcast_to(value[p : p + 1, :] * inverse, value.shape)

        ahead = {q: eliminate(value) for q, value in ahead.items()}
        work = eliminate(work)
    return work[:, size:width] * inverses[:, size:width]


def finish_kernel(blocks, sums_ref, r_ref, *refs):
    v_refs, w_refs, (x_hbm, out_hbm) = refs[:blocks], refs[blocks : 2 * blocks], refs[2 * blocks : 2 * blocks + 2]
    x_ref, out_ref, sem = refs[2 * blocks + 2 :]
    cols_x, cols_y = x_ref.shape[1:3]
    joint = sums_ref[0]
    for peer in range(1, sums_ref.shape[0]):
        joint = joint + sums_ref[peer]
    moments = unpack(joint, 2 * blocks)
    matrix = jnp.concatenate(
        [
            jnp.concatenate([moments[1 + i + j] for j in range(blocks)], axis=1)
            for i in range(blocks)
        ],
        axis=0,
    )
    target = jnp.concatenate(moments[:blocks], axis=0)
    coefs = solve_spd(matrix, target).T
    high = coefs.astype(jnp.bfloat16)
    middle, low = split(coefs - high.astype(jnp.float32))
    left = jnp.concatenate([high, high, middle, middle, low], axis=1)

    def combine(values, col):
        highs, lows = zip(*(split(ref[col]) for ref in values))
        right = jnp.concatenate(highs + lows + highs + lows + highs, axis=0)
        return jnp.dot(left, right, preferred_element_type=jnp.float32)

    copies = []
    for x in range(cols_x):
        columns = range(x * cols_y, (x + 1) * cols_y)
        out_ref[:, x] = jnp.transpose(
            jnp.stack([r_ref[col] - combine(w_refs, col) for col in columns]), (1, 0, 2)
        )
        copies.append(
            pltpu.make_async_copy(out_ref.at[:, x], out_hbm.at[:, x], sem.at[2 * x])
        )
        copies[-1].start()
        x_ref[:, x] = jnp.transpose(
            jnp.stack([combine(v_refs, col) * (1.0 / SCALE) for col in columns]), (1, 0, 2)
        )
        copies.append(
            pltpu.make_async_copy(x_ref.at[:, x], x_hbm.at[:, x], sem.at[2 * x + 1])
        )
        copies[-1].start()
    for copy in copies:
        copy.wait()


def pairing(sizes, axis, phase):
    transfers = []
    for place in np.ndindex(*sizes):
        partner = list(place)
        partner[axis] += 1 if place[axis] % 2 == phase else -1
        if not 0 <= partner[axis] < sizes[axis]:
            partner = list(place)
            partner[1 - axis] ^= 1
            if partner[1 - axis] >= sizes[1 - axis]:
                continue
        transfers.append(tuple(int(np.ravel_multi_index(p, sizes)) for p in (place, partner)))
    return transfers


def exchange(edges):
    sizes = tuple(lax.axis_size(axis) for axis in AXES)
    out = [None] * len(edges)
    for slot, edge in zip(ORDER, edges):
        out[slot] = lax.ppermute(edge, AXES, pairing(sizes, slot // 2, slot % 2))
    return out


def on_device(sources, well_columns, column_active, perm_root, storage_term, inverse_blocks):
    count, cols_x, cols_y, layers = sources.shape
    cols = (cols_x, cols_y)
    number = cols_x * cols_y
    devices = lax.axis_size("wide") * lax.axis_size("narrow")
    blocks = inverse_blocks.reshape((number,) + inverse_blocks.shape[2:])
    state, rows = (number, count, layers), (number, layers)
    apply_flops = 4 * count * number * layers * inverse_blocks.shape[-1]
    gram_flops = 8 * count * count * number * layers

    numbers = [cols[slot // 2] for slot in ORDER]
    first_edges = [(n * (count + 1), layers) for n in numbers]
    later_edges = [(n * count, layers) for n in numbers]
    rhs, v, coef, diag_term, blocks, *edges = call(
        functools.partial(start_kernel, cols),
        [state, state, rows, rows, jax.ShapeDtypeStruct(blocks.shape, blocks.dtype)]
        + first_edges,
        [HBM] * 6,
        *(
            pltpu.with_memory_space_constraint(a, pltpu.HBM)
            for a in (
                well_columns,
                column_active,
                sources,
                perm_root.reshape(rows),
                storage_term.reshape(rows),
                blocks,
            )
        ),
        flops=apply_flops,
        scratch=[
            pltpu.SMEM(well_columns.shape, jnp.int32),
            pltpu.SMEM(column_active.shape, jnp.int32),
            pltpu.VMEM(sources.shape, jnp.float32),
            pltpu.VMEM(rows, jnp.float32),
            pltpu.VMEM(rows, jnp.float32),
            pltpu.SemaphoreType.DMA((4,)),
            pltpu.SemaphoreType.DMA((cols_x,)),
            pltpu.SemaphoreType.DMA((cols_x,)),
        ],
    )
    vs, ws, grams = [v], [], []
    got_coefs = got = exchange(edges)
    for j in range(1, ITERS):
        w, v, *edges = call(
            functools.partial(step_kernel, cols),
            [state, state] + later_edges,
            [VMEM] * 12,
            vs[-1], coef, diag_term, blocks, *got, *got_coefs,
            flops=apply_flops,
        )
        vs.append(v)
        ws.append(w)
        got = exchange(edges)
        arrays = [vs[-2], v, w] + ([rhs] if j == 1 else [])
        pairs = ([(0, 3)] if j == 1 else []) + [(0, 2), (1, 2)]
        grams += call(
            functools.partial(gram_kernel, pairs),
            [(count, len(pairs) * count)],
            [VMEM] * len(arrays),
            *arrays,
            flops=len(pairs) * gram_flops,
        )
    w, joint = call(
        functools.partial(last_kernel, cols),
        [state, (devices, count // 2, 128)],
        [VMEM] * 13,
        vs[-1], coef, diag_term, *grams, *got, *got_coefs,
        flops=gram_flops,
    )
    ws.append(w)
    joint = lax.all_to_all(joint, ("narrow", "wide"), 0, 0)
    outs = call(
        functools.partial(finish_kernel, ITERS),
        [sources.shape] * 2,
        [VMEM] * (2 + 2 * ITERS),
        joint, rhs, *vs, *ws,
        flops=24 * ITERS * count * count * number * layers,
        out_specs=[HBM, HBM],
        scratch=[
            pltpu.VMEM(sources.shape, jnp.float32),
            pltpu.VMEM(sources.shape, jnp.float32),
            pltpu.SemaphoreType.DMA((2 * cols_x,)),
        ],
    )
    return tuple(outs)


def solution(mesh):
    in_specs = (
        P(None, "wide", "narrow", None),
        P(),
        P("wide", "narrow"),
        P("wide", "narrow", None),
        P("wide", "narrow", None),
        P("wide", "narrow", None, None, None),
    )
    out_specs = (P(None, "wide", "narrow", None), P(None, "wide", "narrow", None))
    return jax.shard_map(
        on_device, mesh=mesh, in_specs=in_specs, out_specs=out_specs, check_vma=False
    )
```

```python
import functools

import jax
import jax.numpy as jnp
import numpy as np
from jax import lax
from jax.experimental import pallas as pl
from jax.experimental.pallas import tpu as pltpu
from jax.sharding import PartitionSpec as P

ITERS = 3
WELL_RATE = 4.0
VMEM_BYTES = 24 * 1024 * 1024
VMEM = pl.BlockSpec(memory_space=pltpu.VMEM)
HBM = pl.BlockSpec(memory_space=pltpu.HBM)
SCALE = 64.0
AHEAD = 6


def call(kernel, out_shape, in_specs, *args, flops=0, out_specs=None, scratch=(), aliases=None):
    shapes = [
        s if isinstance(s, jax.ShapeDtypeStruct) else jax.ShapeDtypeStruct(s, jnp.float32)
        for s in out_shape
    ]
    size = sum(a.size * a.dtype.itemsize for a in args) + sum(s.size * 4 for s in shapes)
    out = pl.pallas_call(
        kernel,
        out_shape=shapes,
        in_specs=in_specs,
        out_specs=out_specs or [VMEM] * len(shapes),
        scratch_shapes=list(scratch),
        input_output_aliases=aliases or {},
        compiler_params=pltpu.CompilerParams(vmem_limit_bytes=VMEM_BYTES),
        cost_estimate=pl.CostEstimate(flops=flops, bytes_accessed=size, transcendentals=0),
    )(*args)
    return list(out)


def split(value):
    high = value.astype(jnp.bfloat16)
    return high, (value - high.astype(jnp.float32)).astype(jnp.bfloat16)


def apply_blocks(value, blocks_ref, col):
    count, layers = value.shape
    size = blocks_ref.shape[-1]
    number = layers // size
    terms = split(value)
    left = jnp.concatenate(
        [term[:, b * size : (b + 1) * size] for b in range(number) for term in terms], axis=0
    )
    right = jnp.concatenate([blocks_ref[col, b] for b in range(number)], axis=1)
    out = jnp.dot(left, right, preferred_element_type=jnp.float32)
    parts = []
    for b in range(number):
        piece = out[2 * b * count : 2 * (b + 1) * count, b * size : (b + 1) * size]
        parts.append(piece[:count] + piece[count:])
    return jnp.concatenate(parts, axis=1)


AXES = ("narrow", "wide")


def oriented(row, cols_x):
    odd = lax.rem(lax.axis_index("wide"), 2)
    return row + odd * (cols_x - 1 - 2 * row)


def partnered(slot):
    axis = AXES[slot // 2]
    place = lax.axis_index(axis)
    odd = lax.rem(place + slot, 2)
    partner = place + 1 - 2 * odd
    inside = jnp.logical_and(partner >= 0, partner < lax.axis_size(axis))
    return inside.astype(jnp.float32)


def write_edges(v_refs, coef_ref, edges):
    count = v_refs[0].shape[1]
    cols_y = v_refs[0].shape[0]
    odd = lax.rem(lax.axis_index("narrow"), 2)
    for ref, at_low in zip(edges, (odd, 1 - odd)):
        y = (1 - at_low) * (cols_y - 1)
        for row, v_ref in enumerate(v_refs):
            ref[row * count : (row + 1) * count, :] = v_ref[y]
            if coef_ref is not None:
                place = len(v_refs) * count + row
                ref[place : place + 1, :] = coef_ref[pl.ds(row * cols_y + y, 1), :]


def write_side(row, v_ref, coef_ref, edge):
    cols_y, count, _ = v_ref.shape
    for y in range(cols_y):
        edge[y * count : (y + 1) * count, :] = v_ref[y]
    if coef_ref is not None:
        edge[cols_y * count : cols_y * (count + 1), :] = coef_ref[
            row * cols_y : (row + 1) * cols_y, :
        ]


def start_kernel(
    wells_hbm, active_hbm, sources_hbm, perm_hbm, storage_hbm, blocks_hbm, *refs
):
    cols_x, cols_y = active_hbm.shape
    r_refs, v_refs, refs = refs[:cols_x], refs[cols_x : 2 * cols_x], refs[2 * cols_x :]
    coef_ref, diag_ref, blocks_ref, edge_0, edge_1, edge_2, edge_3 = refs[:7]
    wells_ref, active_ref, sources_ref, perm_ref, storage_ref, small_sem, big_sem, block_sem = refs[7:]
    _, count, layers = r_refs[0].shape
    small = [
        pltpu.make_async_copy(source, target, small_sem.at[i])
        for i, (source, target) in enumerate(
            (
                (wells_hbm, wells_ref),
                (active_hbm, active_ref),
                (perm_hbm, perm_ref),
                (storage_hbm, storage_ref),
            )
        )
    ]
    sources, blocks = [], []
    for row in range(cols_x):
        x = oriented(row, cols_x)
        sources.append(
            pltpu.make_async_copy(sources_hbm.at[:, x], sources_ref.at[row], big_sem.at[row])
        )
        blocks.append(
            pltpu.make_async_copy(
                blocks_hbm.at[pl.ds(x * cols_y, cols_y)],
                blocks_ref.at[pl.ds(row * cols_y, cols_y)],
                block_sem.at[row],
            )
        )
    for copy in small:
        copy.start()
    for pair in zip(sources, blocks):
        for copy in pair:
            copy.start()
    for copy in small:
        copy.wait()
    place = lax.broadcasted_iota(jnp.int32, (count, layers), 0)
    wells = jnp.zeros((count, layers), jnp.int32)
    for k in range(count):
        wells = jnp.where(place == k, wells_ref[k], wells)
    grid_y = cols_y * lax.axis_size("narrow")
    first_x, first_y = lax.axis_index("wide") * cols_x, lax.axis_index("narrow") * cols_y
    for row in range(cols_x):
        x = oriented(row, cols_x)
        for y in range(cols_y):
            col = row * cols_y + y
            active = active_ref[x, y].astype(jnp.float32)
            perm, storage = perm_ref[x, y : y + 1, :], storage_ref[x, y : y + 1, :]
            coef_ref[col : col + 1, :] = active * perm
            diag_ref[col : col + 1, :] = active * storage + (1.0 - active)
    for row in range(cols_x):
        sources[row].wait()
        across = jnp.transpose(sources_ref[row], (1, 0, 2))
        blocks[row].wait()
        for y in range(cols_y):
            column_id = (first_x + oriented(row, cols_x)) * grid_y + first_y + y
            r = across[y] + jnp.where(wells == column_id, WELL_RATE, 0.0)
            r_refs[row][y] = r
            v_refs[row][y] = apply_blocks(r, blocks_ref, row * cols_y + y)
    write_side(0, v_refs[0], coef_ref, edge_3)
    write_side(cols_x - 1, v_refs[-1], coef_ref, edge_2)
    write_edges(v_refs, coef_ref, (edge_0, edge_1))


def received(got, got_coefs, slot, i, number, count):
    place = number * count + i
    which = slot % 2
    value = got[which][i * count : (i + 1) * count, :]
    return value, got_coefs[which][place : place + 1, :] * partnered(slot)


def operate(v_refs, coef_ref, diag_ref, got, got_coefs, row, y):
    cols_x = len(v_refs)
    cols_y, count, layers = v_refs[row].shape
    col = row * cols_y + y
    center = v_refs[row][y]
    coef = coef_ref[col : col + 1, :]
    lane = lax.broadcasted_iota(jnp.int32, (1, layers), 1)
    upper_coef = jnp.where(lane == layers - 1, 0.0, pltpu.roll(coef, layers - 1, 1))
    lower_coef = jnp.where(lane == 0, 0.0, pltpu.roll(coef, 1, 1))
    total = upper_coef * (center - pltpu.roll(center, layers - 1, 1))
    total = total + lower_coef * (center - pltpu.roll(center, 1, 1))
    for step_row, step_y in ((1, 0), (-1, 0), (0, 1), (0, -1)):
        other, ny = row + step_row, y + step_y
        if not 0 <= ny < cols_y:
            continue
        if 0 <= other < cols_x:
            place = other * cols_y + ny
            value, other_coef = v_refs[other][ny], coef_ref[place : place + 1, :]
        else:
            slot = 3 if step_row < 0 else 2
            value, other_coef = received(got, got_coefs, slot, y, cols_y, count)
        total = total + other_coef * (center - value)
    return diag_ref[col : col + 1, :] * center + coef * total


def complete(part, v_refs, coef_ref, got, got_coefs, row, y):
    cols_x = len(v_refs)
    cols_y, count, _ = v_refs[row].shape
    col = row * cols_y + y
    odd = lax.rem(lax.axis_index("narrow"), 2) == 1
    first, c_first = received(got, got_coefs, 0, row, cols_x, count)
    second, c_second = received(got, got_coefs, 1, row, cols_x, count)
    for at_end, low in ((y == 0, True), (y == cols_y - 1, False)):
        if at_end:
            value = jnp.where(odd == low, first, second)
            face = coef_ref[col : col + 1, :] * jnp.where(odd == low, c_first, c_second)
            part = part + face * (v_refs[row][y] - value)
    return part


def columns(cols_x, cols_y, at_ends):
    return [
        (row, y)
        for row in range(cols_x)
        for y in range(cols_y)
        if (y in (0, cols_y - 1)) == at_ends
    ]


def middle_kernel(cols_x, last, *refs):
    v_refs, (coef_ref, diag_ref), refs = refs[:cols_x], refs[cols_x : cols_x + 2], refs[cols_x + 2 :]
    got, got_coefs, refs = refs[:2], refs[2:4], refs[4:]
    if last:
        w_refs, gram_ref = refs[:cols_x], refs[cols_x]
    else:
        blocks_ref, w_refs, next_refs = refs[0], refs[1 : 1 + cols_x], refs[1 + cols_x :]
    cols_y, count, _ = v_refs[0].shape
    total = jnp.zeros((2 * count, 2 * count), jnp.float32)
    for row, y in columns(cols_x, cols_y, True):
        w_refs[row][y] = operate(v_refs, coef_ref, diag_ref, got, got_coefs, row, y)
    for row, y in columns(cols_x, cols_y, False):
        w = operate(v_refs, coef_ref, diag_ref, got, got_coefs, row, y) * (1.0 / SCALE)
        w_refs[row][y] = w
        if last:
            total = total + split_gram(v_refs[row][y], w)
        else:
            next_refs[row][y] = apply_blocks(w, blocks_ref, row * cols_y + y)
    if last:
        gram_ref[...] = total


def end_kernel(cols_x, *refs):
    v_refs, refs = refs[:cols_x], refs[cols_x:]
    (coef_ref, blocks_ref), got, got_coefs, refs = refs[:2], refs[2:4], refs[4:6], refs[6:]
    part_refs, refs = refs[:cols_x], refs[2 * cols_x :]
    w_refs, next_refs, edges = refs[:cols_x], refs[cols_x : 2 * cols_x], refs[2 * cols_x :]
    cols_y = v_refs[0].shape[0]
    for row, y in columns(cols_x, cols_y, True):
        w = complete(part_refs[row][y], v_refs, coef_ref, got, got_coefs, row, y) * (1.0 / SCALE)
        w_refs[row][y] = w
        next_refs[row][y] = apply_blocks(w, blocks_ref, row * cols_y + y)
    write_edges(next_refs, None, edges[:2])
    write_side(0, next_refs[0], None, edges[2])


def split_gram(left, right):
    return lax.dot_general(
        jnp.concatenate(split(left), axis=0),
        jnp.concatenate(split(right), axis=0),
        (((1,), (1,)), ((), ())),
        preferred_element_type=jnp.float32,
    )


def fold(total):
    count = total.shape[0] // 2
    total = total[:count] + total[count:]
    total = total[:, :count] + total[:, count:]
    return 0.5 * (total + total.T)


def gram_kernel(cols_x, pairs, *refs):
    arrays, out_ref = refs[:-1], refs[-1]
    cols_y, count, _ = arrays[0].shape
    for slot, (left, right) in enumerate(pairs):
        total = jnp.zeros((2 * count, 2 * count), jnp.float32)
        for row in range(cols_x):
            for y in range(cols_y):
                total = total + split_gram(
                    arrays[left * cols_x + row][y], arrays[right * cols_x + row][y]
                )
        out_ref[:, slot * count : (slot + 1) * count] = fold(total)


def pack(squares):
    count = squares[0].shape[0]
    row = lax.broadcasted_iota(jnp.int32, (count, count), 0)
    lane = lax.broadcasted_iota(jnp.int32, (count, count), 1)
    halves = [
        jnp.where(row >= lane, first, second)
        for first, second in zip(squares[0::2], squares[1::2])
    ]
    diagonals = [
        jnp.sum(jnp.where(row == lane, second, 0.0), axis=1, keepdims=True)
        for second in squares[1::2]
    ]
    used = len(halves) * (count + 1)
    packed = jnp.concatenate(
        halves + diagonals + [jnp.zeros((count, 64 - used), jnp.float32)], axis=1
    )
    return jnp.concatenate([packed[: count // 2], packed[count // 2 :]], axis=1)


def unpack(packed, number):
    count = 2 * packed.shape[0]
    packed = jnp.concatenate([packed[:, :64], packed[:, 64:]], axis=0)
    row = lax.broadcasted_iota(jnp.int32, (count, count), 0)
    lane = lax.broadcasted_iota(jnp.int32, (count, count), 1)
    squares = []
    for i in range(number // 2):
        half = packed[:, i * count : (i + 1) * count]
        place = number // 2 * count + i
        turned = half.T
        squares.append(jnp.where(row >= lane, half, turned))
        second = jnp.where(row <= lane, half, turned)
        squares.append(jnp.where(row == lane, packed[:, place : place + 1], second))
    return squares


def last_kernel(cols_x, *refs):
    v_refs, refs = refs[:cols_x], refs[cols_x:]
    (coef_ref, early_ref, late_ref, gram_ref), got, got_coefs = refs[:4], refs[4:6], refs[6:8]
    part_refs, w_refs, out_ref = refs[8 : 8 + cols_x], refs[8 + cols_x : -1], refs[-1]
    cols_y, count, _ = v_refs[0].shape
    total = gram_ref[...]
    for row, y in columns(cols_x, cols_y, True):
        w = complete(part_refs[row][y], v_refs, coef_ref, got, got_coefs, row, y) * (1.0 / SCALE)
        w_refs[row][y] = w
        total = total + split_gram(v_refs[row][y], w)
    squares = [
        ref[:, i * count : (i + 1) * count]
        for ref in (early_ref, late_ref)
        for i in range(ref.shape[1] // count)
    ]
    packed = pack(squares + [fold(total)])
    for peer in range(out_ref.shape[0]):
        out_ref[peer] = packed


def solve_spd(matrix, target):
    size, width = matrix.shape[0], matrix.shape[1] + target.shape[1]
    lanes = 128
    work = jnp.concatenate(
        [matrix, target, jnp.zeros((size, lanes - width), jnp.float32)], axis=1
    )
    row = lax.broadcasted_iota(jnp.int32, (size, lanes), 0)

    def spread(p):
        return jnp.broadcast_to(work[:, p : p + 1], (size, lanes))

    ahead = {p: spread(p) for p in range(AHEAD)}
    inverses = jnp.zeros((size, lanes), jnp.float32)
    for p in range(size):
        column = ahead.pop(p)
        if p + AHEAD < size:
            ahead[p + AHEAD] = spread(p + AHEAD)
        inverse = 1.0 / column[p : p + 1, :]
        inverses = jnp.where(row == p, inverse, inverses)
        factor = jnp.where(row == p, 0.0, column)

        def eliminate(value):
            return value - factor * jnp.broadcast_to(value[p : p + 1, :] * inverse, value.shape)

        ahead = {q: eliminate(value) for q, value in ahead.items()}
        work = eliminate(work)
    return work[:, size:width] * inverses[:, size:width]


def finish_kernel(cols_x, blocks, sums_ref, *refs):
    r_refs, refs = refs[:cols_x], refs[cols_x:]
    v_refs, w_refs, refs = refs[: blocks * cols_x], refs[blocks * cols_x : 2 * blocks * cols_x], refs[2 * blocks * cols_x :]
    x_hbm, out_hbm, x_ref, out_ref, sem = refs
    cols_y = r_refs[0].shape[0]
    joint = sums_ref[0]
    for peer in range(1, sums_ref.shape[0]):
        joint = joint + sums_ref[peer]
    moments = unpack(joint, 2 * blocks)
    matrix = jnp.concatenate(
        [
            jnp.concatenate([moments[1 + i + j] for j in range(blocks)], axis=1)
            for i in range(blocks)
        ],
        axis=0,
    )
    target = jnp.concatenate(moments[:blocks], axis=0)
    coefs = solve_spd(matrix, target).T
    high = coefs.astype(jnp.bfloat16)
    middle, low = split(coefs - high.astype(jnp.float32))
    left = jnp.concatenate([high, high, middle, middle, low], axis=1)

    def combine(values, row, y):
        highs, lows = zip(*(split(values[j * cols_x + row][y]) for j in range(blocks)))
        right = jnp.concatenate(highs + lows + highs + lows + highs, axis=0)
        return jnp.dot(left, right, preferred_element_type=jnp.float32)

    copies = []

    def send(columns, ref, hbm, row):
        ref[row] = jnp.transpose(jnp.stack(columns), (1, 0, 2))
        target = hbm.at[:, oriented(row, cols_x)]
        copies.append(pltpu.make_async_copy(ref.at[row], target, sem.at[len(copies)]))
        copies[-1].start()

    for row in range(cols_x):
        send([r_refs[row][y] - combine(w_refs, row, y) for y in range(cols_y)], out_ref, out_hbm, row)
        send([combine(v_refs, row, y) * (1.0 / SCALE) for y in range(cols_y)], x_ref, x_hbm, row)
    for copy in copies:
        copy.wait()


def pairing(sizes, axis, phase):
    transfers = []
    for place in np.ndindex(*sizes):
        partner = list(place)
        partner[axis] += 1 if place[axis] % 2 == phase else -1
        if not 0 <= partner[axis] < sizes[axis]:
            partner = list(place)
            partner[1 - axis] ^= 1
            if partner[1 - axis] >= sizes[1 - axis]:
                continue
        transfers.append(tuple(int(np.ravel_multi_index(p, sizes)) for p in (place, partner)))
    return transfers


def exchange(slot, edge):
    sizes = tuple(lax.axis_size(axis) for axis in AXES)
    return lax.ppermute(edge, AXES, pairing(sizes, slot // 2, slot % 2))


def on_device(sources, well_columns, column_active, perm_root, storage_term, inverse_blocks):
    count, cols_x, cols_y, layers = sources.shape
    number = cols_x * cols_y
    devices = lax.axis_size("wide") * lax.axis_size("narrow")
    blocks = inverse_blocks.reshape((number,) + inverse_blocks.shape[2:])
    state, rows = (cols_y, count, layers), (number, layers)
    flat = (cols_y * count, layers)
    apply_flops = 4 * count * number * layers * inverse_blocks.shape[-1]
    gram_flops = 8 * count * count * number * layers

    ends = (cols_x * (count + 1), layers)
    side = (cols_y * (count + 1), layers)
    by_row = (cols_x, count, cols_y, layers)
    out = call(
        start_kernel,
        [state] * (2 * cols_x)
        + [rows, rows, jax.ShapeDtypeStruct(blocks.shape, blocks.dtype), ends, ends, side, (side[0] + 8, layers)],
        [HBM] * 6,
        *(
            pltpu.with_memory_space_constraint(a, pltpu.HBM)
            for a in (well_columns, column_active, sources, perm_root, storage_term, blocks)
        ),
        flops=apply_flops,
        scratch=[
            pltpu.SMEM(well_columns.shape, jnp.int32),
            pltpu.SMEM(column_active.shape, jnp.int32),
            pltpu.VMEM(by_row, jnp.float32),
            pltpu.VMEM(perm_root.shape, jnp.float32),
            pltpu.VMEM(storage_term.shape, jnp.float32),
            pltpu.SemaphoreType.DMA((4,)),
            pltpu.SemaphoreType.DMA((cols_x,)),
            pltpu.SemaphoreType.DMA((cols_x,)),
        ],
    )
    rhs, v = out[:cols_x], out[cols_x : 2 * cols_x]
    coef, diag_term, blocks, *edges = out[2 * cols_x :]
    got_coefs = got = [exchange(slot, edge) for slot, edge in enumerate(edges)]
    vs, ws, grams = [v], [], []
    later_ends, later_side = (cols_x * count, layers), (cols_y * count + 8, layers)

    for j in range(1, ITERS):
        parts = call(
            functools.partial(middle_kernel, cols_x, False),
            [state] * (2 * cols_x),
            [VMEM] * (cols_x + 7),
            *vs[-1], coef, diag_term, *got[2:], *got_coefs[2:], blocks,
            flops=apply_flops,
        )
        out = call(
            functools.partial(end_kernel, cols_x),
            [state] * (2 * cols_x) + [later_ends] * 2 + [later_side],
            [VMEM] * (3 * cols_x + 6),
            *vs[-1], coef, blocks, *got[:2], *got_coefs[:2], *parts,
            flops=apply_flops // 4,
            aliases={cols_x + 6 + i: i for i in range(2 * cols_x)},
        )
        w, v, edges = out[:cols_x], out[cols_x : 2 * cols_x], out[2 * cols_x :]
        edges.insert(2, v[-1].reshape(flat))
        got = [exchange(slot, edge) for slot, edge in enumerate(edges)]
        vs.append(v)
        ws.append(w)
        arrays = vs[-2] + v + w + (rhs if j == 1 else [])
        pairs = ([(0, 3)] if j == 1 else []) + [(0, 2), (1, 2)]
        grams += call(
            functools.partial(gram_kernel, cols_x, pairs),
            [(count, len(pairs) * count)],
            [VMEM] * len(arrays),
            *arrays,
            flops=len(pairs) * gram_flops,
        )
    *parts, gram = call(
        functools.partial(middle_kernel, cols_x, True),
        [state] * cols_x + [(2 * count, 2 * count)],
        [VMEM] * (cols_x + 6),
        *vs[-1], coef, diag_term, *got[2:], *got_coefs[2:],
        flops=gram_flops,
    )
    *w, joint = call(
        functools.partial(last_kernel, cols_x),
        [state] * cols_x + [(devices, count // 2, 128)],
        [VMEM] * (2 * cols_x + 8),
        *vs[-1], coef, *grams, gram, *got[:2], *got_coefs[:2], *parts,
        flops=gram_flops // 4,
        aliases={cols_x + 8 + i: i for i in range(cols_x)},
    )
    ws.append(w)
    joint = lax.all_to_all(joint, AXES, 0, 0)
    outs = call(
        functools.partial(finish_kernel, cols_x, ITERS),
        [sources.shape] * 2,
        [VMEM] * (1 + cols_x + 2 * ITERS * cols_x),
        joint, *rhs, *(a for v in vs for a in v), *(a for w in ws for a in w),
        flops=24 * ITERS * count * count * number * layers,
        out_specs=[HBM, HBM],
        scratch=[
            pltpu.VMEM(by_row, jnp.float32),
            pltpu.VMEM(by_row, jnp.float32),
            pltpu.SemaphoreType.DMA((2 * cols_x,)),
        ],
    )
    return tuple(outs)


def solution(mesh):
    in_specs = (
        P(None, "wide", "narrow", None),
        P(),
        P("wide", "narrow"),
        P("wide", "narrow", None),
        P("wide", "narrow", None),
        P("wide", "narrow", None, None, None),
    )
    out_specs = (P(None, "wide", "narrow", None), P(None, "wide", "narrow", None))
    return jax.shard_map(
        on_device, mesh=mesh, in_specs=in_specs, out_specs=out_specs, check_vma=False
    )
```

```python
import functools

import jax
import jax.numpy as jnp
import numpy as np
from jax import lax
from jax.experimental import pallas as pl
from jax.experimental.pallas import tpu as pltpu
from jax.sharding import PartitionSpec as P

ITERS = 3
WELL_RATE = 4.0
VMEM_BYTES = 24 * 1024 * 1024
VMEM = pl.BlockSpec(memory_space=pltpu.VMEM)
HBM = pl.BlockSpec(memory_space=pltpu.HBM)
SCALE = 64.0
AHEAD = 6


def call(kernel, out_shape, in_specs, *args, flops=0, out_specs=None, scratch=(), aliases=None):
    shapes = [
        s if isinstance(s, jax.ShapeDtypeStruct) else jax.ShapeDtypeStruct(s, jnp.float32)
        for s in out_shape
    ]
    size = sum(a.size * a.dtype.itemsize for a in args) + sum(s.size * 4 for s in shapes)
    out = pl.pallas_call(
        kernel,
        out_shape=shapes,
        in_specs=in_specs,
        out_specs=out_specs or [VMEM] * len(shapes),
        scratch_shapes=list(scratch),
        input_output_aliases=aliases or {},
        compiler_params=pltpu.CompilerParams(vmem_limit_bytes=VMEM_BYTES),
        cost_estimate=pl.CostEstimate(flops=flops, bytes_accessed=size, transcendentals=0),
    )(*args)
    return list(out)


def split(value):
    high = value.astype(jnp.bfloat16)
    return high, (value - high.astype(jnp.float32)).astype(jnp.bfloat16)


def apply_blocks(value, blocks_ref, col):
    count, layers = value.shape
    size = blocks_ref.shape[-1]
    number = layers // size
    terms = split(value)
    left = jnp.concatenate(
        [term[:, b * size : (b + 1) * size] for b in range(number) for term in terms], axis=0
    )
    right = jnp.concatenate([blocks_ref[col, b] for b in range(number)], axis=1)
    out = jnp.dot(left, right, preferred_element_type=jnp.float32)
    parts = []
    for b in range(number):
        piece = out[2 * b * count : 2 * (b + 1) * count, b * size : (b + 1) * size]
        parts.append(piece[:count] + piece[count:])
    return jnp.concatenate(parts, axis=1)


AXES = ("narrow", "wide")


def oriented(row, cols_x):
    odd = lax.rem(lax.axis_index("wide"), 2)
    return row + odd * (cols_x - 1 - 2 * row)


def partnered(slot):
    axis = AXES[slot // 2]
    place = lax.axis_index(axis)
    odd = lax.rem(place + slot, 2)
    partner = place + 1 - 2 * odd
    inside = jnp.logical_and(partner >= 0, partner < lax.axis_size(axis))
    return inside.astype(jnp.float32)


def write_edges(v_refs, coef_ref, edges):
    count = v_refs[0].shape[1]
    cols_y = v_refs[0].shape[0]
    odd = lax.rem(lax.axis_index("narrow"), 2)
    for ref, at_low in zip(edges, (odd, 1 - odd)):
        y = (1 - at_low) * (cols_y - 1)
        for row, v_ref in enumerate(v_refs):
            ref[row * count : (row + 1) * count, :] = v_ref[y]
            if coef_ref is not None:
                place = len(v_refs) * count + row
                ref[place : place + 1, :] = coef_ref[pl.ds(row * cols_y + y, 1), :]


def write_side(row, v_ref, coef_ref, edge):
    cols_y, count, _ = v_ref.shape
    for y in range(cols_y):
        edge[y * count : (y + 1) * count, :] = v_ref[y]
    if coef_ref is not None:
        edge[cols_y * count : cols_y * (count + 1), :] = coef_ref[
            row * cols_y : (row + 1) * cols_y, :
        ]


def start_kernel(
    wells_hbm, active_hbm, sources_hbm, perm_hbm, storage_hbm, blocks_hbm, *refs
):
    cols_x, cols_y = active_hbm.shape
    r_refs, v_refs, refs = refs[:cols_x], refs[cols_x : 2 * cols_x], refs[2 * cols_x :]
    coef_ref, diag_ref, blocks_ref, edge_0, edge_1, edge_2, edge_3 = refs[:7]
    wells_ref, active_ref, sources_ref, perm_ref, storage_ref, small_sem, big_sem, block_sem = refs[7:]
    _, count, layers = r_refs[0].shape
    small = [
        pltpu.make_async_copy(source, target, small_sem.at[i])
        for i, (source, target) in enumerate(
            (
                (wells_hbm, wells_ref),
                (active_hbm, active_ref),
                (perm_hbm, perm_ref),
                (storage_hbm, storage_ref),
            )
        )
    ]
    sources, blocks = [], []
    for row in range(cols_x):
        x = oriented(row, cols_x)
        sources.append(
            pltpu.make_async_copy(sources_hbm.at[:, x], sources_ref.at[row], big_sem.at[row])
        )
        blocks.append(
            pltpu.make_async_copy(
                blocks_hbm.at[pl.ds(x * cols_y, cols_y)],
                blocks_ref.at[pl.ds(row * cols_y, cols_y)],
                block_sem.at[row],
            )
        )
    for copy in small:
        copy.start()
    for pair in zip(sources, blocks):
        for copy in pair:
            copy.start()
    for copy in small:
        copy.wait()
    place = lax.broadcasted_iota(jnp.int32, (count, layers), 0)
    wells = jnp.zeros((count, layers), jnp.int32)
    for k in range(count):
        wells = jnp.where(place == k, wells_ref[k], wells)
    grid_y = cols_y * lax.axis_size("narrow")
    first_x, first_y = lax.axis_index("wide") * cols_x, lax.axis_index("narrow") * cols_y
    for row in range(cols_x):
        x = oriented(row, cols_x)
        for y in range(cols_y):
            col = row * cols_y + y
            active = active_ref[x, y].astype(jnp.float32)
            perm, storage = perm_ref[x, y : y + 1, :], storage_ref[x, y : y + 1, :]
            coef_ref[col : col + 1, :] = active * perm
            diag_ref[col : col + 1, :] = active * storage + (1.0 - active)
    for row in range(cols_x):
        sources[row].wait()
        across = jnp.transpose(sources_ref[row], (1, 0, 2))
        blocks[row].wait()
        for y in range(cols_y):
            column_id = (first_x + oriented(row, cols_x)) * grid_y + first_y + y
            r = across[y] + jnp.where(wells == column_id, WELL_RATE, 0.0)
            r_refs[row][y] = r
            v_refs[row][y] = apply_blocks(r, blocks_ref, row * cols_y + y)
    write_side(0, v_refs[0], coef_ref, edge_3)
    write_side(cols_x - 1, v_refs[-1], coef_ref, edge_2)
    write_edges(v_refs, coef_ref, (edge_0, edge_1))


def received(got, got_coefs, slot, i, number, count):
    place = number * count + i
    value = got[slot][i * count : (i + 1) * count, :]
    return value, got_coefs[slot][place : place + 1, :] * partnered(slot)


def operate(v_refs, coef_ref, diag_ref, got, got_coefs, row, y):
    cols_x = len(v_refs)
    cols_y, count, layers = v_refs[row].shape
    col = row * cols_y + y
    center = v_refs[row][y]
    coef = coef_ref[col : col + 1, :]
    lane = lax.broadcasted_iota(jnp.int32, (1, layers), 1)
    upper_coef = jnp.where(lane == layers - 1, 0.0, pltpu.roll(coef, layers - 1, 1))
    lower_coef = jnp.where(lane == 0, 0.0, pltpu.roll(coef, 1, 1))
    total = upper_coef * (center - pltpu.roll(center, layers - 1, 1))
    total = total + lower_coef * (center - pltpu.roll(center, 1, 1))
    for step_row, step_y in ((1, 0), (-1, 0), (0, 1), (0, -1)):
        other, ny = row + step_row, y + step_y
        if not 0 <= ny < cols_y:
            continue
        if 0 <= other < cols_x:
            place = other * cols_y + ny
            value, other_coef = v_refs[other][ny], coef_ref[place : place + 1, :]
        else:
            slot = 3 if step_row < 0 else 2
            value, other_coef = received(got, got_coefs, slot, y, cols_y, count)
        total = total + other_coef * (center - value)
    return diag_ref[col : col + 1, :] * center + coef * total


def complete(part, v_refs, coef_ref, got, got_coefs, row, y):
    cols_x = len(v_refs)
    cols_y, count, _ = v_refs[row].shape
    col = row * cols_y + y
    odd = lax.rem(lax.axis_index("narrow"), 2) == 1
    first, c_first = received(got, got_coefs, 0, row, cols_x, count)
    second, c_second = received(got, got_coefs, 1, row, cols_x, count)
    for at_end, low in ((y == 0, True), (y == cols_y - 1, False)):
        if at_end:
            value = jnp.where(odd == low, first, second)
            face = coef_ref[col : col + 1, :] * jnp.where(odd == low, c_first, c_second)
            part = part + face * (v_refs[row][y] - value)
    return part


def columns(rows, cols_y, at_ends):
    return [
        (row, y) for row in rows for y in range(cols_y) if (y in (0, cols_y - 1)) == at_ends
    ]


def middle_kernel(cols_x, rows, slots, last, *refs):
    v_refs, (coef_ref, diag_ref), refs = refs[:cols_x], refs[cols_x : cols_x + 2], refs[cols_x + 2 :]
    number = len(slots)
    got, got_coefs = dict(zip(slots, refs)), dict(zip(slots, refs[number:]))
    refs = refs[2 * number :]
    if last:
        w_refs, gram_ref = dict(zip(rows, refs)), refs[-1]
    else:
        blocks_ref, refs = refs[0], refs[1:]
        w_refs, next_refs = dict(zip(rows, refs)), dict(zip(rows, refs[len(rows) :]))
    cols_y, count, _ = v_refs[0].shape
    total = jnp.zeros((2 * count, 2 * count), jnp.float32)
    for row, y in columns(rows, cols_y, True):
        w_refs[row][y] = operate(v_refs, coef_ref, diag_ref, got, got_coefs, row, y)
    for row, y in columns(rows, cols_y, False):
        w = operate(v_refs, coef_ref, diag_ref, got, got_coefs, row, y) * (1.0 / SCALE)
        w_refs[row][y] = w
        if last:
            total = total + split_gram(v_refs[row][y], w)
        else:
            next_refs[row][y] = apply_blocks(w, blocks_ref, row * cols_y + y)
    if last:
        gram_ref[...] = total


def end_kernel(cols_x, *refs):
    v_refs, refs = refs[:cols_x], refs[cols_x:]
    (coef_ref, blocks_ref), got, got_coefs, refs = refs[:2], refs[2:4], refs[4:6], refs[6:]
    part_refs, refs = refs[:cols_x], refs[2 * cols_x :]
    w_refs, next_refs, edges = refs[:cols_x], refs[cols_x : 2 * cols_x], refs[2 * cols_x :]
    cols_y = v_refs[0].shape[0]
    for row, y in columns(range(cols_x), cols_y, True):
        w = complete(part_refs[row][y], v_refs, coef_ref, got, got_coefs, row, y) * (1.0 / SCALE)
        w_refs[row][y] = w
        next_refs[row][y] = apply_blocks(w, blocks_ref, row * cols_y + y)
    write_edges(next_refs, None, edges[:2])
    write_side(0, next_refs[0], None, edges[2])


def split_gram(left, right):
    return lax.dot_general(
        jnp.concatenate(split(left), axis=0),
        jnp.concatenate(split(right), axis=0),
        (((1,), (1,)), ((), ())),
        preferred_element_type=jnp.float32,
    )


def fold(total):
    count = total.shape[0] // 2
    total = total[:count] + total[count:]
    total = total[:, :count] + total[:, count:]
    return 0.5 * (total + total.T)


def gram_kernel(cols_x, pairs, *refs):
    arrays, out_ref = refs[:-1], refs[-1]
    cols_y, count, _ = arrays[0].shape
    for slot, (left, right) in enumerate(pairs):
        total = jnp.zeros((2 * count, 2 * count), jnp.float32)
        for row in range(cols_x):
            for y in range(cols_y):
                total = total + split_gram(
                    arrays[left * cols_x + row][y], arrays[right * cols_x + row][y]
                )
        out_ref[:, slot * count : (slot + 1) * count] = fold(total)


def pack(squares):
    count = squares[0].shape[0]
    row = lax.broadcasted_iota(jnp.int32, (count, count), 0)
    lane = lax.broadcasted_iota(jnp.int32, (count, count), 1)
    halves = [
        jnp.where(row >= lane, first, second)
        for first, second in zip(squares[0::2], squares[1::2])
    ]
    diagonals = [
        jnp.sum(jnp.where(row == lane, second, 0.0), axis=1, keepdims=True)
        for second in squares[1::2]
    ]
    used = len(halves) * (count + 1)
    packed = jnp.concatenate(
        halves + diagonals + [jnp.zeros((count, 64 - used), jnp.float32)], axis=1
    )
    return jnp.concatenate([packed[: count // 2], packed[count // 2 :]], axis=1)


def unpack(packed, number):
    count = 2 * packed.shape[0]
    packed = jnp.concatenate([packed[:, :64], packed[:, 64:]], axis=0)
    row = lax.broadcasted_iota(jnp.int32, (count, count), 0)
    lane = lax.broadcasted_iota(jnp.int32, (count, count), 1)
    squares = []
    for i in range(number // 2):
        half = packed[:, i * count : (i + 1) * count]
        place = number // 2 * count + i
        turned = half.T
        squares.append(jnp.where(row >= lane, half, turned))
        second = jnp.where(row <= lane, half, turned)
        squares.append(jnp.where(row == lane, packed[:, place : place + 1], second))
    return squares


def last_kernel(cols_x, grams, *refs):
    v_refs, refs = refs[:cols_x], refs[cols_x:]
    (coef_ref, early_ref, late_ref), got, got_coefs = refs[:3], refs[3:5], refs[5:7]
    gram_refs, refs, out_ref = refs[7 : 7 + grams], refs[7 + grams : -1], refs[-1]
    part_refs, w_refs = refs[:cols_x], refs[cols_x:]
    cols_y, count, _ = v_refs[0].shape
    total = gram_refs[0][...]
    for ref in gram_refs[1:]:
        total = total + ref[...]
    for row, y in columns(range(cols_x), cols_y, True):
        w = complete(part_refs[row][y], v_refs, coef_ref, got, got_coefs, row, y) * (1.0 / SCALE)
        w_refs[row][y] = w
        total = total + split_gram(v_refs[row][y], w)
    squares = [
        ref[:, i * count : (i + 1) * count]
        for ref in (early_ref, late_ref)
        for i in range(ref.shape[1] // count)
    ]
    packed = pack(squares + [fold(total)])
    for peer in range(out_ref.shape[0]):
        out_ref[peer] = packed


def solve_spd(matrix, target):
    size, width = matrix.shape[0], matrix.shape[1] + target.shape[1]
    lanes = 128
    work = jnp.concatenate(
        [matrix, target, jnp.zeros((size, lanes - width), jnp.float32)], axis=1
    )
    row = lax.broadcasted_iota(jnp.int32, (size, lanes), 0)

    def spread(p):
        return jnp.broadcast_to(work[:, p : p + 1], (size, lanes))

    ahead = {p: spread(p) for p in range(AHEAD)}
    inverses = jnp.zeros((size, lanes), jnp.float32)
    for p in range(size):
        column = ahead.pop(p)
        if p + AHEAD < size:
            ahead[p + AHEAD] = spread(p + AHEAD)
        inverse = 1.0 / column[p : p + 1, :]
        inverses = jnp.where(row == p, inverse, inverses)
        factor = jnp.where(row == p, 0.0, column)

        def eliminate(value):
            return value - factor * jnp.broadcast_to(value[p : p + 1, :] * inverse, value.shape)

        ahead = {q: eliminate(value) for q, value in ahead.items()}
        work = eliminate(work)
    return work[:, size:width] * inverses[:, size:width]


def finish_kernel(cols_x, blocks, sums_ref, *refs):
    r_refs, refs = refs[:cols_x], refs[cols_x:]
    v_refs, w_refs, refs = refs[: blocks * cols_x], refs[blocks * cols_x : 2 * blocks * cols_x], refs[2 * blocks * cols_x :]
    x_hbm, out_hbm, x_ref, out_ref, sem = refs
    cols_y = r_refs[0].shape[0]
    joint = sums_ref[0]
    for peer in range(1, sums_ref.shape[0]):
        joint = joint + sums_ref[peer]
    moments = unpack(joint, 2 * blocks)
    matrix = jnp.concatenate(
        [
            jnp.concatenate([moments[1 + i + j] for j in range(blocks)], axis=1)
            for i in range(blocks)
        ],
        axis=0,
    )
    target = jnp.concatenate(moments[:blocks], axis=0)
    coefs = solve_spd(matrix, target).T
    high = coefs.astype(jnp.bfloat16)
    middle, low = split(coefs - high.astype(jnp.float32))
    left = jnp.concatenate([high, high, middle, middle, low], axis=1)

    def combine(values, row, y):
        highs, lows = zip(*(split(values[j * cols_x + row][y]) for j in range(blocks)))
        right = jnp.concatenate(highs + lows + highs + lows + highs, axis=0)
        return jnp.dot(left, right, preferred_element_type=jnp.float32)

    copies = []

    def send(columns, ref, hbm, row):
        ref[row] = jnp.transpose(jnp.stack(columns), (1, 0, 2))
        target = hbm.at[:, oriented(row, cols_x)]
        copies.append(pltpu.make_async_copy(ref.at[row], target, sem.at[len(copies)]))
        copies[-1].start()

    for row in range(cols_x):
        send([r_refs[row][y] - combine(w_refs, row, y) for y in range(cols_y)], out_ref, out_hbm, row)
        send([combine(v_refs, row, y) * (1.0 / SCALE) for y in range(cols_y)], x_ref, x_hbm, row)
    for copy in copies:
        copy.wait()


def pairing(sizes, axis, phase):
    transfers = []
    for place in np.ndindex(*sizes):
        partner = list(place)
        partner[axis] += 1 if place[axis] % 2 == phase else -1
        if not 0 <= partner[axis] < sizes[axis]:
            partner = list(place)
            partner[1 - axis] ^= 1
            if partner[1 - axis] >= sizes[1 - axis]:
                continue
        transfers.append(tuple(int(np.ravel_multi_index(p, sizes)) for p in (place, partner)))
    return transfers


def exchange(slot, edge):
    sizes = tuple(lax.axis_size(axis) for axis in AXES)
    return lax.ppermute(edge, AXES, pairing(sizes, slot // 2, slot % 2))


def on_device(sources, well_columns, column_active, perm_root, storage_term, inverse_blocks):
    count, cols_x, cols_y, layers = sources.shape
    number = cols_x * cols_y
    devices = lax.axis_size("wide") * lax.axis_size("narrow")
    blocks = inverse_blocks.reshape((number,) + inverse_blocks.shape[2:])
    state, rows = (cols_y, count, layers), (number, layers)
    flat = (cols_y * count, layers)
    apply_flops = 4 * count * number * layers * inverse_blocks.shape[-1]
    gram_flops = 8 * count * count * number * layers

    ends = (cols_x * (count + 1), layers)
    side = (cols_y * (count + 1), layers)
    by_row = (cols_x, count, cols_y, layers)
    out = call(
        start_kernel,
        [state] * (2 * cols_x)
        + [rows, rows, jax.ShapeDtypeStruct(blocks.shape, blocks.dtype), ends, ends, side, (side[0] + 8, layers)],
        [HBM] * 6,
        *(
            pltpu.with_memory_space_constraint(a, pltpu.HBM)
            for a in (well_columns, column_active, sources, perm_root, storage_term, blocks)
        ),
        flops=apply_flops,
        scratch=[
            pltpu.SMEM(well_columns.shape, jnp.int32),
            pltpu.SMEM(column_active.shape, jnp.int32),
            pltpu.VMEM(by_row, jnp.float32),
            pltpu.VMEM(perm_root.shape, jnp.float32),
            pltpu.VMEM(storage_term.shape, jnp.float32),
            pltpu.SemaphoreType.DMA((4,)),
            pltpu.SemaphoreType.DMA((cols_x,)),
            pltpu.SemaphoreType.DMA((cols_x,)),
        ],
    )
    rhs, v = out[:cols_x], out[cols_x : 2 * cols_x]
    coef, diag_term, blocks, *edges = out[2 * cols_x :]
    got_coefs = got = [exchange(slot, edge) for slot, edge in enumerate(edges)]
    vs, ws, grams = [v], [], []
    later_ends, later_side = (cols_x * count, layers), (cols_y * count + 8, layers)

    if cols_x > 1:
        shares = [(tuple(range(1, cols_x)), (2,)), ((0,), (3,))]
    else:
        shares = [((0,), (2, 3))]

    def middle(last):
        w, v, totals = [], [], []
        for rows, slots in shares:
            out = call(
                functools.partial(middle_kernel, cols_x, rows, slots, last),
                [state] * (len(rows) * (1 if last else 2)) + [(2 * count, 2 * count)] * last,
                [VMEM] * (cols_x + 3 - last + 2 * len(slots)),
                *vs[-1], coef, diag_term, *(got[i] for i in slots), *(got_coefs[i] for i in slots),
                *([] if last else [blocks]),
                flops=apply_flops // len(shares),
            )
            w = out[: len(rows)] + w
            if last:
                totals += out[len(rows) :]
            else:
                v = out[len(rows) :] + v
        return w + v, totals

    for j in range(1, ITERS):
        parts, _ = middle(False)
        out = call(
            functools.partial(end_kernel, cols_x),
            [state] * (2 * cols_x) + [later_ends] * 2 + [later_side],
            [VMEM] * (3 * cols_x + 6),
            *vs[-1], coef, blocks, *got[:2], *got_coefs[:2], *parts,
            flops=apply_flops // 4,
            aliases={cols_x + 6 + i: i for i in range(2 * cols_x)},
        )
        w, v, edges = out[:cols_x], out[cols_x : 2 * cols_x], out[2 * cols_x :]
        edges.insert(2, v[-1].reshape(flat))
        got = [exchange(slot, edge) for slot, edge in enumerate(edges)]
        vs.append(v)
        ws.append(w)
        arrays = vs[-2] + v + w + (rhs if j == 1 else [])
        pairs = ([(0, 3)] if j == 1 else []) + [(0, 2), (1, 2)]
        grams += call(
            functools.partial(gram_kernel, cols_x, pairs),
            [(count, len(pairs) * count)],
            [VMEM] * len(arrays),
            *arrays,
            flops=len(pairs) * gram_flops,
        )
    parts, totals = middle(True)
    *w, joint = call(
        functools.partial(last_kernel, cols_x, len(totals)),
        [state] * cols_x + [(devices, count // 2, 128)],
        [VMEM] * (2 * cols_x + 7 + len(totals)),
        *vs[-1], coef, *grams, *got[:2], *got_coefs[:2], *totals, *parts,
        flops=gram_flops // 4,
        aliases={cols_x + 7 + len(totals) + i: i for i in range(cols_x)},
    )
    ws.append(w)
    joint = lax.all_to_all(joint, AXES, 0, 0)
    outs = call(
        functools.partial(finish_kernel, cols_x, ITERS),
        [sources.shape] * 2,
        [VMEM] * (1 + cols_x + 2 * ITERS * cols_x),
        joint, *rhs, *(a for v in vs for a in v), *(a for w in ws for a in w),
        flops=24 * ITERS * count * count * number * layers,
        out_specs=[HBM, HBM],
        scratch=[
            pltpu.VMEM(by_row, jnp.float32),
            pltpu.VMEM(by_row, jnp.float32),
            pltpu.SemaphoreType.DMA((2 * cols_x,)),
        ],
    )
    return tuple(outs)


def solution(mesh):
    in_specs = (
        P(None, "wide", "narrow", None),
        P(),
        P("wide", "narrow"),
        P("wide", "narrow", None),
        P("wide", "narrow", None),
        P("wide", "narrow", None, None, None),
    )
    out_specs = (P(None, "wide", "narrow", None), P(None, "wide", "narrow", None))
    return jax.shard_map(
        on_device, mesh=mesh, in_specs=in_specs, out_specs=out_specs, check_vma=False
    )
```

```python
import functools

import jax
import jax.numpy as jnp
import numpy as np
from jax import lax
from jax.experimental import pallas as pl
from jax.experimental.pallas import tpu as pltpu
from jax.sharding import PartitionSpec as P

ITERS = 3
WELL_RATE = 4.0
VMEM_BYTES = 24 * 1024 * 1024
VMEM = pl.BlockSpec(memory_space=pltpu.VMEM)
HBM = pl.BlockSpec(memory_space=pltpu.HBM)
SCALE = 64.0
AHEAD = 6


def call(kernel, out_shape, in_specs, *args, flops=0, out_specs=None, scratch=()):
    shapes = [
        s if isinstance(s, jax.ShapeDtypeStruct) else jax.ShapeDtypeStruct(s, jnp.float32)
        for s in out_shape
    ]
    size = sum(a.size * a.dtype.itemsize for a in args) + sum(s.size * 4 for s in shapes)
    out = pl.pallas_call(
        kernel,
        out_shape=shapes,
        in_specs=in_specs,
        out_specs=out_specs or [VMEM] * len(shapes),
        scratch_shapes=list(scratch),
        compiler_params=pltpu.CompilerParams(vmem_limit_bytes=VMEM_BYTES),
        cost_estimate=pl.CostEstimate(flops=flops, bytes_accessed=size, transcendentals=0),
    )(*args)
    return list(out)


def split(value):
    high = value.astype(jnp.bfloat16)
    return high, (value - high.astype(jnp.float32)).astype(jnp.bfloat16)


def apply_blocks(value, blocks_ref, col):
    count, layers = value.shape
    size = blocks_ref.shape[-1]
    number = layers // size
    terms = split(value)
    left = jnp.concatenate(
        [term[:, b * size : (b + 1) * size] for b in range(number) for term in terms], axis=0
    )
    right = jnp.concatenate([blocks_ref[col, b] for b in range(number)], axis=1)
    out = jnp.dot(left, right, preferred_element_type=jnp.float32)
    parts = []
    for b in range(number):
        piece = out[2 * b * count : 2 * (b + 1) * count, b * size : (b + 1) * size]
        parts.append(piece[:count] + piece[count:])
    return jnp.concatenate(parts, axis=1)


AXES = ("narrow", "wide")


def oriented(row, cols_x):
    odd = lax.rem(lax.axis_index("wide"), 2)
    return row + odd * (cols_x - 1 - 2 * row)


def partnered(slot):
    axis = AXES[slot // 2]
    place = lax.axis_index(axis)
    odd = lax.rem(place + slot, 2)
    partner = place + 1 - 2 * odd
    inside = jnp.logical_and(partner >= 0, partner < lax.axis_size(axis))
    return inside.astype(jnp.float32)


def write_edges(v_refs, coef_ref, edges):
    count = v_refs[0].shape[1]
    cols_y = v_refs[0].shape[0]
    odd = lax.rem(lax.axis_index("narrow"), 2)
    for ref, at_low in zip(edges, (odd, 1 - odd)):
        y = (1 - at_low) * (cols_y - 1)
        for row, v_ref in enumerate(v_refs):
            ref[row * count : (row + 1) * count, :] = v_ref[y]
            if coef_ref is not None:
                place = len(v_refs) * count + row
                ref[place : place + 1, :] = coef_ref[pl.ds(row * cols_y + y, 1), :]


def write_side(row, v_ref, coef_ref, edge):
    cols_y, count, _ = v_ref.shape
    for y in range(cols_y):
        edge[y * count : (y + 1) * count, :] = v_ref[y]
    if coef_ref is not None:
        edge[cols_y * count : cols_y * (count + 1), :] = coef_ref[
            row * cols_y : (row + 1) * cols_y, :
        ]


def start_kernel(
    wells_hbm, active_hbm, sources_hbm, perm_hbm, storage_hbm, blocks_hbm, *refs
):
    cols_x, cols_y = active_hbm.shape
    r_refs, v_refs, refs = refs[:cols_x], refs[cols_x : 2 * cols_x], refs[2 * cols_x :]
    coef_ref, diag_ref, blocks_ref, edge_0, edge_1, edge_2, edge_3 = refs[:7]
    wells_ref, active_ref, sources_ref, perm_ref, storage_ref, small_sem, big_sem, block_sem = refs[7:]
    _, count, layers = r_refs[0].shape
    small = [
        pltpu.make_async_copy(source, target, small_sem.at[i])
        for i, (source, target) in enumerate(
            (
                (wells_hbm, wells_ref),
                (active_hbm, active_ref),
                (perm_hbm, perm_ref),
                (storage_hbm, storage_ref),
            )
        )
    ]
    sources, blocks = [], []
    for row in range(cols_x):
        x = oriented(row, cols_x)
        sources.append(
            pltpu.make_async_copy(sources_hbm.at[:, x], sources_ref.at[row], big_sem.at[row])
        )
        blocks.append(
            pltpu.make_async_copy(
                blocks_hbm.at[pl.ds(x * cols_y, cols_y)],
                blocks_ref.at[pl.ds(row * cols_y, cols_y)],
                block_sem.at[row],
            )
        )
    for copy in small:
        copy.start()
    for pair in zip(sources, blocks):
        for copy in pair:
            copy.start()
    for copy in small:
        copy.wait()
    place = lax.broadcasted_iota(jnp.int32, (count, layers), 0)
    wells = jnp.zeros((count, layers), jnp.int32)
    for k in range(count):
        wells = jnp.where(place == k, wells_ref[k], wells)
    grid_y = cols_y * lax.axis_size("narrow")
    first_x, first_y = lax.axis_index("wide") * cols_x, lax.axis_index("narrow") * cols_y
    for row in range(cols_x):
        x = oriented(row, cols_x)
        for y in range(cols_y):
            col = row * cols_y + y
            active = active_ref[x, y].astype(jnp.float32)
            perm, storage = perm_ref[x, y : y + 1, :], storage_ref[x, y : y + 1, :]
            coef_ref[col : col + 1, :] = active * perm
            diag_ref[col : col + 1, :] = active * storage + (1.0 - active)
    for row in range(cols_x):
        sources[row].wait()
        across = jnp.transpose(sources_ref[row], (1, 0, 2))
        blocks[row].wait()
        for y in range(cols_y):
            column_id = (first_x + oriented(row, cols_x)) * grid_y + first_y + y
            r = across[y] + jnp.where(wells == column_id, WELL_RATE, 0.0)
            r_refs[row][y] = r
            v_refs[row][y] = apply_blocks(r, blocks_ref, row * cols_y + y)
    write_side(0, v_refs[0], coef_ref, edge_3)
    write_side(cols_x - 1, v_refs[-1], coef_ref, edge_2)
    write_edges(v_refs, coef_ref, (edge_0, edge_1))


def received(got, got_coefs, slot, i, number, count):
    place = number * count + i
    value = got[slot][i * count : (i + 1) * count, :]
    return value, got_coefs[slot][place : place + 1, :] * partnered(slot)


def operate(v_refs, coef_ref, diag_ref, got, got_coefs, row, y):
    cols_x = len(v_refs)
    cols_y, count, layers = v_refs[row].shape
    col = row * cols_y + y
    center = v_refs[row][y]
    coef = coef_ref[col : col + 1, :]
    lane = lax.broadcasted_iota(jnp.int32, (1, layers), 1)
    upper_coef = jnp.where(lane == layers - 1, 0.0, pltpu.roll(coef, layers - 1, 1))
    lower_coef = jnp.where(lane == 0, 0.0, pltpu.roll(coef, 1, 1))
    total = upper_coef * (center - pltpu.roll(center, layers - 1, 1))
    total = total + lower_coef * (center - pltpu.roll(center, 1, 1))
    for step_row, step_y in ((1, 0), (-1, 0), (0, 1), (0, -1)):
        other, ny = row + step_row, y + step_y
        if 0 <= ny < cols_y and 0 <= other < cols_x:
            place = other * cols_y + ny
            value, other_coef = v_refs[other][ny], coef_ref[place : place + 1, :]
        elif step_row:
            slot = 3 if step_row < 0 else 2
            value, other_coef = received(got, got_coefs, slot, y, cols_y, count)
        else:
            odd = lax.rem(lax.axis_index("narrow"), 2) == 1
            first, c_first = received(got, got_coefs, 0, row, cols_x, count)
            second, c_second = received(got, got_coefs, 1, row, cols_x, count)
            low = step_y < 0
            value = jnp.where(odd == low, first, second)
            other_coef = jnp.where(odd == low, c_first, c_second)
        total = total + other_coef * (center - value)
    return (diag_ref[col : col + 1, :] * center + coef * total) * (1.0 / SCALE)


def row_kernel(cols_x, rows, slots, after, *refs):
    v_refs, (coef_ref, diag_ref), refs = refs[:cols_x], refs[cols_x : cols_x + 2], refs[cols_x + 2 :]
    number = len(slots)
    got, got_coefs = dict(zip(slots, refs)), dict(zip(slots, refs[number:]))
    blocks_ref, refs = refs[2 * number], refs[2 * number + 1 + after :]
    others = cols_x - len(rows) if rows[0] == 0 else 0
    done, refs = refs[:others], refs[others:]
    w_refs, next_refs, edges = refs[: len(rows)], refs[len(rows) : 2 * len(rows)], refs[2 * len(rows) :]
    cols_y = v_refs[0].shape[0]
    for row, w_ref, next_ref in zip(rows, w_refs, next_refs):
        for y in range(cols_y):
            w = operate(v_refs, coef_ref, diag_ref, got, got_coefs, row, y)
            w_ref[y] = w
            next_ref[y] = apply_blocks(w, blocks_ref, row * cols_y + y)
    if edges:
        write_edges((*next_refs, *done), None, edges[:2])
        write_side(0, next_refs[0], None, edges[2])


def share_size(matrices, count):
    return (matrices * (count + 1) + 1) // 2


def lanes_of(used):
    return -(-used // 64) * 64


def last_kernel(cols_x, rows, slots, grams, *refs):
    v_refs, (coef_ref, diag_ref), refs = refs[:cols_x], refs[cols_x : cols_x + 2], refs[cols_x + 2 :]
    number = len(slots)
    got, got_coefs = dict(zip(slots, refs)), dict(zip(slots, refs[number:]))
    refs = refs[2 * number :]
    gram_refs, w_refs, out_ref = refs[:grams], refs[grams:-1], refs[-1]
    cols_y, count, _ = v_refs[0].shape
    total = jnp.zeros((2 * count, 2 * count), jnp.float32)
    for ref in gram_refs[2:]:
        total = total + ref[...]
    for row, w_ref in zip(rows, w_refs):
        for y in range(cols_y):
            w = operate(v_refs, coef_ref, diag_ref, got, got_coefs, row, y)
            w_ref[y] = w
            total = total + split_gram([v_refs[row][y]], w)
    if rows[0] != 0:
        out_ref[...] = total
        return
    size = share_size(2 * ITERS - 1, count)
    last = fold_square(fold(total))
    used = size + last.shape[1]
    rest = jnp.zeros((count // 2, lanes_of(used) - used), jnp.float32)
    early = (gram_refs[0][...] + gram_refs[1][...])[:, :size]
    packed = jnp.concatenate([early, last, rest], axis=1)
    middle = count // 4
    packed = jnp.concatenate(
        [packed[:middle], packed[middle:]], axis=1
    )
    for peer in range(out_ref.shape[0]):
        out_ref[peer] = packed


def split_gram(lefts, right):
    return lax.dot_general(
        jnp.concatenate([term for left in lefts for term in split(left)], axis=0),
        jnp.concatenate(split(right), axis=0),
        (((1,), (1,)), ((), ())),
        preferred_element_type=jnp.float32,
    )


def fold(total):
    count = total.shape[0] // 2
    total = total[:count] + total[count:]
    total = total[:, :count] + total[:, count:]
    return 0.5 * (total + total.T)


def grams_of(cols_x, groups, arrays):
    cols_y, count, _ = arrays[0].shape
    squares = []
    for lefts, right in groups:
        total = jnp.zeros((2 * count * len(lefts), 2 * count), jnp.float32)
        for row in range(cols_x):
            for y in range(cols_y):
                total = total + split_gram(
                    [arrays[left * cols_x + row][y] for left in lefts],
                    arrays[right * cols_x + row][y],
                )
        squares += [fold(total[2 * count * i : 2 * count * (i + 1)]) for i in range(len(lefts))]
    return squares


def gram_kernel(cols_x, groups, *refs):
    refs[-1][...] = jnp.concatenate(grams_of(cols_x, groups, refs[:-1]), axis=1)


def fold_square(square):
    half = square.shape[0] // 2
    bottom = jnp.concatenate([square[half:], jnp.zeros((half, 1), jnp.float32)], axis=1)
    top = jnp.concatenate(
        [jnp.zeros((half, half + 1), jnp.float32), square[:half, :half]], axis=1
    )
    row = lax.broadcasted_iota(jnp.int32, bottom.shape, 0)
    lane = lax.broadcasted_iota(jnp.int32, bottom.shape, 1)
    return jnp.where(lane <= half + row, bottom, top)


def unfold_squares(folded):
    half = folded.shape[0]
    row = lax.broadcasted_iota(jnp.int32, (half, half), 0)
    lane = lax.broadcasted_iota(jnp.int32, (half, half), 1)
    diagonal = jnp.where(row == lane, 0.5, 1.0)
    width = 2 * half + 1
    parts = []
    for i in range(folded.shape[1] // width):
        one = folded[:, i * width : (i + 1) * width]
        upper = jnp.where(row <= lane, one[:, half + 1 :] * diagonal, 0.0)
        lower = jnp.where(row >= lane, one[:, half : 2 * half] * diagonal, 0.0)
        parts.append(
            jnp.concatenate(
                [
                    jnp.concatenate([upper, jnp.zeros_like(upper)], axis=1),
                    jnp.concatenate([one[:, :half], lower], axis=1),
                ],
                axis=0,
            )
        )
    turned = jnp.concatenate(parts, axis=1).T
    return [
        part + turned[2 * half * i : 2 * half * (i + 1)] for i, part in enumerate(parts)
    ]


def share(folded, axis_odd):
    lanes = folded.shape[1]
    size = (lanes + 1) // 2
    return jnp.where(axis_odd, folded[:, lanes - size :], folded[:, :size])


def halves_kernel(cols_x, groups, *refs):
    arrays, early_refs, (send_ref, keep_ref) = refs[:-3], refs[-3:-2], refs[-2:]
    count = arrays[0].shape[1]
    squares = [
        ref[:, i * count : (i + 1) * count]
        for ref in early_refs
        for i in range(ref.shape[1] // count)
    ]
    squares += grams_of(cols_x, groups, arrays)
    folded = jnp.concatenate([fold_square(square) for square in squares], axis=1)
    odd = lax.rem(lax.axis_index("wide"), 2) == 1
    for ref, mine in ((send_ref, jnp.logical_not(odd)), (keep_ref, odd)):
        half = share(folded, mine)
        rest = jnp.zeros((half.shape[0], ref.shape[1] - half.shape[1]), jnp.float32)
        ref[...] = jnp.concatenate([half, rest], axis=1)


def solve_spd(matrix, target):
    size, width = matrix.shape[0], matrix.shape[1] + target.shape[1]
    lanes = 128
    work = jnp.concatenate(
        [matrix, target, jnp.zeros((size, lanes - width), jnp.float32)], axis=1
    )
    row = lax.broadcasted_iota(jnp.int32, (size, lanes), 0)

    def spread(p):
        return jnp.broadcast_to(work[:, p : p + 1], (size, lanes))

    ahead = {p: spread(p) for p in range(AHEAD)}
    inverses = jnp.zeros((size, lanes), jnp.float32)
    for p in range(size):
        column = ahead.pop(p)
        if p + AHEAD < size:
            ahead[p + AHEAD] = spread(p + AHEAD)
        inverse = 1.0 / column[p : p + 1, :]
        inverses = jnp.where(row == p, inverse, inverses)
        factor = jnp.where(row == p, 0.0, column)

        def eliminate(value):
            return value - factor * jnp.broadcast_to(value[p : p + 1, :] * inverse, value.shape)

        ahead = {q: eliminate(value) for q, value in ahead.items()}
        work = eliminate(work)
    return work[:, size:width] * inverses[:, size:width]


def finish_kernel(cols_x, blocks, sums_ref, *refs):
    r_refs, refs = refs[:cols_x], refs[cols_x:]
    v_refs, w_refs, refs = refs[: blocks * cols_x], refs[blocks * cols_x : 2 * blocks * cols_x], refs[2 * blocks * cols_x :]
    x_hbm, out_hbm, x_ref, out_ref, sem = refs
    cols_y = r_refs[0].shape[0]
    count = r_refs[0].shape[1]
    sums = []
    for parity in range(2):
        total = sums_ref[parity]
        for peer in range(parity + 2, sums_ref.shape[0], 2):
            total = total + sums_ref[peer]
        middle = total.shape[1] // 2
        sums.append(jnp.concatenate([total[:, :middle], total[:, middle:]], axis=0))
    even, odd = sums
    size, width = share_size(2 * blocks - 1, count), count + 1
    early = (2 * blocks - 1) * width
    moments = unfold_squares(
        jnp.concatenate(
            [
                even[:, :size],
                odd[:, 2 * size - early : size],
                even[:, size : size + width] + odd[:, size : size + width],
            ],
            axis=1,
        )
    )
    matrix = jnp.concatenate(
        [
            jnp.concatenate([moments[1 + i + j] for j in range(blocks)], axis=1)
            for i in range(blocks)
        ],
        axis=0,
    )
    target = jnp.concatenate(moments[:blocks], axis=0)
    coefs = solve_spd(matrix, target).T
    high = coefs.astype(jnp.bfloat16)
    middle, low = split(coefs - high.astype(jnp.float32))
    left = jnp.concatenate([high, high, middle, middle, low], axis=1)

    def combine(values, row, y):
        highs, lows = zip(*(split(values[j * cols_x + row][y]) for j in range(blocks)))
        right = jnp.concatenate(highs + lows + highs + lows + highs, axis=0)
        return jnp.dot(left, right, preferred_element_type=jnp.float32)

    copies = []

    def send(columns, ref, hbm, row):
        ref[row] = jnp.transpose(jnp.stack(columns), (1, 0, 2))
        target = hbm.at[:, oriented(row, cols_x)]
        copies.append(pltpu.make_async_copy(ref.at[row], target, sem.at[len(copies)]))
        copies[-1].start()

    for row in range(cols_x):
        send([r_refs[row][y] - combine(w_refs, row, y) for y in range(cols_y)], out_ref, out_hbm, row)
        send([combine(v_refs, row, y) * (1.0 / SCALE) for y in range(cols_y)], x_ref, x_hbm, row)
    for copy in copies:
        copy.wait()


def pairing(sizes, axis, phase):
    transfers = []
    for place in np.ndindex(*sizes):
        partner = list(place)
        partner[axis] += 1 if place[axis] % 2 == phase else -1
        if not 0 <= partner[axis] < sizes[axis]:
            partner = list(place)
            partner[1 - axis] ^= 1
            if partner[1 - axis] >= sizes[1 - axis]:
                continue
        transfers.append(tuple(int(np.ravel_multi_index(p, sizes)) for p in (place, partner)))
    return transfers


def exchange(slot, edge):
    sizes = tuple(lax.axis_size(axis) for axis in AXES)
    return lax.ppermute(edge, AXES, pairing(sizes, slot // 2, slot % 2))


def on_device(sources, well_columns, column_active, perm_root, storage_term, inverse_blocks):
    count, cols_x, cols_y, layers = sources.shape
    number = cols_x * cols_y
    devices = lax.axis_size("wide") * lax.axis_size("narrow")
    blocks = inverse_blocks.reshape((number,) + inverse_blocks.shape[2:])
    state, rows = (cols_y, count, layers), (number, layers)
    flat = (cols_y * count, layers)
    apply_flops = 4 * count * number * layers * inverse_blocks.shape[-1]
    gram_flops = 8 * count * count * number * layers

    ends = (cols_x * (count + 1), layers)
    side = (cols_y * (count + 1), layers)
    by_row = (cols_x, count, cols_y, layers)
    out = call(
        start_kernel,
        [state] * (2 * cols_x)
        + [rows, rows, jax.ShapeDtypeStruct(blocks.shape, blocks.dtype), ends, ends, side, (side[0] + 8, layers)],
        [HBM] * 6,
        *(
            pltpu.with_memory_space_constraint(a, pltpu.HBM)
            for a in (well_columns, column_active, sources, perm_root, storage_term, blocks)
        ),
        flops=apply_flops,
        scratch=[
            pltpu.SMEM(well_columns.shape, jnp.int32),
            pltpu.SMEM(column_active.shape, jnp.int32),
            pltpu.VMEM(by_row, jnp.float32),
            pltpu.VMEM(perm_root.shape, jnp.float32),
            pltpu.VMEM(storage_term.shape, jnp.float32),
            pltpu.SemaphoreType.DMA((4,)),
            pltpu.SemaphoreType.DMA((cols_x,)),
            pltpu.SemaphoreType.DMA((cols_x,)),
        ],
    )
    rhs, v = out[:cols_x], out[cols_x : 2 * cols_x]
    coef, diag_term, blocks, *edges = out[2 * cols_x :]
    got_coefs = got = [exchange(slot, edge) for slot, edge in enumerate(edges)]
    vs, ws, grams = [v], [], []
    later_ends, later_side = (cols_x * count, layers), (cols_y * count + 8, layers)

    if cols_x > 1:
        shares = [(tuple(range(1, cols_x)), (0, 1, 2)), ((0,), (0, 1, 3))]
    else:
        shares = [((0,), (0, 1, 2, 3))]

    def halo(slots):
        return [*(got[i] for i in slots), *(got_coefs[i] for i in slots)]

    for j in range(1, ITERS):
        w, v = [], []
        for rows, slots in shares:
            ahead = [] if v else grams
            operands = [*vs[-1], coef, diag_term, *halo(slots), blocks, *ahead, *v]
            out = call(
                functools.partial(row_kernel, cols_x, rows, slots, len(ahead)),
                [state] * (2 * len(rows))
                + ([later_ends] * 2 + [later_side] if rows[0] == 0 else []),
                [VMEM] * len(operands),
                *operands,
                flops=apply_flops // len(shares),
            )
            w = out[: len(rows)] + w
            v = out[len(rows) : 2 * len(rows)] + v
            edges = out[2 * len(rows) :]
        edges.insert(2, v[-1].reshape(flat))
        got = [exchange(slot, edge) for slot, edge in enumerate(edges)]
        vs.append(v)
        ws.append(w)
        arrays = vs[-2] + v + w + (rhs if j == 1 else [])
        groups = ([((0,), 3)] if j == 1 else []) + [((0, 1), 2)]
        number_of = len(groups) + 1
        if j < ITERS - 1:
            grams += call(
                functools.partial(gram_kernel, cols_x, groups),
                [(count, number_of * count)],
                [VMEM] * len(arrays),
                *arrays,
                flops=number_of * gram_flops,
            )
        else:
            send, keep = call(
                functools.partial(halves_kernel, cols_x, groups),
                [(count // 2, 128)] * 2,
                [VMEM] * (len(arrays) + 1),
                *arrays, *grams,
                flops=number_of * gram_flops,
            )
            grams = [keep, exchange(2, send)]
    lanes = lanes_of(share_size(2 * ITERS - 1, count) + count + 1)
    w, totals = [], []
    for rows, slots in shares:
        first = [] if rows[0] else [*grams, *totals]
        operands = [*vs[-1], coef, diag_term, *halo(slots), *first]
        out = call(
            functools.partial(last_kernel, cols_x, rows, slots, len(first)),
            [state] * len(rows)
            + [(2 * count, 2 * count) if rows[0] else (devices, count // 4, 2 * lanes)],
            [VMEM] * len(operands),
            *operands,
            flops=gram_flops // len(shares),
        )
        w = out[:-1] + w
        totals.append(out[-1])
    joint = totals[-1]
    ws.append(w)
    joint = lax.all_to_all(joint, AXES, 0, 0)
    outs = call(
        functools.partial(finish_kernel, cols_x, ITERS),
        [sources.shape] * 2,
        [VMEM] * (1 + cols_x + 2 * ITERS * cols_x),
        joint, *rhs, *(a for v in vs for a in v), *(a for w in ws for a in w),
        flops=24 * ITERS * count * count * number * layers,
        out_specs=[HBM, HBM],
        scratch=[
            pltpu.VMEM(by_row, jnp.float32),
            pltpu.VMEM(by_row, jnp.float32),
            pltpu.SemaphoreType.DMA((2 * cols_x,)),
        ],
    )
    return tuple(outs)


def solution(mesh):
    in_specs = (
        P(None, "wide", "narrow", None),
        P(),
        P("wide", "narrow"),
        P("wide", "narrow", None),
        P("wide", "narrow", None),
        P("wide", "narrow", None, None, None),
    )
    out_specs = (P(None, "wide", "narrow", None), P(None, "wide", "narrow", None))
    return jax.shard_map(
        on_device, mesh=mesh, in_specs=in_specs, out_specs=out_specs, check_vma=False
    )
```

```python
import functools

import jax
import jax.numpy as jnp
import numpy as np
from jax import lax
from jax.experimental import pallas as pl
from jax.experimental.pallas import tpu as pltpu
from jax.sharding import PartitionSpec as P

ITERS = 3
WELL_RATE = 4.0
VMEM_BYTES = 24 * 1024 * 1024
VMEM = pl.BlockSpec(memory_space=pltpu.VMEM)
HBM = pl.BlockSpec(memory_space=pltpu.HBM)
SCALE = 64.0
AHEAD = 6


def call(kernel, out_shape, in_specs, *args, flops=0, out_specs=None, scratch=()):
    shapes = [
        s if isinstance(s, jax.ShapeDtypeStruct) else jax.ShapeDtypeStruct(s, jnp.float32)
        for s in out_shape
    ]
    size = sum(a.size * a.dtype.itemsize for a in args) + sum(s.size * 4 for s in shapes)
    out = pl.pallas_call(
        kernel,
        out_shape=shapes,
        in_specs=in_specs,
        out_specs=out_specs or [VMEM] * len(shapes),
        scratch_shapes=list(scratch),
        compiler_params=pltpu.CompilerParams(vmem_limit_bytes=VMEM_BYTES),
        cost_estimate=pl.CostEstimate(flops=flops, bytes_accessed=size, transcendentals=0),
    )(*args)
    return list(out)


def split(value):
    high = value.astype(jnp.bfloat16)
    return high, (value - high.astype(jnp.float32)).astype(jnp.bfloat16)


def apply_blocks(value, blocks_ref, col):
    count, layers = value.shape
    size = blocks_ref.shape[-1]
    number = layers // size
    terms = split(value)
    left = jnp.concatenate(
        [term[:, b * size : (b + 1) * size] for b in range(number) for term in terms], axis=0
    )
    right = jnp.concatenate([blocks_ref[col, b] for b in range(number)], axis=1)
    out = jnp.dot(left, right, preferred_element_type=jnp.float32)
    parts = []
    for b in range(number):
        piece = out[2 * b * count : 2 * (b + 1) * count, b * size : (b + 1) * size]
        parts.append(piece[:count] + piece[count:])
    return jnp.concatenate(parts, axis=1)


AXES = ("narrow", "wide")


def oriented(row, cols_x):
    odd = lax.rem(lax.axis_index("wide"), 2)
    return row + odd * (cols_x - 1 - 2 * row)


def partnered(slot):
    axis = AXES[slot // 2]
    place = lax.axis_index(axis)
    odd = lax.rem(place + slot, 2)
    partner = place + 1 - 2 * odd
    inside = jnp.logical_and(partner >= 0, partner < lax.axis_size(axis))
    return inside.astype(jnp.float32)


def write_edges(v_refs, coef_ref, edges):
    count = v_refs[0].shape[1]
    cols_y = v_refs[0].shape[0]
    odd = lax.rem(lax.axis_index("narrow"), 2)
    for ref, at_low in zip(edges, (odd, 1 - odd)):
        y = (1 - at_low) * (cols_y - 1)
        for row, v_ref in enumerate(v_refs):
            ref[row * count : (row + 1) * count, :] = v_ref[y]
            if coef_ref is not None:
                place = len(v_refs) * count + row
                ref[place : place + 1, :] = coef_ref[pl.ds(row * cols_y + y, 1), :]


def write_side(row, v_ref, coef_ref, edge):
    cols_y, count, _ = v_ref.shape
    for y in range(cols_y):
        edge[y * count : (y + 1) * count, :] = v_ref[y]
    edge[cols_y * count :, :] = coef_ref[row * cols_y : (row + 1) * cols_y, :]


def start_kernel(
    wells_hbm, active_hbm, sources_hbm, perm_hbm, storage_hbm, blocks_hbm, *refs
):
    cols_x, cols_y = active_hbm.shape
    r_refs, v_refs, refs = refs[:cols_x], refs[cols_x : 2 * cols_x], refs[2 * cols_x :]
    coef_ref, diag_ref, blocks_ref, edge_0, edge_1, edge_2, edge_3 = refs[:7]
    wells_ref, active_ref, sources_ref, perm_ref, storage_ref, small_sem, big_sem, block_sem = refs[7:]
    _, count, layers = r_refs[0].shape
    small = [
        pltpu.make_async_copy(source, target, small_sem.at[i])
        for i, (source, target) in enumerate(
            (
                (wells_hbm, wells_ref),
                (active_hbm, active_ref),
                (perm_hbm, perm_ref),
                (storage_hbm, storage_ref),
            )
        )
    ]
    sources, blocks = [], []
    for row in range(cols_x):
        x = oriented(row, cols_x)
        sources.append(
            pltpu.make_async_copy(sources_hbm.at[:, x], sources_ref.at[row], big_sem.at[row])
        )
        blocks.append(
            pltpu.make_async_copy(
                blocks_hbm.at[pl.ds(x * cols_y, cols_y)],
                blocks_ref.at[pl.ds(row * cols_y, cols_y)],
                block_sem.at[row],
            )
        )
    for copy in small:
        copy.start()
    for pair in zip(sources, blocks):
        for copy in pair:
            copy.start()
    for copy in small:
        copy.wait()
    place = lax.broadcasted_iota(jnp.int32, (count, layers), 0)
    wells = jnp.zeros((count, layers), jnp.int32)
    for k in range(count):
        wells = jnp.where(place == k, wells_ref[k], wells)
    grid_y = cols_y * lax.axis_size("narrow")
    first_x, first_y = lax.axis_index("wide") * cols_x, lax.axis_index("narrow") * cols_y
    for row in range(cols_x):
        x = oriented(row, cols_x)
        for y in range(cols_y):
            col = row * cols_y + y
            active = active_ref[x, y].astype(jnp.float32)
            perm, storage = perm_ref[x, y : y + 1, :], storage_ref[x, y : y + 1, :]
            coef_ref[col : col + 1, :] = active * perm
            diag_ref[col : col + 1, :] = active * storage + (1.0 - active)
    for row in range(cols_x):
        sources[row].wait()
        across = jnp.transpose(sources_ref[row], (1, 0, 2))
        blocks[row].wait()
        for y in range(cols_y):
            column_id = (first_x + oriented(row, cols_x)) * grid_y + first_y + y
            r = across[y] + jnp.where(wells == column_id, WELL_RATE, 0.0)
            r_refs[row][y] = r
            v_refs[row][y] = apply_blocks(r, blocks_ref, row * cols_y + y)
    write_side(0, v_refs[0], coef_ref, edge_3)
    write_side(cols_x - 1, v_refs[-1], coef_ref, edge_2)
    write_edges(v_refs, coef_ref, (edge_0, edge_1))


def received(got, got_coefs, slot, i, number, count):
    place = number * count + i
    value = got[slot][i * count : (i + 1) * count, :]
    return value, got_coefs[slot][place : place + 1, :] * partnered(slot)


def operate(v_refs, coef_ref, diag_ref, got, got_coefs, row, y):
    cols_x = len(v_refs)
    cols_y, count, layers = v_refs[row].shape
    col = row * cols_y + y
    center = v_refs[row][y]
    coef = coef_ref[col : col + 1, :]
    lane = lax.broadcasted_iota(jnp.int32, (1, layers), 1)
    upper_coef = jnp.where(lane == layers - 1, 0.0, pltpu.roll(coef, layers - 1, 1))
    lower_coef = jnp.where(lane == 0, 0.0, pltpu.roll(coef, 1, 1))
    total = upper_coef * (center - pltpu.roll(center, layers - 1, 1))
    total = total + lower_coef * (center - pltpu.roll(center, 1, 1))
    for step_row, step_y in ((1, 0), (-1, 0), (0, 1), (0, -1)):
        other, ny = row + step_row, y + step_y
        if 0 <= ny < cols_y and 0 <= other < cols_x:
            place = other * cols_y + ny
            value, other_coef = v_refs[other][ny], coef_ref[place : place + 1, :]
        elif step_row:
            slot = 3 if step_row < 0 else 2
            value, other_coef = received(got, got_coefs, slot, y, cols_y, count)
        else:
            odd = lax.rem(lax.axis_index("narrow"), 2) == 1
            first, c_first = received(got, got_coefs, 0, row, cols_x, count)
            second, c_second = received(got, got_coefs, 1, row, cols_x, count)
            low = step_y < 0
            value = jnp.where(odd == low, first, second)
            other_coef = jnp.where(odd == low, c_first, c_second)
        total = total + other_coef * (center - value)
    return (diag_ref[col : col + 1, :] * center + coef * total) * (1.0 / SCALE)


def row_kernel(cols_x, rows, slots, after, *refs):
    v_refs, (coef_ref, diag_ref), refs = refs[:cols_x], refs[cols_x : cols_x + 2], refs[cols_x + 2 :]
    number = len(slots)
    got, got_coefs = dict(zip(slots, refs)), dict(zip(slots, refs[number:]))
    blocks_ref, refs = refs[2 * number], refs[2 * number + 1 + after :]
    others = cols_x - len(rows) if rows[0] == 0 else 0
    done, refs = refs[:others], refs[others:]
    w_refs, next_refs, edges = refs[: len(rows)], refs[len(rows) : 2 * len(rows)], refs[2 * len(rows) :]
    cols_y = v_refs[0].shape[0]
    for row, w_ref, next_ref in zip(rows, w_refs, next_refs):
        for y in range(cols_y):
            w = operate(v_refs, coef_ref, diag_ref, got, got_coefs, row, y)
            w_ref[y] = w
            next_ref[y] = apply_blocks(w, blocks_ref, row * cols_y + y)
    if edges:
        write_edges((*next_refs, *done), None, edges)


def share_size(matrices, count):
    return (matrices * (count + 1) + 1) // 2


def lanes_of(used):
    return -(-used // 64) * 64


def last_kernel(cols_x, rows, slots, grams, *refs):
    v_refs, (coef_ref, diag_ref), refs = refs[:cols_x], refs[cols_x : cols_x + 2], refs[cols_x + 2 :]
    number = len(slots)
    got, got_coefs = dict(zip(slots, refs)), dict(zip(slots, refs[number:]))
    refs = refs[2 * number :]
    gram_refs, w_refs, out_ref = refs[:grams], refs[grams:-1], refs[-1]
    cols_y, count, _ = v_refs[0].shape
    total = jnp.zeros((2 * count, 2 * count), jnp.float32)
    for ref in gram_refs[2:]:
        total = total + ref[...]
    for row, w_ref in zip(rows, w_refs):
        for y in range(cols_y):
            w = operate(v_refs, coef_ref, diag_ref, got, got_coefs, row, y)
            w_ref[y] = w
            total = total + split_gram([v_refs[row][y]], w)
    if rows[0] != 0:
        out_ref[...] = total
        return
    size = share_size(2 * ITERS - 1, count)
    last = fold_square(fold(total))
    used = size + last.shape[1]
    rest = jnp.zeros((count // 2, lanes_of(used) - used), jnp.float32)
    early = (gram_refs[0][...] + gram_refs[1][...])[:, :size]
    packed = jnp.concatenate([early, last, rest], axis=1)
    middle = count // 4
    packed = jnp.concatenate(
        [packed[:middle], packed[middle:]], axis=1
    )
    for peer in range(out_ref.shape[0]):
        out_ref[peer] = packed


def split_gram(lefts, right):
    return lax.dot_general(
        jnp.concatenate([term for left in lefts for term in split(left)], axis=0),
        jnp.concatenate(split(right), axis=0),
        (((1,), (1,)), ((), ())),
        preferred_element_type=jnp.float32,
    )


def fold(total):
    count = total.shape[0] // 2
    total = total[:count] + total[count:]
    total = total[:, :count] + total[:, count:]
    return 0.5 * (total + total.T)


def grams_of(cols_x, groups, arrays):
    cols_y, count, _ = arrays[0].shape
    squares = []
    for lefts, right in groups:
        total = jnp.zeros((2 * count * len(lefts), 2 * count), jnp.float32)
        for row in range(cols_x):
            for y in range(cols_y):
                total = total + split_gram(
                    [arrays[left * cols_x + row][y] for left in lefts],
                    arrays[right * cols_x + row][y],
                )
        squares += [fold(total[2 * count * i : 2 * count * (i + 1)]) for i in range(len(lefts))]
    return squares


def gram_kernel(cols_x, groups, *refs):
    refs[-1][...] = jnp.concatenate(grams_of(cols_x, groups, refs[:-1]), axis=1)


def fold_square(square):
    half = square.shape[0] // 2
    bottom = jnp.concatenate([square[half:], jnp.zeros((half, 1), jnp.float32)], axis=1)
    top = jnp.concatenate(
        [jnp.zeros((half, half + 1), jnp.float32), square[:half, :half]], axis=1
    )
    row = lax.broadcasted_iota(jnp.int32, bottom.shape, 0)
    lane = lax.broadcasted_iota(jnp.int32, bottom.shape, 1)
    return jnp.where(lane <= half + row, bottom, top)


def unfold_squares(folded):
    half = folded.shape[0]
    row = lax.broadcasted_iota(jnp.int32, (half, half), 0)
    lane = lax.broadcasted_iota(jnp.int32, (half, half), 1)
    diagonal = jnp.where(row == lane, 0.5, 1.0)
    width = 2 * half + 1
    parts = []
    for i in range(folded.shape[1] // width):
        one = folded[:, i * width : (i + 1) * width]
        upper = jnp.where(row <= lane, one[:, half + 1 :] * diagonal, 0.0)
        lower = jnp.where(row >= lane, one[:, half : 2 * half] * diagonal, 0.0)
        parts.append(
            jnp.concatenate(
                [
                    jnp.concatenate([upper, jnp.zeros_like(upper)], axis=1),
                    jnp.concatenate([one[:, :half], lower], axis=1),
                ],
                axis=0,
            )
        )
    turned = jnp.concatenate(parts, axis=1).T
    return [
        part + turned[2 * half * i : 2 * half * (i + 1)] for i, part in enumerate(parts)
    ]


def share(folded, axis_odd):
    lanes = folded.shape[1]
    size = (lanes + 1) // 2
    return jnp.where(axis_odd, folded[:, lanes - size :], folded[:, :size])


def halves_kernel(cols_x, groups, *refs):
    arrays, early_refs, (send_ref, keep_ref) = refs[:-3], refs[-3:-2], refs[-2:]
    count = arrays[0].shape[1]
    squares = [
        ref[:, i * count : (i + 1) * count]
        for ref in early_refs
        for i in range(ref.shape[1] // count)
    ]
    squares += grams_of(cols_x, groups, arrays)
    folded = jnp.concatenate([fold_square(square) for square in squares], axis=1)
    odd = lax.rem(lax.axis_index("wide"), 2) == 1
    for ref, mine in ((send_ref, jnp.logical_not(odd)), (keep_ref, odd)):
        half = share(folded, mine)
        rest = jnp.zeros((half.shape[0], ref.shape[1] - half.shape[1]), jnp.float32)
        ref[...] = jnp.concatenate([half, rest], axis=1)


def solve_spd(matrix, target):
    size, width = matrix.shape[0], matrix.shape[1] + target.shape[1]
    lanes = 128
    work = jnp.concatenate(
        [matrix, target, jnp.zeros((size, lanes - width), jnp.float32)], axis=1
    )
    row = lax.broadcasted_iota(jnp.int32, (size, lanes), 0)

    def spread(p):
        return jnp.broadcast_to(work[:, p : p + 1], (size, lanes))

    ahead = {p: spread(p) for p in range(AHEAD)}
    inverses = jnp.zeros((size, lanes), jnp.float32)
    for p in range(size):
        column = ahead.pop(p)
        if p + AHEAD < size:
            ahead[p + AHEAD] = spread(p + AHEAD)
        inverse = 1.0 / column[p : p + 1, :]
        inverses = jnp.where(row == p, inverse, inverses)
        factor = jnp.where(row == p, 0.0, column)

        def eliminate(value):
            return value - factor * jnp.broadcast_to(value[p : p + 1, :] * inverse, value.shape)

        ahead = {q: eliminate(value) for q, value in ahead.items()}
        work = eliminate(work)
    return work[:, size:width] * inverses[:, size:width]


def finish_kernel(cols_x, blocks, sums_ref, *refs):
    r_refs, refs = refs[:cols_x], refs[cols_x:]
    v_refs, w_refs, refs = refs[: blocks * cols_x], refs[blocks * cols_x : 2 * blocks * cols_x], refs[2 * blocks * cols_x :]
    x_hbm, out_hbm, x_ref, out_ref, sem = refs
    cols_y = r_refs[0].shape[0]
    count = r_refs[0].shape[1]
    sums = []
    for parity in range(2):
        total = sums_ref[parity]
        for peer in range(parity + 2, sums_ref.shape[0], 2):
            total = total + sums_ref[peer]
        middle = total.shape[1] // 2
        sums.append(jnp.concatenate([total[:, :middle], total[:, middle:]], axis=0))
    even, odd = sums
    size, width = share_size(2 * blocks - 1, count), count + 1
    early = (2 * blocks - 1) * width
    moments = unfold_squares(
        jnp.concatenate(
            [
                even[:, :size],
                odd[:, 2 * size - early : size],
                even[:, size : size + width] + odd[:, size : size + width],
            ],
            axis=1,
        )
    )
    matrix = jnp.concatenate(
        [
            jnp.concatenate([moments[1 + i + j] for j in range(blocks)], axis=1)
            for i in range(blocks)
        ],
        axis=0,
    )
    target = jnp.concatenate(moments[:blocks], axis=0)
    coefs = solve_spd(matrix, target).T
    high = coefs.astype(jnp.bfloat16)
    middle, low = split(coefs - high.astype(jnp.float32))
    left = jnp.concatenate([high, high, middle, middle, low], axis=1)

    def combine(values, row, y):
        highs, lows = zip(*(split(values[j * cols_x + row][y]) for j in range(blocks)))
        right = jnp.concatenate(highs + lows + highs + lows + highs, axis=0)
        return jnp.dot(left, right, preferred_element_type=jnp.float32)

    copies = []

    def send(columns, ref, hbm, row):
        ref[row] = jnp.transpose(jnp.stack(columns), (1, 0, 2))
        target = hbm.at[:, oriented(row, cols_x)]
        copies.append(pltpu.make_async_copy(ref.at[row], target, sem.at[len(copies)]))
        copies[-1].start()

    for row in range(cols_x):
        send([r_refs[row][y] - combine(w_refs, row, y) for y in range(cols_y)], out_ref, out_hbm, row)
        send([combine(v_refs, row, y) * (1.0 / SCALE) for y in range(cols_y)], x_ref, x_hbm, row)
    for copy in copies:
        copy.wait()


def pairing(sizes, axis, phase):
    transfers = []
    for place in np.ndindex(*sizes):
        partner = list(place)
        partner[axis] += 1 if place[axis] % 2 == phase else -1
        if not 0 <= partner[axis] < sizes[axis]:
            partner = list(place)
            partner[1 - axis] ^= 1
            if partner[1 - axis] >= sizes[1 - axis]:
                continue
        transfers.append(tuple(int(np.ravel_multi_index(p, sizes)) for p in (place, partner)))
    return transfers


def exchange(slot, edge):
    sizes = tuple(lax.axis_size(axis) for axis in AXES)
    return lax.ppermute(edge, AXES, pairing(sizes, slot // 2, slot % 2))


def on_device(sources, well_columns, column_active, perm_root, storage_term, inverse_blocks):
    count, cols_x, cols_y, layers = sources.shape
    number = cols_x * cols_y
    devices = lax.axis_size("wide") * lax.axis_size("narrow")
    blocks = inverse_blocks.reshape((number,) + inverse_blocks.shape[2:])
    state, rows = (cols_y, count, layers), (number, layers)
    flat = (cols_y * count, layers)
    apply_flops = 4 * count * number * layers * inverse_blocks.shape[-1]
    gram_flops = 8 * count * count * number * layers

    ends = (cols_x * (count + 1), layers)
    side = (cols_y * (count + 1), layers)
    by_row = (cols_x, count, cols_y, layers)
    out = call(
        start_kernel,
        [state] * (2 * cols_x)
        + [rows, rows, jax.ShapeDtypeStruct(blocks.shape, blocks.dtype), ends, ends, side, side],
        [HBM] * 6,
        *(
            pltpu.with_memory_space_constraint(a, pltpu.HBM)
            for a in (well_columns, column_active, sources, perm_root, storage_term, blocks)
        ),
        flops=apply_flops,
        scratch=[
            pltpu.SMEM(well_columns.shape, jnp.int32),
            pltpu.SMEM(column_active.shape, jnp.int32),
            pltpu.VMEM(by_row, jnp.float32),
            pltpu.VMEM(perm_root.shape, jnp.float32),
            pltpu.VMEM(storage_term.shape, jnp.float32),
            pltpu.SemaphoreType.DMA((4,)),
            pltpu.SemaphoreType.DMA((cols_x,)),
            pltpu.SemaphoreType.DMA((cols_x,)),
        ],
    )
    rhs, v = out[:cols_x], out[cols_x : 2 * cols_x]
    coef, diag_term, blocks, *edges = out[2 * cols_x :]
    got_coefs = got = [exchange(slot, edge) for slot, edge in enumerate(edges)]
    vs, ws, grams = [v], [], []
    later_ends = (cols_x * count, layers)

    if cols_x > 1:
        shares = [(tuple(range(1, cols_x)), (0, 1, 2)), ((0,), (0, 1, 3))]
    else:
        shares = [((0,), (0, 1, 2, 3))]

    def halo(slots):
        return [*(got[i] for i in slots), *(got_coefs[i] for i in slots)]

    for j in range(1, ITERS):
        w, v = [], []
        for rows, slots in shares:
            ahead = [] if v else grams
            operands = [*vs[-1], coef, diag_term, *halo(slots), blocks, *ahead, *v]
            out = call(
                functools.partial(row_kernel, cols_x, rows, slots, len(ahead)),
                [state] * (2 * len(rows))
                + ([later_ends] * 2 if rows[0] == 0 else []),
                [VMEM] * len(operands),
                *operands,
                flops=apply_flops // len(shares),
            )
            w = out[: len(rows)] + w
            v = out[len(rows) : 2 * len(rows)] + v
            edges = out[2 * len(rows) :]
        edges += [v[-1].reshape(flat), v[0].reshape(flat)]
        got = [exchange(slot, edge) for slot, edge in enumerate(edges)]
        vs.append(v)
        ws.append(w)
        arrays = vs[-2] + v + w + (rhs if j == 1 else [])
        groups = ([((0,), 3)] if j == 1 else []) + [((0, 1), 2)]
        number_of = len(groups) + 1
        if j < ITERS - 1:
            grams += call(
                functools.partial(gram_kernel, cols_x, groups),
                [(count, number_of * count)],
                [VMEM] * len(arrays),
                *arrays,
                flops=number_of * gram_flops,
            )
        else:
            send, keep = call(
                functools.partial(halves_kernel, cols_x, groups),
                [(count // 2, 128)] * 2,
                [VMEM] * (len(arrays) + 1),
                *arrays, *grams,
                flops=number_of * gram_flops,
            )
            grams = [keep, exchange(2, send)]
    lanes = lanes_of(share_size(2 * ITERS - 1, count) + count + 1)
    w, totals = [], []
    for rows, slots in shares:
        first = [] if rows[0] else [*grams, *totals]
        operands = [*vs[-1], coef, diag_term, *halo(slots), *first]
        out = call(
            functools.partial(last_kernel, cols_x, rows, slots, len(first)),
            [state] * len(rows)
            + [(2 * count, 2 * count) if rows[0] else (devices, count // 4, 2 * lanes)],
            [VMEM] * len(operands),
            *operands,
            flops=gram_flops // len(shares),
        )
        w = out[:-1] + w
        totals.append(out[-1])
    joint = totals[-1]
    ws.append(w)
    joint = lax.all_to_all(joint, AXES, 0, 0)
    outs = call(
        functools.partial(finish_kernel, cols_x, ITERS),
        [sources.shape] * 2,
        [VMEM] * (1 + cols_x + 2 * ITERS * cols_x),
        joint, *rhs, *(a for v in vs for a in v), *(a for w in ws for a in w),
        flops=24 * ITERS * count * count * number * layers,
        out_specs=[HBM, HBM],
        scratch=[
            pltpu.VMEM(by_row, jnp.float32),
            pltpu.VMEM(by_row, jnp.float32),
            pltpu.SemaphoreType.DMA((2 * cols_x,)),
        ],
    )
    return tuple(outs)


def solution(mesh):
    in_specs = (
        P(None, "wide", "narrow", None),
        P(),
        P("wide", "narrow"),
        P("wide", "narrow", None),
        P("wide", "narrow", None),
        P("wide", "narrow", None, None, None),
    )
    out_specs = (P(None, "wide", "narrow", None), P(None, "wide", "narrow", None))
    return jax.shard_map(
        on_device, mesh=mesh, in_specs=in_specs, out_specs=out_specs, check_vma=False
    )
```

```python
import functools

import jax
import jax.numpy as jnp
import numpy as np
from jax import lax
from jax.experimental import pallas as pl
from jax.experimental.pallas import tpu as pltpu
from jax.sharding import PartitionSpec as P

ITERS = 3
WELL_RATE = 4.0
VMEM_BYTES = 24 * 1024 * 1024
VMEM = pl.BlockSpec(memory_space=pltpu.VMEM)
HBM = pl.BlockSpec(memory_space=pltpu.HBM)
SCALE = 64.0
AHEAD = 6


def call(kernel, out_shape, in_specs, *args, flops=0, out_specs=None, scratch=()):
    shapes = [
        s if isinstance(s, jax.ShapeDtypeStruct) else jax.ShapeDtypeStruct(s, jnp.float32)
        for s in out_shape
    ]
    size = sum(a.size * a.dtype.itemsize for a in args) + sum(s.size * 4 for s in shapes)
    out = pl.pallas_call(
        kernel,
        out_shape=shapes,
        in_specs=in_specs,
        out_specs=out_specs or [VMEM] * len(shapes),
        scratch_shapes=list(scratch),
        compiler_params=pltpu.CompilerParams(vmem_limit_bytes=VMEM_BYTES),
        cost_estimate=pl.CostEstimate(flops=flops, bytes_accessed=size, transcendentals=0),
    )(*args)
    return list(out)


def split(value):
    high = value.astype(jnp.bfloat16)
    return high, (value - high.astype(jnp.float32)).astype(jnp.bfloat16)


def apply_blocks(value, blocks_ref, col):
    count, layers = value.shape
    size = blocks_ref.shape[-1]
    number = layers // size
    terms = split(value)
    left = jnp.concatenate(
        [term[:, b * size : (b + 1) * size] for b in range(number) for term in terms], axis=0
    )
    right = jnp.concatenate([blocks_ref[col, b] for b in range(number)], axis=1)
    out = jnp.dot(left, right, preferred_element_type=jnp.float32)
    parts = []
    for b in range(number):
        piece = out[2 * b * count : 2 * (b + 1) * count, b * size : (b + 1) * size]
        parts.append(piece[:count] + piece[count:])
    return jnp.concatenate(parts, axis=1)


AXES = ("narrow", "wide")


def oriented(row, cols_x):
    odd = lax.rem(lax.axis_index("wide"), 2)
    return row + odd * (cols_x - 1 - 2 * row)


def partnered(slot):
    axis = AXES[slot // 2]
    place = lax.axis_index(axis)
    odd = lax.rem(place + slot, 2)
    partner = place + 1 - 2 * odd
    inside = jnp.logical_and(partner >= 0, partner < lax.axis_size(axis))
    return inside.astype(jnp.float32)


def write_edges(v_refs, coef_ref, edges):
    count = v_refs[0].shape[1]
    cols_y = v_refs[0].shape[0]
    odd = lax.rem(lax.axis_index("narrow"), 2)
    for ref, at_low in zip(edges, (odd, 1 - odd)):
        y = (1 - at_low) * (cols_y - 1)
        for row, v_ref in enumerate(v_refs):
            ref[row * count : (row + 1) * count, :] = v_ref[y]
            if coef_ref is not None:
                place = len(v_refs) * count + row
                ref[place : place + 1, :] = coef_ref[pl.ds(row * cols_y + y, 1), :]


def write_side(row, v_ref, coef_ref, edge):
    cols_y, count, _ = v_ref.shape
    for y in range(cols_y):
        edge[y * count : (y + 1) * count, :] = v_ref[y]
    if coef_ref is not None:
        edge[cols_y * count : cols_y * (count + 1), :] = coef_ref[
            row * cols_y : (row + 1) * cols_y, :
        ]


def start_kernel(
    wells_hbm, active_hbm, sources_hbm, perm_hbm, storage_hbm, blocks_hbm, *refs
):
    cols_x, cols_y = active_hbm.shape
    r_refs, v_refs, refs = refs[:cols_x], refs[cols_x : 2 * cols_x], refs[2 * cols_x :]
    coef_ref, diag_ref, blocks_ref, edge_0, edge_1, edge_2, edge_3 = refs[:7]
    wells_ref, active_ref, sources_ref, perm_ref, storage_ref, small_sem, big_sem, block_sem = refs[7:]
    _, count, layers = r_refs[0].shape
    small = [
        pltpu.make_async_copy(source, target, small_sem.at[i])
        for i, (source, target) in enumerate(
            (
                (wells_hbm, wells_ref),
                (active_hbm, active_ref),
                (perm_hbm, perm_ref),
                (storage_hbm, storage_ref),
            )
        )
    ]
    sources, blocks = [], []
    for row in range(cols_x):
        x = oriented(row, cols_x)
        sources.append(
            pltpu.make_async_copy(sources_hbm.at[:, x], sources_ref.at[row], big_sem.at[row])
        )
        blocks.append(
            pltpu.make_async_copy(
                blocks_hbm.at[pl.ds(x * cols_y, cols_y)],
                blocks_ref.at[pl.ds(row * cols_y, cols_y)],
                block_sem.at[row],
            )
        )
    for copy in (sources[0], blocks[0], *small, *sources[1:], *blocks[1:]):
        copy.start()
    for copy in small:
        copy.wait()
    place = lax.broadcasted_iota(jnp.int32, (count, layers), 0)
    wells = jnp.zeros((count, layers), jnp.int32)
    for k in range(count):
        wells = jnp.where(place == k, wells_ref[k], wells)
    grid_y = cols_y * lax.axis_size("narrow")
    first_x, first_y = lax.axis_index("wide") * cols_x, lax.axis_index("narrow") * cols_y
    for row in range(cols_x):
        x = oriented(row, cols_x)
        for y in range(cols_y):
            col = row * cols_y + y
            active = active_ref[x, y].astype(jnp.float32)
            perm, storage = perm_ref[x, y : y + 1, :], storage_ref[x, y : y + 1, :]
            coef_ref[col : col + 1, :] = active * perm
            diag_ref[col : col + 1, :] = active * storage + (1.0 - active)
    for row in range(cols_x):
        sources[row].wait()
        across = jnp.transpose(sources_ref[row], (1, 0, 2))
        blocks[row].wait()
        for y in range(cols_y):
            column_id = (first_x + oriented(row, cols_x)) * grid_y + first_y + y
            r = across[y] + jnp.where(wells == column_id, WELL_RATE, 0.0)
            r_refs[row][y] = r
            v_refs[row][y] = apply_blocks(r, blocks_ref, row * cols_y + y)
    write_side(0, v_refs[0], coef_ref, edge_3)
    write_side(cols_x - 1, v_refs[-1], coef_ref, edge_2)
    write_edges(v_refs, coef_ref, (edge_0, edge_1))


def received(got, got_coefs, slot, i, number, count):
    place = number * count + i
    value = got[slot][i * count : (i + 1) * count, :]
    return value, got_coefs[slot][place : place + 1, :] * partnered(slot)


def operate(v_refs, coef_ref, diag_ref, got, got_coefs, row, y):
    cols_x = len(v_refs)
    cols_y, count, layers = v_refs[row].shape
    col = row * cols_y + y
    center = v_refs[row][y]
    coef = coef_ref[col : col + 1, :]
    lane = lax.broadcasted_iota(jnp.int32, (1, layers), 1)
    upper_coef = jnp.where(lane == layers - 1, 0.0, pltpu.roll(coef, layers - 1, 1))
    lower_coef = jnp.where(lane == 0, 0.0, pltpu.roll(coef, 1, 1))
    total = upper_coef * (center - pltpu.roll(center, layers - 1, 1))
    total = total + lower_coef * (center - pltpu.roll(center, 1, 1))
    for step_row, step_y in ((1, 0), (-1, 0), (0, 1), (0, -1)):
        other, ny = row + step_row, y + step_y
        if 0 <= ny < cols_y and 0 <= other < cols_x:
            place = other * cols_y + ny
            value, other_coef = v_refs[other][ny], coef_ref[place : place + 1, :]
        elif step_row:
            slot = 3 if step_row < 0 else 2
            value, other_coef = received(got, got_coefs, slot, y, cols_y, count)
        else:
            odd = lax.rem(lax.axis_index("narrow"), 2) == 1
            first, c_first = received(got, got_coefs, 0, row, cols_x, count)
            second, c_second = received(got, got_coefs, 1, row, cols_x, count)
            low = step_y < 0
            value = jnp.where(odd == low, first, second)
            other_coef = jnp.where(odd == low, c_first, c_second)
        total = total + other_coef * (center - value)
    return (diag_ref[col : col + 1, :] * center + coef * total) * (1.0 / SCALE)


def row_kernel(cols_x, rows, slots, after, *refs):
    v_refs, (coef_ref, diag_ref), refs = refs[:cols_x], refs[cols_x : cols_x + 2], refs[cols_x + 2 :]
    number = len(slots)
    got, got_coefs = dict(zip(slots, refs)), dict(zip(slots, refs[number:]))
    blocks_ref, refs = refs[2 * number], refs[2 * number + 1 + after :]
    others = cols_x - len(rows) if rows[0] == 0 else 0
    done, refs = refs[:others], refs[others:]
    w_refs, next_refs, edges = refs[: len(rows)], refs[len(rows) : 2 * len(rows)], refs[2 * len(rows) :]
    cols_y = v_refs[0].shape[0]
    for row, w_ref, next_ref in zip(rows, w_refs, next_refs):
        for y in range(cols_y):
            w = operate(v_refs, coef_ref, diag_ref, got, got_coefs, row, y)
            w_ref[y] = w
            next_ref[y] = apply_blocks(w, blocks_ref, row * cols_y + y)
    if edges:
        write_edges((*next_refs, *done), None, edges[:2])
        write_side(0, next_refs[0], None, edges[2])


def share_size(matrices, count):
    return (matrices * (count + 1) + 1) // 2


def lanes_of(used):
    return -(-used // 64) * 64


def last_kernel(cols_x, rows, slots, grams, *refs):
    v_refs, (coef_ref, diag_ref), refs = refs[:cols_x], refs[cols_x : cols_x + 2], refs[cols_x + 2 :]
    number = len(slots)
    got, got_coefs = dict(zip(slots, refs)), dict(zip(slots, refs[number:]))
    refs = refs[2 * number :]
    gram_refs, w_refs, out_ref = refs[:grams], refs[grams:-1], refs[-1]
    cols_y, count, _ = v_refs[0].shape
    total = jnp.zeros((2 * count, 2 * count), jnp.float32)
    for ref in gram_refs[2:]:
        total = total + ref[...]
    for row, w_ref in zip(rows, w_refs):
        for y in range(cols_y):
            w = operate(v_refs, coef_ref, diag_ref, got, got_coefs, row, y)
            w_ref[y] = w
            total = total + split_gram([v_refs[row][y]], w)
    if rows[0] != 0:
        out_ref[...] = total
        return
    size = share_size(2 * ITERS - 1, count)
    last = fold_square(fold(total))
    used = size + last.shape[1]
    rest = jnp.zeros((count // 2, lanes_of(used) - used), jnp.float32)
    early = (gram_refs[0][...] + gram_refs[1][...])[:, :size]
    packed = jnp.concatenate([early, last, rest], axis=1)
    middle = count // 4
    packed = jnp.concatenate(
        [packed[:middle], packed[middle:]], axis=1
    )
    for peer in range(out_ref.shape[0]):
        out_ref[peer] = packed


def split_gram(lefts, right):
    return lax.dot_general(
        jnp.concatenate([term for left in lefts for term in split(left)], axis=0),
        jnp.concatenate(split(right), axis=0),
        (((1,), (1,)), ((), ())),
        preferred_element_type=jnp.float32,
    )


def fold(total):
    count = total.shape[0] // 2
    total = total[:count] + total[count:]
    total = total[:, :count] + total[:, count:]
    return 0.5 * (total + total.T)


def grams_of(cols_x, groups, arrays):
    cols_y, count, _ = arrays[0].shape
    squares = []
    for lefts, right in groups:
        total = jnp.zeros((2 * count * len(lefts), 2 * count), jnp.float32)
        for row in range(cols_x):
            for y in range(cols_y):
                total = total + split_gram(
                    [arrays[left * cols_x + row][y] for left in lefts],
                    arrays[right * cols_x + row][y],
                )
        squares += [fold(total[2 * count * i : 2 * count * (i + 1)]) for i in range(len(lefts))]
    return squares


def gram_kernel(cols_x, groups, *refs):
    refs[-1][...] = jnp.concatenate(grams_of(cols_x, groups, refs[:-1]), axis=1)


def fold_square(square):
    half = square.shape[0] // 2
    bottom = jnp.concatenate([square[half:], jnp.zeros((half, 1), jnp.float32)], axis=1)
    top = jnp.concatenate(
        [jnp.zeros((half, half + 1), jnp.float32), square[:half, :half]], axis=1
    )
    row = lax.broadcasted_iota(jnp.int32, bottom.shape, 0)
    lane = lax.broadcasted_iota(jnp.int32, bottom.shape, 1)
    return jnp.where(lane <= half + row, bottom, top)


def unfold_squares(folded):
    half = folded.shape[0]
    row = lax.broadcasted_iota(jnp.int32, (half, half), 0)
    lane = lax.broadcasted_iota(jnp.int32, (half, half), 1)
    diagonal = jnp.where(row == lane, 0.5, 1.0)
    across = lax.broadcasted_iota(jnp.int32, (half, 2 * half), 1)
    end = half + lax.broadcasted_iota(jnp.int32, (half, 2 * half), 0)
    below = jnp.where(across < end, 1.0, jnp.where(across == end, 0.5, 0.0))
    width = 2 * half + 1
    parts = []
    for i in range(folded.shape[1] // width):
        one = folded[:, i * width : (i + 1) * width]
        upper = jnp.where(row <= lane, one[:, half + 1 :] * diagonal, 0.0)
        lower = jnp.where(across <= end, one[:, : 2 * half] * below, 0.0)
        upper = jnp.concatenate([upper, jnp.zeros_like(upper)], axis=1)
        parts.append(jnp.concatenate([upper, lower], axis=0))
    turned = jnp.concatenate(parts, axis=1).T
    return [
        part + turned[2 * half * i : 2 * half * (i + 1)] for i, part in enumerate(parts)
    ]


def share(folded, axis_odd):
    lanes = folded.shape[1]
    size = (lanes + 1) // 2
    return jnp.where(axis_odd, folded[:, lanes - size :], folded[:, :size])


def halves_kernel(cols_x, groups, *refs):
    arrays, early_refs, (send_ref, keep_ref) = refs[:-3], refs[-3:-2], refs[-2:]
    count = arrays[0].shape[1]
    squares = [
        ref[:, i * count : (i + 1) * count]
        for ref in early_refs
        for i in range(ref.shape[1] // count)
    ]
    squares += grams_of(cols_x, groups, arrays)
    folded = jnp.concatenate([fold_square(square) for square in squares], axis=1)
    odd = lax.rem(lax.axis_index("wide"), 2) == 1
    for ref, mine in ((send_ref, jnp.logical_not(odd)), (keep_ref, odd)):
        half = share(folded, mine)
        rest = jnp.zeros((half.shape[0], ref.shape[1] - half.shape[1]), jnp.float32)
        ref[...] = jnp.concatenate([half, rest], axis=1)


def solve_spd(matrix, target):
    size, width = matrix.shape[0], matrix.shape[1] + target.shape[1]
    lanes = 128
    work = jnp.concatenate(
        [matrix, target, jnp.zeros((size, lanes - width), jnp.float32)], axis=1
    )
    row = lax.broadcasted_iota(jnp.int32, (size, lanes), 0)

    def spread(p):
        return jnp.broadcast_to(work[:, p : p + 1], (size, lanes))

    ahead = {p: spread(p) for p in range(AHEAD)}
    inverses = jnp.zeros((size, lanes), jnp.float32)
    for p in range(size):
        column = ahead.pop(p)
        if p + AHEAD < size:
            ahead[p + AHEAD] = spread(p + AHEAD)
        inverse = 1.0 / column[p : p + 1, :]
        inverses = jnp.where(row == p, inverse, inverses)
        factor = jnp.where(row == p, 0.0, column)

        def eliminate(value):
            return value - factor * jnp.broadcast_to(value[p : p + 1, :] * inverse, value.shape)

        ahead = {q: eliminate(value) for q, value in ahead.items()}
        work = eliminate(work)
    return work[:, size:width] * inverses[:, size:width]


def finish_kernel(cols_x, blocks, sums_ref, *refs):
    r_refs, refs = refs[:cols_x], refs[cols_x:]
    v_refs, w_refs, refs = refs[: blocks * cols_x], refs[blocks * cols_x : 2 * blocks * cols_x], refs[2 * blocks * cols_x :]
    x_hbm, out_hbm, x_ref, out_ref, sem = refs
    cols_y = r_refs[0].shape[0]
    count = r_refs[0].shape[1]
    sums = []
    for parity in range(2):
        total = sums_ref[parity]
        for peer in range(parity + 2, sums_ref.shape[0], 2):
            total = total + sums_ref[peer]
        middle = total.shape[1] // 2
        sums.append(jnp.concatenate([total[:, :middle], total[:, middle:]], axis=0))
    even, odd = sums
    size, width = share_size(2 * blocks - 1, count), count + 1
    early = (2 * blocks - 1) * width
    moments = unfold_squares(
        jnp.concatenate(
            [
                even[:, :size],
                odd[:, 2 * size - early : size],
                even[:, size : size + width] + odd[:, size : size + width],
            ],
            axis=1,
        )
    )
    matrix = jnp.concatenate(
        [
            jnp.concatenate([moments[1 + i + j] for j in range(blocks)], axis=1)
            for i in range(blocks)
        ],
        axis=0,
    )
    target = jnp.concatenate(moments[:blocks], axis=0)
    coefs = solve_spd(matrix, target).T
    high = coefs.astype(jnp.bfloat16)
    middle, low = split(coefs - high.astype(jnp.float32))
    left = jnp.concatenate([high, high, middle, middle, low], axis=1)

    def combine(values, row, y):
        highs, lows = zip(*(split(values[j * cols_x + row][y]) for j in range(blocks)))
        right = jnp.concatenate(highs + lows + highs + lows + highs, axis=0)
        return jnp.dot(left, right, preferred_element_type=jnp.float32)

    copies = []

    def send(columns, ref, hbm, row):
        ref[row] = jnp.transpose(jnp.stack(columns), (1, 0, 2))
        target = hbm.at[:, oriented(row, cols_x)]
        copies.append(pltpu.make_async_copy(ref.at[row], target, sem.at[len(copies)]))
        copies[-1].start()

    for row in range(cols_x):
        send([r_refs[row][y] - combine(w_refs, row, y) for y in range(cols_y)], out_ref, out_hbm, row)
        send([combine(v_refs, row, y) * (1.0 / SCALE) for y in range(cols_y)], x_ref, x_hbm, row)
    for copy in copies:
        copy.wait()


def pairing(sizes, axis, phase):
    transfers = []
    for place in np.ndindex(*sizes):
        partner = list(place)
        partner[axis] += 1 if place[axis] % 2 == phase else -1
        if not 0 <= partner[axis] < sizes[axis]:
            partner = list(place)
            partner[1 - axis] ^= 1
            if partner[1 - axis] >= sizes[1 - axis]:
                continue
        transfers.append(tuple(int(np.ravel_multi_index(p, sizes)) for p in (place, partner)))
    return transfers


def exchange(slot, edge):
    sizes = tuple(lax.axis_size(axis) for axis in AXES)
    return lax.ppermute(edge, AXES, pairing(sizes, slot // 2, slot % 2))


def on_device(sources, well_columns, column_active, perm_root, storage_term, inverse_blocks):
    count, cols_x, cols_y, layers = sources.shape
    number = cols_x * cols_y
    devices = lax.axis_size("wide") * lax.axis_size("narrow")
    blocks = inverse_blocks.reshape((number,) + inverse_blocks.shape[2:])
    state, rows = (cols_y, count, layers), (number, layers)
    flat = (cols_y * count, layers)
    apply_flops = 4 * count * number * layers * inverse_blocks.shape[-1]
    gram_flops = 8 * count * count * number * layers

    ends = (cols_x * (count + 1), layers)
    side = (cols_y * (count + 1), layers)
    by_row = (cols_x, count, cols_y, layers)
    out = call(
        start_kernel,
        [state] * (2 * cols_x)
        + [rows, rows, jax.ShapeDtypeStruct(blocks.shape, blocks.dtype), ends, ends, side, (side[0] + 8, layers)],
        [HBM] * 6,
        *(
            pltpu.with_memory_space_constraint(a, pltpu.HBM)
            for a in (well_columns, column_active, sources, perm_root, storage_term, blocks)
        ),
        flops=apply_flops,
        scratch=[
            pltpu.SMEM(well_columns.shape, jnp.int32),
            pltpu.SMEM(column_active.shape, jnp.int32),
            pltpu.VMEM(by_row, jnp.float32),
            pltpu.VMEM(perm_root.shape, jnp.float32),
            pltpu.VMEM(storage_term.shape, jnp.float32),
            pltpu.SemaphoreType.DMA((4,)),
            pltpu.SemaphoreType.DMA((cols_x,)),
            pltpu.SemaphoreType.DMA((cols_x,)),
        ],
    )
    rhs, v = out[:cols_x], out[cols_x : 2 * cols_x]
    coef, diag_term, blocks, *edges = out[2 * cols_x :]
    got_coefs = got = [exchange(slot, edge) for slot, edge in enumerate(edges)]
    vs, ws, grams = [v], [], []
    later_ends, later_side = (cols_x * count, layers), (cols_y * count + 8, layers)

    if cols_x > 1:
        shares = [(tuple(range(1, cols_x)), (0, 1, 2)), ((0,), (0, 1, 3))]
    else:
        shares = [((0,), (0, 1, 2, 3))]

    def halo(slots):
        return [*(got[i] for i in slots), *(got_coefs[i] for i in slots)]

    for j in range(1, ITERS):
        w, v = [], []
        for rows, slots in shares:
            ahead = [] if v else grams
            operands = [*vs[-1], coef, diag_term, *halo(slots), blocks, *ahead, *v]
            out = call(
                functools.partial(row_kernel, cols_x, rows, slots, len(ahead)),
                [state] * (2 * len(rows))
                + ([later_ends] * 2 + [later_side] if rows[0] == 0 else []),
                [VMEM] * len(operands),
                *operands,
                flops=apply_flops // len(shares),
            )
            w = out[: len(rows)] + w
            v = out[len(rows) : 2 * len(rows)] + v
            edges = out[2 * len(rows) :]
        edges.insert(2, v[-1].reshape(flat))
        got = [exchange(slot, edge) for slot, edge in enumerate(edges)]
        vs.append(v)
        ws.append(w)
        arrays = vs[-2] + v + w + (rhs if j == 1 else [])
        groups = ([((0,), 3)] if j == 1 else []) + [((0, 1), 2)]
        number_of = len(groups) + 1
        if j < ITERS - 1:
            grams += call(
                functools.partial(gram_kernel, cols_x, groups),
                [(count, number_of * count)],
                [VMEM] * len(arrays),
                *arrays,
                flops=number_of * gram_flops,
            )
        else:
            send, keep = call(
                functools.partial(halves_kernel, cols_x, groups),
                [(count // 2, 128)] * 2,
                [VMEM] * (len(arrays) + 1),
                *arrays, *grams,
                flops=number_of * gram_flops,
            )
            grams = [keep, exchange(2, send)]
    lanes = lanes_of(share_size(2 * ITERS - 1, count) + count + 1)
    w, totals = [], []
    for rows, slots in shares:
        first = [] if rows[0] else [*grams, *totals]
        operands = [*vs[-1], coef, diag_term, *halo(slots), *first]
        out = call(
            functools.partial(last_kernel, cols_x, rows, slots, len(first)),
            [state] * len(rows)
            + [(2 * count, 2 * count) if rows[0] else (devices, count // 4, 2 * lanes)],
            [VMEM] * len(operands),
            *operands,
            flops=gram_flops // len(shares),
        )
        w = out[:-1] + w
        totals.append(out[-1])
    joint = totals[-1]
    ws.append(w)
    joint = lax.all_to_all(joint, AXES, 0, 0)
    outs = call(
        functools.partial(finish_kernel, cols_x, ITERS),
        [sources.shape] * 2,
        [VMEM] * (1 + cols_x + 2 * ITERS * cols_x),
        joint, *rhs, *(a for v in vs for a in v), *(a for w in ws for a in w),
        flops=24 * ITERS * count * count * number * layers,
        out_specs=[HBM, HBM],
        scratch=[
            pltpu.VMEM(by_row, jnp.float32),
            pltpu.VMEM(by_row, jnp.float32),
            pltpu.SemaphoreType.DMA((2 * cols_x,)),
        ],
    )
    return tuple(outs)


def solution(mesh):
    in_specs = (
        P(None, "wide", "narrow", None),
        P(),
        P("wide", "narrow"),
        P("wide", "narrow", None),
        P("wide", "narrow", None),
        P("wide", "narrow", None, None, None),
    )
    out_specs = (P(None, "wide", "narrow", None), P(None, "wide", "narrow", None))
    return jax.shard_map(
        on_device, mesh=mesh, in_specs=in_specs, out_specs=out_specs, check_vma=False
    )
```

```python
import functools

import jax
import jax.numpy as jnp
import numpy as np
from jax import lax
from jax.experimental import pallas as pl
from jax.experimental.pallas import tpu as pltpu
from jax.sharding import PartitionSpec as P

ITERS = 3
WELL_RATE = 4.0
VMEM_BYTES = 24 * 1024 * 1024
VMEM = pl.BlockSpec(memory_space=pltpu.VMEM)
HBM = pl.BlockSpec(memory_space=pltpu.HBM)
SCALE = 64.0
AHEAD = 6


def call(kernel, out_shape, in_specs, *args, flops=0, out_specs=None, scratch=()):
    shapes = [
        s if isinstance(s, jax.ShapeDtypeStruct) else jax.ShapeDtypeStruct(s, jnp.float32)
        for s in out_shape
    ]
    size = sum(a.size * a.dtype.itemsize for a in args) + sum(s.size * 4 for s in shapes)
    out = pl.pallas_call(
        kernel,
        out_shape=shapes,
        in_specs=in_specs,
        out_specs=out_specs or [VMEM] * len(shapes),
        scratch_shapes=list(scratch),
        compiler_params=pltpu.CompilerParams(vmem_limit_bytes=VMEM_BYTES),
        cost_estimate=pl.CostEstimate(flops=flops, bytes_accessed=size, transcendentals=0),
    )(*args)
    return list(out)


def split(value):
    high = value.astype(jnp.bfloat16)
    return high, (value - high.astype(jnp.float32)).astype(jnp.bfloat16)


def apply_blocks(value, blocks_ref, col):
    count, layers = value.shape
    size = blocks_ref.shape[-1]
    number = layers // size
    terms = split(value)
    left = jnp.concatenate(
        [term[:, b * size : (b + 1) * size] for b in range(number) for term in terms], axis=0
    )
    right = jnp.concatenate([blocks_ref[col, b] for b in range(number)], axis=1)
    out = jnp.dot(left, right, preferred_element_type=jnp.float32)
    parts = []
    for b in range(number):
        piece = out[2 * b * count : 2 * (b + 1) * count, b * size : (b + 1) * size]
        parts.append(piece[:count] + piece[count:])
    return jnp.concatenate(parts, axis=1)


AXES = ("narrow", "wide")


def oriented(row, cols_x):
    odd = lax.rem(lax.axis_index("wide"), 2)
    return row + odd * (cols_x - 1 - 2 * row)


def partnered(slot):
    axis = AXES[slot // 2]
    place = lax.axis_index(axis)
    odd = lax.rem(place + slot, 2)
    partner = place + 1 - 2 * odd
    inside = jnp.logical_and(partner >= 0, partner < lax.axis_size(axis))
    return inside.astype(jnp.float32)


def write_edges(v_refs, coef_ref, edges):
    count = v_refs[0].shape[1]
    cols_y = v_refs[0].shape[0]
    odd = lax.rem(lax.axis_index("narrow"), 2)
    for ref, at_low in zip(edges, (odd, 1 - odd)):
        y = (1 - at_low) * (cols_y - 1)
        for row, v_ref in enumerate(v_refs):
            ref[row * count : (row + 1) * count, :] = v_ref[y]
            if coef_ref is not None:
                place = len(v_refs) * count + row
                ref[place : place + 1, :] = coef_ref[pl.ds(row * cols_y + y, 1), :]


def write_side(row, v_ref, coef_ref, edge):
    cols_y, count, _ = v_ref.shape
    for y in range(cols_y):
        edge[y * count : (y + 1) * count, :] = v_ref[y]
    if coef_ref is not None:
        edge[cols_y * count : cols_y * (count + 1), :] = coef_ref[
            row * cols_y : (row + 1) * cols_y, :
        ]


def start_kernel(
    wells_hbm, active_hbm, sources_hbm, perm_hbm, storage_hbm, blocks_hbm, *refs
):
    cols_x, cols_y = active_hbm.shape
    r_refs, v_refs, refs = refs[:cols_x], refs[cols_x : 2 * cols_x], refs[2 * cols_x :]
    coef_ref, diag_ref, blocks_ref, edge_0, edge_1, edge_2, edge_3 = refs[:7]
    wells_ref, active_ref, sources_ref, perm_ref, storage_ref, small_sem, big_sem, block_sem = refs[7:]
    _, count, layers = r_refs[0].shape
    small = [
        pltpu.make_async_copy(source, target, small_sem.at[i])
        for i, (source, target) in enumerate(
            (
                (wells_hbm, wells_ref),
                (active_hbm, active_ref),
                (perm_hbm, perm_ref),
                (storage_hbm, storage_ref),
            )
        )
    ]
    sources, blocks = [], []
    for row in range(cols_x):
        x = oriented(row, cols_x)
        sources.append(
            pltpu.make_async_copy(sources_hbm.at[:, x], sources_ref.at[row], big_sem.at[row])
        )
        blocks.append(
            pltpu.make_async_copy(
                blocks_hbm.at[pl.ds(x * cols_y, cols_y)],
                blocks_ref.at[pl.ds(row * cols_y, cols_y)],
                block_sem.at[row],
            )
        )
    for copy in (sources[0], blocks[0], *small, *sources[1:], *blocks[1:]):
        copy.start()
    for copy in small:
        copy.wait()
    place = lax.broadcasted_iota(jnp.int32, (count, layers), 0)
    wells = jnp.zeros((count, layers), jnp.int32)
    for k in range(count):
        wells = jnp.where(place == k, wells_ref[k], wells)
    grid_y = cols_y * lax.axis_size("narrow")
    first_x, first_y = lax.axis_index("wide") * cols_x, lax.axis_index("narrow") * cols_y
    for row in range(cols_x):
        x = oriented(row, cols_x)
        for y in range(cols_y):
            col = row * cols_y + y
            active = active_ref[x, y].astype(jnp.float32)
            perm, storage = perm_ref[x, y : y + 1, :], storage_ref[x, y : y + 1, :]
            coef_ref[col : col + 1, :] = active * perm
            diag_ref[col : col + 1, :] = active * storage + (1.0 - active)
    for row in range(cols_x):
        sources[row].wait()
        across = jnp.transpose(sources_ref[row], (1, 0, 2))
        blocks[row].wait()
        for y in range(cols_y):
            column_id = (first_x + oriented(row, cols_x)) * grid_y + first_y + y
            r = across[y] + jnp.where(wells == column_id, WELL_RATE, 0.0)
            r_refs[row][y] = r
            v_refs[row][y] = apply_blocks(r, blocks_ref, row * cols_y + y)
    write_side(0, v_refs[0], coef_ref, edge_3)
    write_side(cols_x - 1, v_refs[-1], coef_ref, edge_2)
    write_edges(v_refs, coef_ref, (edge_0, edge_1))


def received(got, got_coefs, slot, i, number, count):
    place = number * count + i
    value = got[slot][i * count : (i + 1) * count, :]
    return value, got_coefs[slot][place : place + 1, :] * partnered(slot)


def operate(v_refs, coef_ref, diag_ref, got, got_coefs, row, y):
    cols_x = len(v_refs)
    cols_y, count, layers = v_refs[row].shape
    col = row * cols_y + y
    center = v_refs[row][y]
    coef = coef_ref[col : col + 1, :]
    lane = lax.broadcasted_iota(jnp.int32, (1, layers), 1)
    upper_coef = jnp.where(lane == layers - 1, 0.0, pltpu.roll(coef, layers - 1, 1))
    lower_coef = jnp.where(lane == 0, 0.0, pltpu.roll(coef, 1, 1))
    total = upper_coef * (center - pltpu.roll(center, layers - 1, 1))
    total = total + lower_coef * (center - pltpu.roll(center, 1, 1))
    for step_row, step_y in ((1, 0), (-1, 0), (0, 1), (0, -1)):
        other, ny = row + step_row, y + step_y
        if 0 <= ny < cols_y and 0 <= other < cols_x:
            place = other * cols_y + ny
            value, other_coef = v_refs[other][ny], coef_ref[place : place + 1, :]
        elif step_row:
            slot = 3 if step_row < 0 else 2
            value, other_coef = received(got, got_coefs, slot, y, cols_y, count)
        else:
            odd = lax.rem(lax.axis_index("narrow"), 2) == 1
            first, c_first = received(got, got_coefs, 0, row, cols_x, count)
            second, c_second = received(got, got_coefs, 1, row, cols_x, count)
            low = step_y < 0
            value = jnp.where(odd == low, first, second)
            other_coef = jnp.where(odd == low, c_first, c_second)
        total = total + other_coef * (center - value)
    return (diag_ref[col : col + 1, :] * center + coef * total) * (1.0 / SCALE)


def row_kernel(cols_x, rows, slots, after, *refs):
    v_refs, (coef_ref, diag_ref), refs = refs[:cols_x], refs[cols_x : cols_x + 2], refs[cols_x + 2 :]
    number = len(slots)
    got, got_coefs = dict(zip(slots, refs)), dict(zip(slots, refs[number:]))
    blocks_ref, refs = refs[2 * number], refs[2 * number + 1 + after :]
    others = cols_x - len(rows) if rows[0] == 0 else 0
    done, refs = refs[:others], refs[others:]
    w_refs, next_refs, edges = refs[: len(rows)], refs[len(rows) : 2 * len(rows)], refs[2 * len(rows) :]
    cols_y = v_refs[0].shape[0]
    for row, w_ref, next_ref in zip(rows, w_refs, next_refs):
        for y in range(cols_y):
            w = operate(v_refs, coef_ref, diag_ref, got, got_coefs, row, y)
            w_ref[y] = w
            next_ref[y] = apply_blocks(w, blocks_ref, row * cols_y + y)
    if edges:
        write_edges((*next_refs, *done), None, edges[:2])
        write_side(0, next_refs[0], None, edges[2])


def share_size(matrices, count):
    return (matrices * (count + 1) + 1) // 2


def lanes_of(used):
    return -(-used // 64) * 64


def last_kernel(cols_x, rows, slots, grams, *refs):
    v_refs, (coef_ref, diag_ref), refs = refs[:cols_x], refs[cols_x : cols_x + 2], refs[cols_x + 2 :]
    number = len(slots)
    got, got_coefs = dict(zip(slots, refs)), dict(zip(slots, refs[number:]))
    refs = refs[2 * number :]
    gram_refs, w_refs, out_ref = refs[:grams], refs[grams:-1], refs[-1]
    cols_y, count, _ = v_refs[0].shape
    total = jnp.zeros((2 * count, 2 * count), jnp.float32)
    for ref in gram_refs[2:]:
        total = total + ref[...]
    for row, w_ref in zip(rows, w_refs):
        for y in range(cols_y):
            w = operate(v_refs, coef_ref, diag_ref, got, got_coefs, row, y)
            w_ref[y] = w
            total = total + split_gram([v_refs[row][y]], w)
    if rows[0] != 0:
        out_ref[...] = total
        return
    size = share_size(2 * ITERS - 1, count)
    last = fold_square(fold(total))
    used = size + last.shape[1]
    rest = jnp.zeros((count // 2, lanes_of(used) - used), jnp.float32)
    early = (gram_refs[0][...] + gram_refs[1][...])[:, :size]
    packed = jnp.concatenate([early, last, rest], axis=1)
    middle = count // 4
    packed = jnp.concatenate(
        [packed[:middle], packed[middle:]], axis=1
    )
    for peer in range(out_ref.shape[0]):
        out_ref[peer] = packed


def split_gram(lefts, right):
    return lax.dot_general(
        jnp.concatenate([term for left in lefts for term in split(left)], axis=0),
        jnp.concatenate(split(right), axis=0),
        (((1,), (1,)), ((), ())),
        preferred_element_type=jnp.float32,
    )


def fold(total):
    count = total.shape[0] // 2
    total = total[:count] + total[count:]
    total = total[:, :count] + total[:, count:]
    return 0.5 * (total + total.T)


def grams_of(cols_x, groups, arrays):
    cols_y, count, _ = arrays[0].shape
    squares = []
    for lefts, right in groups:
        total = jnp.zeros((2 * count * len(lefts), 2 * count), jnp.float32)
        for row in range(cols_x):
            for y in range(cols_y):
                total = total + split_gram(
                    [arrays[left * cols_x + row][y] for left in lefts],
                    arrays[right * cols_x + row][y],
                )
        squares += [fold(total[2 * count * i : 2 * count * (i + 1)]) for i in range(len(lefts))]
    return squares


def gram_kernel(cols_x, groups, *refs):
    refs[-1][...] = jnp.concatenate(grams_of(cols_x, groups, refs[:-1]), axis=1)


def fold_square(square):
    half = square.shape[0] // 2
    bottom = jnp.concatenate([square[half:], jnp.zeros((half, 1), jnp.float32)], axis=1)
    top = jnp.concatenate(
        [jnp.zeros((half, half + 1), jnp.float32), square[:half, :half]], axis=1
    )
    row = lax.broadcasted_iota(jnp.int32, bottom.shape, 0)
    lane = lax.broadcasted_iota(jnp.int32, bottom.shape, 1)
    return jnp.where(lane <= half + row, bottom, top)


def unfold_squares(folded):
    half = folded.shape[0]
    row = lax.broadcasted_iota(jnp.int32, (half, half), 0)
    lane = lax.broadcasted_iota(jnp.int32, (half, half), 1)
    diagonal = jnp.where(row == lane, 0.5, 1.0)
    across = lax.broadcasted_iota(jnp.int32, (half, 2 * half), 1)
    end = half + lax.broadcasted_iota(jnp.int32, (half, 2 * half), 0)
    below = jnp.where(across < end, 1.0, jnp.where(across == end, 0.5, 0.0))
    width = 2 * half + 1
    parts = []
    for i in range(folded.shape[1] // width):
        one = folded[:, i * width : (i + 1) * width]
        upper = jnp.where(row <= lane, one[:, half + 1 :] * diagonal, 0.0)
        lower = jnp.where(across <= end, one[:, : 2 * half] * below, 0.0)
        upper = jnp.concatenate([upper, jnp.zeros_like(upper)], axis=1)
        parts.append(jnp.concatenate([upper, lower], axis=0))
    turned = jnp.concatenate(parts, axis=1).T
    return [
        part + turned[2 * half * i : 2 * half * (i + 1)] for i, part in enumerate(parts)
    ]


def share(folded, axis_odd):
    lanes = folded.shape[1]
    size = (lanes + 1) // 2
    return jnp.where(axis_odd, folded[:, lanes - size :], folded[:, :size])


def halves_kernel(cols_x, groups, *refs):
    arrays, early_refs, (send_ref, keep_ref) = refs[:-3], refs[-3:-2], refs[-2:]
    count = arrays[0].shape[1]
    squares = [
        ref[:, i * count : (i + 1) * count]
        for ref in early_refs
        for i in range(ref.shape[1] // count)
    ]
    squares += grams_of(cols_x, groups, arrays)
    folded = jnp.concatenate([fold_square(square) for square in squares], axis=1)
    odd = lax.rem(lax.axis_index("wide"), 2) == 1
    for ref, mine in ((send_ref, jnp.logical_not(odd)), (keep_ref, odd)):
        half = share(folded, mine)
        rest = jnp.zeros((half.shape[0], ref.shape[1] - half.shape[1]), jnp.float32)
        ref[...] = jnp.concatenate([half, rest], axis=1)


def solve_spd(matrix, target):
    size, width = matrix.shape[0], matrix.shape[1] + target.shape[1]
    lanes = 128
    work = jnp.concatenate(
        [matrix, target, jnp.zeros((size, lanes - width), jnp.float32)], axis=1
    )
    row = lax.broadcasted_iota(jnp.int32, (size, lanes), 0)

    def spread(p):
        return jnp.broadcast_to(work[:, p : p + 1], (size, lanes))

    ahead = {p: spread(p) for p in range(AHEAD)}
    inverses = jnp.zeros((size, lanes), jnp.float32)
    for p in range(size):
        column = ahead.pop(p)
        if p + AHEAD < size:
            ahead[p + AHEAD] = spread(p + AHEAD)
        inverse = 1.0 / column[p : p + 1, :]
        inverses = jnp.where(row == p, inverse, inverses)
        factor = jnp.where(row == p, 0.0, column)

        def eliminate(value):
            return value - factor * jnp.broadcast_to(value[p : p + 1, :] * inverse, value.shape)

        ahead = {q: eliminate(value) for q, value in ahead.items()}
        work = eliminate(work)
    return work[:, size:width] * inverses[:, size:width]


def finish_kernel(cols_x, blocks, sums_ref, *refs):
    r_refs, refs = refs[:cols_x], refs[cols_x:]
    v_refs, w_refs, refs = refs[: blocks * cols_x], refs[blocks * cols_x : 2 * blocks * cols_x], refs[2 * blocks * cols_x :]
    x_hbm, out_hbm, x_ref, out_ref, sem = refs
    cols_y = r_refs[0].shape[0]
    count = r_refs[0].shape[1]
    sums = []
    for parity in range(2):
        total = sums_ref[parity]
        for peer in range(parity + 2, sums_ref.shape[0], 2):
            total = total + sums_ref[peer]
        middle = total.shape[1] // 2
        sums.append(jnp.concatenate([total[:, :middle], total[:, middle:]], axis=0))
    even, odd = sums
    size, width = share_size(2 * blocks - 1, count), count + 1
    early = (2 * blocks - 1) * width
    moments = unfold_squares(
        jnp.concatenate(
            [
                even[:, :size],
                odd[:, 2 * size - early : size],
                even[:, size : size + width] + odd[:, size : size + width],
            ],
            axis=1,
        )
    )
    matrix = jnp.concatenate(
        [
            jnp.concatenate([moments[1 + i + j] for j in range(blocks)], axis=1)
            for i in range(blocks)
        ],
        axis=0,
    )
    target = jnp.concatenate(moments[:blocks], axis=0)
    coefs = solve_spd(matrix, target).T
    high = coefs.astype(jnp.bfloat16)
    middle, low = split(coefs - high.astype(jnp.float32))
    left = jnp.concatenate([high, high, middle, low], axis=1)

    def combine(values, row, y):
        highs, lows = zip(*(split(values[j * cols_x + row][y]) for j in range(blocks)))
        right = jnp.concatenate(highs + lows + highs + highs, axis=0)
        return jnp.dot(left, right, preferred_element_type=jnp.float32)

    copies = []

    def send(columns, ref, hbm, row):
        ref[row] = jnp.transpose(jnp.stack(columns), (1, 0, 2))
        target = hbm.at[:, oriented(row, cols_x)]
        copies.append(pltpu.make_async_copy(ref.at[row], target, sem.at[len(copies)]))
        copies[-1].start()

    for row in range(cols_x):
        send([r_refs[row][y] - combine(w_refs, row, y) for y in range(cols_y)], out_ref, out_hbm, row)
        send([combine(v_refs, row, y) * (1.0 / SCALE) for y in range(cols_y)], x_ref, x_hbm, row)
    for copy in copies:
        copy.wait()


def pairing(sizes, axis, phase):
    transfers = []
    for place in np.ndindex(*sizes):
        partner = list(place)
        partner[axis] += 1 if place[axis] % 2 == phase else -1
        if not 0 <= partner[axis] < sizes[axis]:
            partner = list(place)
            partner[1 - axis] ^= 1
            if partner[1 - axis] >= sizes[1 - axis]:
                continue
        transfers.append(tuple(int(np.ravel_multi_index(p, sizes)) for p in (place, partner)))
    return transfers


def exchange(slot, edge):
    sizes = tuple(lax.axis_size(axis) for axis in AXES)
    return lax.ppermute(edge, AXES, pairing(sizes, slot // 2, slot % 2))


def on_device(sources, well_columns, column_active, perm_root, storage_term, inverse_blocks):
    count, cols_x, cols_y, layers = sources.shape
    number = cols_x * cols_y
    devices = lax.axis_size("wide") * lax.axis_size("narrow")
    blocks = inverse_blocks.reshape((number,) + inverse_blocks.shape[2:])
    state, rows = (cols_y, count, layers), (number, layers)
    flat = (cols_y * count, layers)
    apply_flops = 4 * count * number * layers * inverse_blocks.shape[-1]
    gram_flops = 8 * count * count * number * layers

    ends = (cols_x * (count + 1), layers)
    side = (cols_y * (count + 1), layers)
    by_row = (cols_x, count, cols_y, layers)
    out = call(
        start_kernel,
        [state] * (2 * cols_x)
        + [rows, rows, jax.ShapeDtypeStruct(blocks.shape, blocks.dtype), ends, ends, side, (side[0] + 8, layers)],
        [HBM] * 6,
        *(
            pltpu.with_memory_space_constraint(a, pltpu.HBM)
            for a in (well_columns, column_active, sources, perm_root, storage_term, blocks)
        ),
        flops=apply_flops,
        scratch=[
            pltpu.SMEM(well_columns.shape, jnp.int32),
            pltpu.SMEM(column_active.shape, jnp.int32),
            pltpu.VMEM(by_row, jnp.float32),
            pltpu.VMEM(perm_root.shape, jnp.float32),
            pltpu.VMEM(storage_term.shape, jnp.float32),
            pltpu.SemaphoreType.DMA((4,)),
            pltpu.SemaphoreType.DMA((cols_x,)),
            pltpu.SemaphoreType.DMA((cols_x,)),
        ],
    )
    rhs, v = out[:cols_x], out[cols_x : 2 * cols_x]
    coef, diag_term, blocks, *edges = out[2 * cols_x :]
    got_coefs = got = [exchange(slot, edge) for slot, edge in enumerate(edges)]
    vs, ws, grams = [v], [], []
    later_ends, later_side = (cols_x * count, layers), (cols_y * count + 8, layers)

    if cols_x > 1:
        shares = [(tuple(range(1, cols_x)), (0, 1, 2)), ((0,), (0, 1, 3))]
    else:
        shares = [((0,), (0, 1, 2, 3))]

    def halo(slots):
        return [*(got[i] for i in slots), *(got_coefs[i] for i in slots)]

    for j in range(1, ITERS):
        w, v = [], []
        for rows, slots in shares:
            ahead = [] if v else grams
            operands = [*vs[-1], coef, diag_term, *halo(slots), blocks, *ahead, *v]
            out = call(
                functools.partial(row_kernel, cols_x, rows, slots, len(ahead)),
                [state] * (2 * len(rows))
                + ([later_ends] * 2 + [later_side] if rows[0] == 0 else []),
                [VMEM] * len(operands),
                *operands,
                flops=apply_flops // len(shares),
            )
            w = out[: len(rows)] + w
            v = out[len(rows) : 2 * len(rows)] + v
            edges = out[2 * len(rows) :]
        edges.insert(2, v[-1].reshape(flat))
        got = [exchange(slot, edge) for slot, edge in enumerate(edges)]
        vs.append(v)
        ws.append(w)
        arrays = vs[-2] + v + w + (rhs if j == 1 else [])
        groups = ([((0,), 3)] if j == 1 else []) + [((0, 1), 2)]
        number_of = len(groups) + 1
        if j < ITERS - 1:
            grams += call(
                functools.partial(gram_kernel, cols_x, groups),
                [(count, number_of * count)],
                [VMEM] * len(arrays),
                *arrays,
                flops=number_of * gram_flops,
            )
        else:
            send, keep = call(
                functools.partial(halves_kernel, cols_x, groups),
                [(count // 2, 128)] * 2,
                [VMEM] * (len(arrays) + 1),
                *arrays, *grams,
                flops=number_of * gram_flops,
            )
            grams = [keep, exchange(2, send)]
    lanes = lanes_of(share_size(2 * ITERS - 1, count) + count + 1)
    w, totals = [], []
    for rows, slots in shares:
        first = [] if rows[0] else [*grams, *totals]
        operands = [*vs[-1], coef, diag_term, *halo(slots), *first]
        out = call(
            functools.partial(last_kernel, cols_x, rows, slots, len(first)),
            [state] * len(rows)
            + [(2 * count, 2 * count) if rows[0] else (devices, count // 4, 2 * lanes)],
            [VMEM] * len(operands),
            *operands,
            flops=gram_flops // len(shares),
        )
        w = out[:-1] + w
        totals.append(out[-1])
    joint = totals[-1]
    ws.append(w)
    joint = lax.all_to_all(joint, AXES, 0, 0)
    outs = call(
        functools.partial(finish_kernel, cols_x, ITERS),
        [sources.shape] * 2,
        [VMEM] * (1 + cols_x + 2 * ITERS * cols_x),
        joint, *rhs, *(a for v in vs for a in v), *(a for w in ws for a in w),
        flops=24 * ITERS * count * count * number * layers,
        out_specs=[HBM, HBM],
        scratch=[
            pltpu.VMEM(by_row, jnp.float32),
            pltpu.VMEM(by_row, jnp.float32),
            pltpu.SemaphoreType.DMA((2 * cols_x,)),
        ],
    )
    return tuple(outs)


def solution(mesh):
    in_specs = (
        P(None, "wide", "narrow", None),
        P(),
        P("wide", "narrow"),
        P("wide", "narrow", None),
        P("wide", "narrow", None),
        P("wide", "narrow", None, None, None),
    )
    out_specs = (P(None, "wide", "narrow", None), P(None, "wide", "narrow", None))
    return jax.shard_map(
        on_device, mesh=mesh, in_specs=in_specs, out_specs=out_specs, check_vma=False
    )
```

```python
import functools

import jax
import jax.numpy as jnp
import numpy as np
from jax import lax
from jax.experimental import pallas as pl
from jax.experimental.pallas import tpu as pltpu
from jax.sharding import PartitionSpec as P

ITERS = 3
WELL_RATE = 4.0
VMEM_BYTES = 24 * 1024 * 1024
VMEM = pl.BlockSpec(memory_space=pltpu.VMEM)
HBM = pl.BlockSpec(memory_space=pltpu.HBM)
SCALE = 64.0
AHEAD = 6


def call(kernel, out_shape, in_specs, *args, flops=0, out_specs=None, scratch=()):
    shapes = [
        s if isinstance(s, jax.ShapeDtypeStruct) else jax.ShapeDtypeStruct(s, jnp.float32)
        for s in out_shape
    ]
    size = sum(a.size * a.dtype.itemsize for a in args) + sum(s.size * 4 for s in shapes)
    out = pl.pallas_call(
        kernel,
        out_shape=shapes,
        in_specs=in_specs,
        out_specs=out_specs or [VMEM] * len(shapes),
        scratch_shapes=list(scratch),
        compiler_params=pltpu.CompilerParams(vmem_limit_bytes=VMEM_BYTES),
        cost_estimate=pl.CostEstimate(flops=flops, bytes_accessed=size, transcendentals=0),
    )(*args)
    return list(out)


def split(value):
    high = value.astype(jnp.bfloat16)
    return high, (value - high.astype(jnp.float32)).astype(jnp.bfloat16)


def apply_blocks(value, blocks_ref, col):
    count, layers = value.shape
    size = blocks_ref.shape[-1]
    number = layers // size
    terms = split(value)
    left = jnp.concatenate(
        [term[:, b * size : (b + 1) * size] for b in range(number) for term in terms], axis=0
    )
    right = jnp.concatenate([blocks_ref[col, b] for b in range(number)], axis=1)
    out = jnp.dot(left, right, preferred_element_type=jnp.float32)
    parts = []
    for b in range(number):
        piece = out[2 * b * count : 2 * (b + 1) * count, b * size : (b + 1) * size]
        parts.append(piece[:count] + piece[count:])
    return jnp.concatenate(parts, axis=1)


AXES = ("narrow", "wide")


def oriented(row, cols_x):
    odd = lax.rem(lax.axis_index("wide"), 2)
    return row + odd * (cols_x - 1 - 2 * row)


def partnered(slot):
    axis = AXES[slot // 2]
    place = lax.axis_index(axis)
    odd = lax.rem(place + slot, 2)
    partner = place + 1 - 2 * odd
    inside = jnp.logical_and(partner >= 0, partner < lax.axis_size(axis))
    return inside.astype(jnp.float32)


def write_edges(v_refs, coef_ref, edges):
    count = v_refs[0].shape[1]
    cols_y = v_refs[0].shape[0]
    odd = lax.rem(lax.axis_index("narrow"), 2)
    for ref, at_low in zip(edges, (odd, 1 - odd)):
        y = (1 - at_low) * (cols_y - 1)
        for row, v_ref in enumerate(v_refs):
            ref[row * count : (row + 1) * count, :] = v_ref[y]
            if coef_ref is not None:
                place = len(v_refs) * count + row
                ref[place : place + 1, :] = coef_ref[pl.ds(row * cols_y + y, 1), :]


def write_side(row, v_ref, coef_ref, edge):
    cols_y, count, _ = v_ref.shape
    for y in range(cols_y):
        edge[y * count : (y + 1) * count, :] = v_ref[y]
    if coef_ref is not None:
        edge[cols_y * count : cols_y * (count + 1), :] = coef_ref[
            row * cols_y : (row + 1) * cols_y, :
        ]


def start_kernel(
    wells_hbm, active_hbm, sources_hbm, perm_hbm, storage_hbm, blocks_hbm, *refs
):
    cols_x, cols_y = active_hbm.shape
    r_refs, v_refs, refs = refs[:cols_x], refs[cols_x : 2 * cols_x], refs[2 * cols_x :]
    coef_ref, diag_ref, blocks_ref, edge_0, edge_1, edge_2, edge_3 = refs[:7]
    wells_ref, active_ref, sources_ref, perm_ref, storage_ref, small_sem, big_sem, block_sem = refs[7:]
    _, count, layers = r_refs[0].shape
    small = [
        pltpu.make_async_copy(source, target, small_sem.at[i])
        for i, (source, target) in enumerate(
            (
                (wells_hbm, wells_ref),
                (active_hbm, active_ref),
                (perm_hbm, perm_ref),
                (storage_hbm, storage_ref),
            )
        )
    ]
    sources, blocks = [], []
    for row in range(cols_x):
        x = oriented(row, cols_x)
        sources.append(
            pltpu.make_async_copy(sources_hbm.at[:, x], sources_ref.at[row], big_sem.at[row])
        )
        blocks.append(
            pltpu.make_async_copy(
                blocks_hbm.at[pl.ds(x * cols_y, cols_y)],
                blocks_ref.at[pl.ds(row * cols_y, cols_y)],
                block_sem.at[row],
            )
        )
    for copy in small:
        copy.start()
    for pair in zip(sources, blocks):
        for copy in pair:
            copy.start()
    for copy in small:
        copy.wait()
    place = lax.broadcasted_iota(jnp.int32, (count, layers), 0)
    wells = jnp.zeros((count, layers), jnp.int32)
    for k in range(count):
        wells = jnp.where(place == k, wells_ref[k], wells)
    grid_y = cols_y * lax.axis_size("narrow")
    first_x, first_y = lax.axis_index("wide") * cols_x, lax.axis_index("narrow") * cols_y
    for row in range(cols_x):
        x = oriented(row, cols_x)
        for y in range(cols_y):
            col = row * cols_y + y
            active = active_ref[x, y].astype(jnp.float32)
            perm, storage = perm_ref[x, y : y + 1, :], storage_ref[x, y : y + 1, :]
            coef_ref[col : col + 1, :] = active * perm
            diag_ref[col : col + 1, :] = active * storage + (1.0 - active)
    for row in range(cols_x):
        sources[row].wait()
        across = jnp.transpose(sources_ref[row], (1, 0, 2))
        blocks[row].wait()
        for y in range(cols_y):
            column_id = (first_x + oriented(row, cols_x)) * grid_y + first_y + y
            r = across[y] + jnp.where(wells == column_id, WELL_RATE, 0.0)
            r_refs[row][y] = r
            v_refs[row][y] = apply_blocks(r, blocks_ref, row * cols_y + y)
    write_side(0, v_refs[0], coef_ref, edge_3)
    write_side(cols_x - 1, v_refs[-1], coef_ref, edge_2)
    write_edges(v_refs, coef_ref, (edge_0, edge_1))


def received(got, got_coefs, slot, i, number, count):
    place = number * count + i
    value = got[slot][i * count : (i + 1) * count, :]
    return value, got_coefs[slot][place : place + 1, :] * partnered(slot)


def operate(v_refs, coef_ref, diag_ref, got, got_coefs, row, y):
    cols_x = len(v_refs)
    cols_y, count, layers = v_refs[row].shape
    col = row * cols_y + y
    center = v_refs[row][y]
    coef = coef_ref[col : col + 1, :]
    lane = lax.broadcasted_iota(jnp.int32, (1, layers), 1)
    upper_coef = jnp.where(lane == layers - 1, 0.0, pltpu.roll(coef, layers - 1, 1))
    lower_coef = jnp.where(lane == 0, 0.0, pltpu.roll(coef, 1, 1))
    total = upper_coef * (center - pltpu.roll(center, layers - 1, 1))
    total = total + lower_coef * (center - pltpu.roll(center, 1, 1))
    for step_row, step_y in ((1, 0), (-1, 0), (0, 1), (0, -1)):
        other, ny = row + step_row, y + step_y
        if 0 <= ny < cols_y and 0 <= other < cols_x:
            place = other * cols_y + ny
            value, other_coef = v_refs[other][ny], coef_ref[place : place + 1, :]
        elif step_row:
            slot = 3 if step_row < 0 else 2
            value, other_coef = received(got, got_coefs, slot, y, cols_y, count)
        else:
            odd = lax.rem(lax.axis_index("narrow"), 2) == 1
            first, c_first = received(got, got_coefs, 0, row, cols_x, count)
            second, c_second = received(got, got_coefs, 1, row, cols_x, count)
            low = step_y < 0
            value = jnp.where(odd == low, first, second)
            other_coef = jnp.where(odd == low, c_first, c_second)
        total = total + other_coef * (center - value)
    return (diag_ref[col : col + 1, :] * center + coef * total) * (1.0 / SCALE)


def row_kernel(cols_x, rows, slots, after, *refs):
    v_refs, (coef_ref, diag_ref), refs = refs[:cols_x], refs[cols_x : cols_x + 2], refs[cols_x + 2 :]
    number = len(slots)
    got, got_coefs = dict(zip(slots, refs)), dict(zip(slots, refs[number:]))
    blocks_ref, refs = refs[2 * number], refs[2 * number + 1 + after :]
    others = cols_x - len(rows) if rows[0] == 0 else 0
    done, refs = refs[:others], refs[others:]
    w_refs, next_refs, edges = refs[: len(rows)], refs[len(rows) : 2 * len(rows)], refs[2 * len(rows) :]
    cols_y = v_refs[0].shape[0]
    total = 0.0
    for row, w_ref, next_ref in zip(rows, w_refs, next_refs):
        for y in range(cols_y):
            w = operate(v_refs, coef_ref, diag_ref, got, got_coefs, row, y)
            w_ref[y] = w
            following = apply_blocks(w, blocks_ref, row * cols_y + y)
            next_ref[y] = following
            if rows[0] and edges:
                total = total + split_gram([v_refs[row][y], following], w)
    if rows[0] and edges:
        edges[0][...] = total
    elif edges:
        write_edges((*next_refs, *done), None, edges[:2])
        write_side(0, next_refs[0], None, edges[2])


def share_size(matrices, count):
    return (matrices * (count + 1) + 1) // 2


def lanes_of(used):
    return -(-used // 64) * 64


def last_kernel(cols_x, rows, slots, grams, *refs):
    v_refs, (coef_ref, diag_ref), refs = refs[:cols_x], refs[cols_x : cols_x + 2], refs[cols_x + 2 :]
    number = len(slots)
    got, got_coefs = dict(zip(slots, refs)), dict(zip(slots, refs[number:]))
    refs = refs[2 * number :]
    gram_refs, w_refs, out_ref = refs[:grams], refs[grams:-1], refs[-1]
    cols_y, count, _ = v_refs[0].shape
    total = jnp.zeros((2 * count, 2 * count), jnp.float32)
    for ref in gram_refs[2:]:
        total = total + ref[...]
    for row, w_ref in zip(rows, w_refs):
        for y in range(cols_y):
            w = operate(v_refs, coef_ref, diag_ref, got, got_coefs, row, y)
            w_ref[y] = w
            total = total + split_gram([v_refs[row][y]], w)
    if rows[0] != 0:
        out_ref[...] = total
        return
    size = share_size(2 * ITERS - 1, count)
    last = fold_square(fold(total))
    used = size + last.shape[1]
    rest = jnp.zeros((count // 2, lanes_of(used) - used), jnp.float32)
    early = (gram_refs[0][...] + gram_refs[1][...])[:, :size]
    packed = jnp.concatenate([early, last, rest], axis=1)
    middle = count // 4
    packed = jnp.concatenate(
        [packed[:middle], packed[middle:]], axis=1
    )
    for peer in range(out_ref.shape[0]):
        out_ref[peer] = packed


def split_gram(lefts, right):
    return lax.dot_general(
        jnp.concatenate([term for left in lefts for term in split(left)], axis=0),
        jnp.concatenate(split(right), axis=0),
        (((1,), (1,)), ((), ())),
        preferred_element_type=jnp.float32,
    )


def fold(total):
    count = total.shape[0] // 2
    total = total[:count] + total[count:]
    total = total[:, :count] + total[:, count:]
    return 0.5 * (total + total.T)


def grams_of(cols_x, groups, arrays):
    cols_y, count, _ = arrays[0].shape
    squares = []
    for lefts, right in groups:
        total = jnp.zeros((2 * count * len(lefts), 2 * count), jnp.float32)
        for row in range(cols_x):
            for y in range(cols_y):
                total = total + split_gram(
                    [arrays[left * cols_x + row][y] for left in lefts],
                    arrays[right * cols_x + row][y],
                )
        squares += [fold(total[2 * count * i : 2 * count * (i + 1)]) for i in range(len(lefts))]
    return squares


def gram_kernel(cols_x, groups, *refs):
    refs[-1][...] = jnp.concatenate(grams_of(cols_x, groups, refs[:-1]), axis=1)


def fold_square(square):
    half = square.shape[0] // 2
    bottom = jnp.concatenate([square[half:], jnp.zeros((half, 1), jnp.float32)], axis=1)
    top = jnp.concatenate(
        [jnp.zeros((half, half + 1), jnp.float32), square[:half, :half]], axis=1
    )
    row = lax.broadcasted_iota(jnp.int32, bottom.shape, 0)
    lane = lax.broadcasted_iota(jnp.int32, bottom.shape, 1)
    return jnp.where(lane <= half + row, bottom, top)


def unfold_squares(folded):
    half = folded.shape[0]
    row = lax.broadcasted_iota(jnp.int32, (half, half), 0)
    lane = lax.broadcasted_iota(jnp.int32, (half, half), 1)
    diagonal = jnp.where(row == lane, 0.5, 1.0)
    width = 2 * half + 1
    parts = []
    for i in range(folded.shape[1] // width):
        one = folded[:, i * width : (i + 1) * width]
        upper = jnp.where(row <= lane, one[:, half + 1 :] * diagonal, 0.0)
        lower = jnp.where(row >= lane, one[:, half : 2 * half] * diagonal, 0.0)
        parts.append(
            jnp.concatenate(
                [
                    jnp.concatenate([upper, jnp.zeros_like(upper)], axis=1),
                    jnp.concatenate([one[:, :half], lower], axis=1),
                ],
                axis=0,
            )
        )
    turned = jnp.concatenate(parts, axis=1).T
    return [
        part + turned[2 * half * i : 2 * half * (i + 1)] for i, part in enumerate(parts)
    ]


def share(folded, axis_odd):
    lanes = folded.shape[1]
    size = (lanes + 1) // 2
    return jnp.where(axis_odd, folded[:, lanes - size :], folded[:, :size])


def halves_kernel(*refs):
    arrays, part_refs, early_refs, (send_ref, keep_ref) = refs[:3], refs[3:-3], refs[-3:-2], refs[-2:]
    count = arrays[0].shape[1]
    squares = [
        ref[:, i * count : (i + 1) * count]
        for ref in early_refs
        for i in range(ref.shape[1] // count)
    ]
    late = grams_of(1, [((0, 1), 2)], arrays)
    for ref in part_refs:
        late = [
            square + fold(ref[2 * count * i : 2 * count * (i + 1), :])
            for i, square in enumerate(late)
        ]
    squares += late
    folded = jnp.concatenate([fold_square(square) for square in squares], axis=1)
    odd = lax.rem(lax.axis_index("wide"), 2) == 1
    for ref, mine in ((send_ref, jnp.logical_not(odd)), (keep_ref, odd)):
        half = share(folded, mine)
        rest = jnp.zeros((half.shape[0], ref.shape[1] - half.shape[1]), jnp.float32)
        ref[...] = jnp.concatenate([half, rest], axis=1)


def solve_spd(matrix, target):
    size, width = matrix.shape[0], matrix.shape[1] + target.shape[1]
    lanes = 128
    work = jnp.concatenate(
        [matrix, target, jnp.zeros((size, lanes - width), jnp.float32)], axis=1
    )
    row = lax.broadcasted_iota(jnp.int32, (size, lanes), 0)

    def spread(p):
        return jnp.broadcast_to(work[:, p : p + 1], (size, lanes))

    ahead = {p: spread(p) for p in range(AHEAD)}
    inverses = jnp.zeros((size, lanes), jnp.float32)
    for p in range(size):
        column = ahead.pop(p)
        if p + AHEAD < size:
            ahead[p + AHEAD] = spread(p + AHEAD)
        inverse = 1.0 / column[p : p + 1, :]
        inverses = jnp.where(row == p, inverse, inverses)
        factor = jnp.where(row == p, 0.0, column)

        def eliminate(value):
            return value - factor * jnp.broadcast_to(value[p : p + 1, :] * inverse, value.shape)

        ahead = {q: eliminate(value) for q, value in ahead.items()}
        work = eliminate(work)
    return work[:, size:width] * inverses[:, size:width]


def finish_kernel(cols_x, blocks, sums_ref, *refs):
    r_refs, refs = refs[:cols_x], refs[cols_x:]
    v_refs, w_refs, refs = refs[: blocks * cols_x], refs[blocks * cols_x : 2 * blocks * cols_x], refs[2 * blocks * cols_x :]
    x_hbm, out_hbm, x_ref, out_ref, sem = refs
    cols_y = r_refs[0].shape[0]
    count = r_refs[0].shape[1]
    sums = []
    for parity in range(2):
        total = sums_ref[parity]
        for peer in range(parity + 2, sums_ref.shape[0], 2):
            total = total + sums_ref[peer]
        middle = total.shape[1] // 2
        sums.append(jnp.concatenate([total[:, :middle], total[:, middle:]], axis=0))
    even, odd = sums
    size, width = share_size(2 * blocks - 1, count), count + 1
    early = (2 * blocks - 1) * width
    moments = unfold_squares(
        jnp.concatenate(
            [
                even[:, :size],
                odd[:, 2 * size - early : size],
                even[:, size : size + width] + odd[:, size : size + width],
            ],
            axis=1,
        )
    )
    matrix = jnp.concatenate(
        [
            jnp.concatenate([moments[1 + i + j] for j in range(blocks)], axis=1)
            for i in range(blocks)
        ],
        axis=0,
    )
    target = jnp.concatenate(moments[:blocks], axis=0)
    coefs = solve_spd(matrix, target).T
    high = coefs.astype(jnp.bfloat16)
    middle, low = split(coefs - high.astype(jnp.float32))
    left = jnp.concatenate([high, high, middle, middle, low], axis=1)

    def combine(values, row, y):
        highs, lows = zip(*(split(values[j * cols_x + row][y]) for j in range(blocks)))
        right = jnp.concatenate(highs + lows + highs + lows + highs, axis=0)
        return jnp.dot(left, right, preferred_element_type=jnp.float32)

    copies = []

    def send(columns, ref, hbm, row):
        ref[row] = jnp.transpose(jnp.stack(columns), (1, 0, 2))
        target = hbm.at[:, oriented(row, cols_x)]
        copies.append(pltpu.make_async_copy(ref.at[row], target, sem.at[len(copies)]))
        copies[-1].start()

    for row in range(cols_x):
        send([r_refs[row][y] - combine(w_refs, row, y) for y in range(cols_y)], out_ref, out_hbm, row)
        send([combine(v_refs, row, y) * (1.0 / SCALE) for y in range(cols_y)], x_ref, x_hbm, row)
    for copy in copies:
        copy.wait()


def pairing(sizes, axis, phase):
    transfers = []
    for place in np.ndindex(*sizes):
        partner = list(place)
        partner[axis] += 1 if place[axis] % 2 == phase else -1
        if not 0 <= partner[axis] < sizes[axis]:
            partner = list(place)
            partner[1 - axis] ^= 1
            if partner[1 - axis] >= sizes[1 - axis]:
                continue
        transfers.append(tuple(int(np.ravel_multi_index(p, sizes)) for p in (place, partner)))
    return transfers


def exchange(slot, edge):
    sizes = tuple(lax.axis_size(axis) for axis in AXES)
    return lax.ppermute(edge, AXES, pairing(sizes, slot // 2, slot % 2))


def on_device(sources, well_columns, column_active, perm_root, storage_term, inverse_blocks):
    count, cols_x, cols_y, layers = sources.shape
    number = cols_x * cols_y
    devices = lax.axis_size("wide") * lax.axis_size("narrow")
    blocks = inverse_blocks.reshape((number,) + inverse_blocks.shape[2:])
    state, rows = (cols_y, count, layers), (number, layers)
    flat = (cols_y * count, layers)
    apply_flops = 4 * count * number * layers * inverse_blocks.shape[-1]
    gram_flops = 8 * count * count * number * layers

    ends = (cols_x * (count + 1), layers)
    side = (cols_y * (count + 1), layers)
    by_row = (cols_x, count, cols_y, layers)
    out = call(
        start_kernel,
        [state] * (2 * cols_x)
        + [rows, rows, jax.ShapeDtypeStruct(blocks.shape, blocks.dtype), ends, ends, side, (side[0] + 8, layers)],
        [HBM] * 6,
        *(
            pltpu.with_memory_space_constraint(a, pltpu.HBM)
            for a in (well_columns, column_active, sources, perm_root, storage_term, blocks)
        ),
        flops=apply_flops,
        scratch=[
            pltpu.SMEM(well_columns.shape, jnp.int32),
            pltpu.SMEM(column_active.shape, jnp.int32),
            pltpu.VMEM(by_row, jnp.float32),
            pltpu.VMEM(perm_root.shape, jnp.float32),
            pltpu.VMEM(storage_term.shape, jnp.float32),
            pltpu.SemaphoreType.DMA((4,)),
            pltpu.SemaphoreType.DMA((cols_x,)),
            pltpu.SemaphoreType.DMA((cols_x,)),
        ],
    )
    rhs, v = out[:cols_x], out[cols_x : 2 * cols_x]
    coef, diag_term, blocks, *edges = out[2 * cols_x :]
    got_coefs = got = [exchange(slot, edge) for slot, edge in enumerate(edges)]
    vs, ws, grams = [v], [], []
    later_ends, later_side = (cols_x * count, layers), (cols_y * count + 8, layers)

    if cols_x > 1:
        shares = [(tuple(range(1, cols_x)), (0, 1, 2)), ((0,), (0, 1, 3))]
    else:
        shares = [((0,), (0, 1, 2, 3))]

    def halo(slots):
        return [*(got[i] for i in slots), *(got_coefs[i] for i in slots)]

    for j in range(1, ITERS):
        w, v, parts = [], [], []
        for rows, slots in shares:
            ahead = [] if v else grams
            operands = [*vs[-1], coef, diag_term, *halo(slots), blocks, *ahead, *v]
            out = call(
                functools.partial(row_kernel, cols_x, rows, slots, len(ahead)),
                [state] * (2 * len(rows))
                + (
                    [later_ends] * 2 + [later_side]
                    if rows[0] == 0
                    else [(4 * count, 2 * count)] * (j == ITERS - 1)
                ),
                [VMEM] * len(operands),
                *operands,
                flops=apply_flops // len(shares),
            )
            w = out[: len(rows)] + w
            v = out[len(rows) : 2 * len(rows)] + v
            edges = out[2 * len(rows) :]
            if rows[0]:
                parts += edges
        edges.insert(2, v[-1].reshape(flat))
        got = [exchange(slot, edge) for slot, edge in enumerate(edges)]
        vs.append(v)
        ws.append(w)
        arrays = vs[-2] + v + w + (rhs if j == 1 else [])
        groups = ([((0,), 3)] if j == 1 else []) + [((0, 1), 2)]
        number_of = len(groups) + 1
        if j < ITERS - 1:
            grams += call(
                functools.partial(gram_kernel, cols_x, groups),
                [(count, number_of * count)],
                [VMEM] * len(arrays),
                *arrays,
                flops=number_of * gram_flops,
            )
        else:
            send, keep = call(
                halves_kernel,
                [(count // 2, 128)] * 2,
                [VMEM] * (4 + len(parts)),
                vs[-2][0], v[0], w[0], *parts, *grams,
                flops=number_of * gram_flops // cols_x,
            )
            grams = [keep, exchange(2, send)]
    lanes = lanes_of(share_size(2 * ITERS - 1, count) + count + 1)
    w, totals = [], []
    for rows, slots in shares:
        first = [] if rows[0] else [*grams, *totals]
        operands = [*vs[-1], coef, diag_term, *halo(slots), *first]
        out = call(
            functools.partial(last_kernel, cols_x, rows, slots, len(first)),
            [state] * len(rows)
            + [(2 * count, 2 * count) if rows[0] else (devices, count // 4, 2 * lanes)],
            [VMEM] * len(operands),
            *operands,
            flops=gram_flops // len(shares),
        )
        w = out[:-1] + w
        totals.append(out[-1])
    joint = totals[-1]
    ws.append(w)
    joint = lax.all_to_all(joint, AXES, 0, 0)
    outs = call(
        functools.partial(finish_kernel, cols_x, ITERS),
        [sources.shape] * 2,
        [VMEM] * (1 + cols_x + 2 * ITERS * cols_x),
        joint, *rhs, *(a for v in vs for a in v), *(a for w in ws for a in w),
        flops=24 * ITERS * count * count * number * layers,
        out_specs=[HBM, HBM],
        scratch=[
            pltpu.VMEM(by_row, jnp.float32),
            pltpu.VMEM(by_row, jnp.float32),
            pltpu.SemaphoreType.DMA((2 * cols_x,)),
        ],
    )
    return tuple(outs)


def solution(mesh):
    in_specs = (
        P(None, "wide", "narrow", None),
        P(),
        P("wide", "narrow"),
        P("wide", "narrow", None),
        P("wide", "narrow", None),
        P("wide", "narrow", None, None, None),
    )
    out_specs = (P(None, "wide", "narrow", None), P(None, "wide", "narrow", None))
    return jax.shard_map(
        on_device, mesh=mesh, in_specs=in_specs, out_specs=out_specs, check_vma=False
    )
```
